32 devices in a mesh: scene: 2 (over y), brick: 4 (over z), chan: 2 (over x), rep: 2 (over core).
Axes of the slice: x: 2, y: 2, z: 4, core: 2. Of those that a mesh axis runs over, the one named last changes fastest.
Arguments:
- features: bfloat16 [128, 73728], P('chan', ('scene', 'brick', 'rep')), parts along dimension 1, may hold values from -6 to 6
- conv_weight: bfloat16 [27, 128, 128], P(None, None, 'chan'), may hold values from -0.109375 to 0.109375
- neighbours: int32 [27, 73728], P(None, ('scene', 'brick', 'rep')), parts along dimension 1, may hold values from -1 to 36863, as said below
- cotangent: bfloat16 [128, 73728], P('chan', ('scene', 'brick', 'rep')), parts along dimension 1, may hold values from -6 to 6
Outputs:
- output: bfloat16 [128, 73728], P('chan', ('scene', 'brick', 'rep')), parts along dimension 1
- grad_features: bfloat16 [128, 73728], P('chan', ('scene', 'brick', 'rep')), parts along dimension 1
- grad_weight: float32 [54, 128, 128], P('scene', None, 'chan'), parts along dimension 0
The draws below stay inside these ranges and needn't reach their ends.
There are 2 independent parts, one for each index of `scene`. The reference program is written for one: setup_inputs(seed, part) draws one part's arguments, and reference() takes and returns one part's arrays. A program takes and returns all parts, laid end to end along the dimension named above; an argument that names none is the same for every part. Nothing has to cross between parts.
Inputs may be any that keep to these rules, and one draw needn't show every extreme that they name: Each entry neighbours[k, s] is -1 or s + (k // 9 - 1) * 256 + (k // 3 % 3 - 1) * 16 + (k % 3 - 1), the site beside s at that offset on a column of 16 x 16 cross-sections; neighbours[26 - k, neighbours[k, s]] = s wherever neighbours[k, s] >= 0; neighbours[13, s] is s or -1.
All inputs are finite; a program needn't handle non-finite values.
Results may differ from the reference program's by a relative error of at most 0.0065.
Values may be sent and summed in bfloat16 or wider, within the bound.
No kernel may reach another device: no remote copies, remote signals or barrier semaphores. Data moves between devices by JAX's collectives and lax.ppermute only.
A program may use at most 64 MiB of HBM per device.

```python
import jax
import jax.numpy as jnp
from jax import lax

C = 128
EDGE = 16
TAPS = 27
FACE = 256
SITES = 36864


def draw_neighbours(key, part):
    key = jax.random.fold_in(key, 5)
    total = SITES
    cells = jnp.arange(total, dtype=jnp.int32)
    column_x = cells % EDGE
    column_y = cells // EDGE % EDGE
    height = cells // FACE
    levels = total // FACE
    rolls = jax.random.randint(key, (total,), 0, 100, dtype=jnp.int32)
    chance = 45 + height * 50 // levels
    active = (rolls < chance) | (cells == total - 1)
    result = []
    for offset in range(27):
        step_z = offset // 9 - 1
        step_y = offset // 3 % 3 - 1
        step_x = offset % 3 - 1
        moved_x = column_x + step_x
        moved_y = column_y + step_y
        moved_z = height + step_z
        inside = (moved_x >= 0) & (moved_x < EDGE) & (moved_y >= 0) & (moved_y < EDGE) & (moved_z >= 0) & (moved_z < levels)
        target = cells + step_z * FACE + step_y * EDGE + step_x
        clipped = jnp.clip(target, 0, total - 1)
        usable = inside & active & active[clipped]
        result.append(jnp.where(usable, target, -1).astype(jnp.int32))
    return jnp.stack(result, axis=0)


def level_of(rng, dims, shards, smallest, high):
    factor_of = 1.0
    for axis_at, parts in shards:
        heights = jax.random.uniform(jax.random.fold_in(jax.random.fold_in(rng, 6), axis_at), (parts,), jnp.float32, smallest / len(shards), high / len(shards))
        factor_of = factor_of * jnp.repeat(jnp.exp(heights), dims[axis_at] // parts).reshape((-1,) + (1,) * (len(dims) - 1 - axis_at))
    return factor_of


def noise(own_key, dims, spread, bound, cuts=(), kind=jnp.bfloat16):
    entries = jax.random.normal(own_key, dims, jnp.float32) * spread
    if len(cuts) > 0:
        entries = level_of(own_key, dims, cuts, -0.22, 0.18) * entries
    return jnp.clip(entries, min=-bound, max=bound).astype(kind)


def setup_inputs(seed: int = 0, part: int = 0) -> dict:
    arg_keys = jax.random.split(jax.random.key(seed), 5)
    part_splits = jax.random.split(jax.random.fold_in(arg_keys[4], part), 5)
    return {
        "features": noise(part_splits[0], (C, SITES), 1.0, 6.0, ((0, 2), (1, 8))),
        "conv_weight": noise(arg_keys[1], (TAPS, C, C), (TAPS * C) ** -0.5, 0.109375, ((2, 2),)),
        "neighbours": draw_neighbours(jax.random.fold_in(jax.random.fold_in(arg_keys[4], part), 71), part),
        "cotangent": noise(part_splits[3], (C, SITES), 1.0, 6.0, ((0, 2), (1, 8))),
    }


def take_masked(values, index_row):
    valid = index_row >= 0
    safe = jnp.where(valid, index_row, 0).astype(jnp.int32)
    taken = jnp.take(values, safe, axis=1)
    return jnp.where(valid[None, :], taken, jnp.zeros((), values.dtype))


def reference(features, conv_weight, neighbours, cotangent):
    total = features.shape[1]
    hidden = jnp.zeros((conv_weight.shape[2], total), jnp.float32)
    for offset in range(TAPS):
        gathered = take_masked(features, neighbours[offset])
        hidden = hidden + lax.dot_general(conv_weight[offset], gathered, (((0,), (0,)), ((), ())), preferred_element_type=jnp.float32)
    output = (features.astype(jnp.float32) + jax.nn.silu(hidden)).astype(jnp.bfloat16)
    sigma = jax.nn.sigmoid(hidden)
    grad_hidden = (cotangent.astype(jnp.float32) * sigma * (1.0 + hidden * (1.0 - sigma))).astype(jnp.bfloat16)
    grad_conv = jnp.zeros((conv_weight.shape[1], total), jnp.float32)
    grads = []
    for offset in range(TAPS):
        reversed_rows = take_masked(grad_hidden, neighbours[TAPS - 1 - offset])
        grad_conv = grad_conv + jnp.dot(conv_weight[offset], reversed_rows, preferred_element_type=jnp.float32)
        grads.append(lax.dot_general(features, reversed_rows, (((1,), (1,)), ((), ())), preferred_element_type=jnp.float32))
    grad_features = (cotangent.astype(jnp.float32) + grad_conv).astype(jnp.bfloat16)
    grad_weight = jnp.stack(grads, axis=0)
    return output, grad_features, grad_weight
```

```python
import functools

import jax
import jax.numpy as jnp
from jax import lax
from jax.experimental import pallas as pl
from jax.experimental.pallas import tpu as pltpu
from jax.sharding import PartitionSpec as P

EDGE = 16
FACE = EDGE * EDGE
TAPS = 27
HALO = 384
ROWS = 16
GROUP = 4
SITES = ("brick", "rep")
LINE = ("brick", "chan", "rep")
VMEM = 56 * 1024 * 1024

STEPS = [(k // 3 - 1) * EDGE + k % 3 - 1 for k in range(9)]


def cost(flops, moved):
    return pl.CostEstimate(flops=flops, bytes_accessed=moved, transcendentals=0)


def call(body, outs, scratch, flops, moved, name, scalars=0):
    return pl.pallas_call(
        body,
        out_shape=outs,
        grid_spec=pltpu.PrefetchScalarGridSpec(
            num_scalar_prefetch=scalars, grid=(), scratch_shapes=scratch
        ),
        compiler_params=pltpu.CompilerParams(vmem_limit_bytes=VMEM),
        cost_estimate=cost(flops, moved),
        name=name,
    )


def lay_out(left, middle, right, shifts):
    sites = middle.shape[1]
    length = sites + 2 * HALO
    for at in range(0, middle.shape[0], ROWS):
        rows = pl.ds(at, ROWS)
        shifts[4, rows, :HALO] = left[rows, :]
        shifts[4, rows, HALO : HALO + sites] = middle[rows, :]
        shifts[4, rows, HALO + sites :] = right[rows, :]
        for j, step in enumerate(STEPS):
            if j != 4:
                shifts[j, rows, 128 : length - 128] = shifts[
                    4, rows, 128 + step : length - 128 + step
                ]


def masked(shifts, valid, tap, mask_tap, start, width):
    channels = shifts.shape[1]
    row = valid[pl.ds(mask_tap, 1), pl.ds(start, width)]
    keep = jnp.broadcast_to((row >= 0).astype(jnp.float32), (ROWS, width)).astype(jnp.bfloat16)
    begin = pl.multiple_of(start + HALO + (tap // 9 - 1) * FACE, 128)
    return [
        shifts[tap % 9, at : at + ROWS, pl.ds(begin, width)] * keep
        for at in range(0, channels, ROWS)
    ]


def forward(width, left, middle, right, weights, valid, shifts, start):
    channels = middle.shape[0]
    total = None
    for first in range(0, TAPS, GROUP):
        last = min(first + GROUP, TAPS)
        rows = []
        for tap in range(first, last):
            rows += masked(shifts, valid, tap, tap, start, width)
        part = jnp.dot(
            weights[:, first * channels : last * channels],
            jnp.concatenate(rows, axis=0),
            preferred_element_type=jnp.float32,
        )
        total = part if total is None else total + part
    return total


def own_body(width, left, middle, right, weights, valid, hidden, shifts):
    lay_out(left, middle, right, shifts)

    def block(j, carry):
        start = pl.multiple_of(j * width, width)
        hidden[:, pl.ds(start, width)] = forward(
            width, left, middle, right, weights, valid, shifts, start
        )
        return carry

    lax.fori_loop(0, middle.shape[1] // width, block, 0)


def rest_body(
    width, left, middle, right, weights, valid, begun, features, cotangent, output, grad, first, last, shifts
):
    lay_out(left, middle, right, shifts)

    def block(j, carry):
        start = pl.multiple_of(j * width, width)
        here = pl.ds(start, width)
        hidden = begun[:, here] + forward(width, left, middle, right, weights, valid, shifts, start)
        sigma = jax.nn.sigmoid(hidden)
        output[:, here] = (features[:, here].astype(jnp.float32) + hidden * sigma).astype(jnp.bfloat16)
        grad[:, here] = (
            cotangent[:, here].astype(jnp.float32) * sigma * (1.0 + hidden * (1.0 - sigma))
        ).astype(jnp.bfloat16)
        return carry

    lax.fori_loop(0, middle.shape[1] // width, block, 0)
    first[...] = grad[:, :HALO]
    last[...] = grad[:, grad.shape[1] - HALO :]


def weight_body(
    width, half, rep, left, middle, right, valid, own, rest, kept, sent, shifts, total
):
    lay_out(left, middle, right, shifts)
    share = middle.shape[0]
    total[...] = jnp.zeros_like(total)

    def block(j, carry):
        start = pl.multiple_of(j * width, width)
        here = pl.ds(start, width)
        features = jnp.concatenate([own[:, here], rest[:, here]], axis=0)
        for first in range(0, TAPS, GROUP):
            last = min(first + GROUP, TAPS)
            rows = []
            for tap in range(first, last):
                rows += masked(shifts, valid, TAPS - 1 - tap, TAPS - 1 - tap, start, width)
            total[first * share : last * share, :] += lax.dot_general(
                jnp.concatenate(rows, axis=0),
                features,
                (((1,), (1,)), ((), ())),
                preferred_element_type=jnp.float32,
            )
        return carry

    lax.fori_loop(0, middle.shape[1] // width, block, 0)
    mine = rep[0]
    kept[...] = total[pl.ds(pl.multiple_of(mine * half, ROWS), half), :]
    sent[...] = total[pl.ds(pl.multiple_of((1 - mine) * half, ROWS), half), :].astype(jnp.bfloat16)


def feature_body(width, left, middle, right, valid, weights, own, rest, shifts):
    lay_out(left, middle, right, shifts)
    share = middle.shape[0]

    def block(j, carry):
        start = pl.multiple_of(j * width, width)
        here = pl.ds(start, width)
        total = None
        for first in range(0, TAPS, GROUP):
            last = min(first + GROUP, TAPS)
            rows = []
            for tap in range(first, last):
                rows += masked(shifts, valid, TAPS - 1 - tap, TAPS - 1 - tap, start, width)
            part = jnp.dot(
                weights[:, first * share : last * share],
                jnp.concatenate(rows, axis=0),
                preferred_element_type=jnp.float32,
            )
            total = part if total is None else total + part
        own[:, here] = total[:share]
        rest[:, here] = total[share:].astype(jnp.bfloat16)
        return carry

    lax.fori_loop(0, middle.shape[1] // width, block, 0)


def split_body(bricks, brick, kept, arrived, mine, *pieces):
    size = mine.shape[0]
    for d in range(bricks):
        rows = pl.ds(pl.multiple_of((brick[0] + d) % bricks * size, ROWS), size)
        summed = kept[rows, :] + arrived[rows, :].astype(jnp.float32)
        if d == 0:
            mine[...] = summed
        else:
            pieces[d - 1][...] = summed.astype(jnp.bfloat16)


def merge_body(mine, *rest):
    *pieces, done = rest
    total = mine[...]
    for piece in pieces:
        total += piece[...].astype(jnp.float32)
    done[...] = total.astype(jnp.bfloat16)


def gather_body(bricks, brick, *rest):
    *pieces, side = rest
    size = pieces[0].shape[0]
    for d, piece in enumerate(pieces):
        at = (brick[0] + bricks - d) % bricks * size
        side[pl.ds(pl.multiple_of(at, ROWS), size), :] = piece[...]


def join_body(half, rep, turn, side, other, out, both):
    mine = rep[0]
    both[pl.ds(pl.multiple_of(mine * half, ROWS), half), :] = side[...]
    both[pl.ds(pl.multiple_of((1 - mine) * half, ROWS), half), :] = other[...]
    out[...] = pltpu.roll(both[: out.shape[0], :].astype(jnp.float32), turn[0], 1)


def hop(x, step, over):
    bricks, chans, reps = (lax.axis_size(axis) for axis in LINE)
    pairs = []
    for at in range(bricks * reps):
        to = at + step
        if not 0 <= to < bricks * reps:
            continue
        for chan in range(chans):
            pairs.append(
                (
                    (at // reps * chans + (chan + over) % chans) * reps + at % reps,
                    (to // reps * chans + chan) * reps + to % reps,
                )
            )
    return lax.ppermute(x, LINE, pairs)


def local(features, conv_weight, neighbours, cotangent):
    share, sites = features.shape
    total = conv_weight.shape[1]
    chans, bricks, reps = (lax.axis_size(axis) for axis in ("chan", "brick", "rep"))
    chan, brick, rep = (lax.axis_index(axis) for axis in ("chan", "brick", "rep"))
    width = 512
    f32, bf16 = jnp.float32, jnp.bfloat16
    shape = jax.ShapeDtypeStruct
    length = sites + 2 * HALO
    flops = 2 * TAPS * share * sites

    others = [
        lax.ppermute(features, "chan", [((i + over) % chans, i) for i in range(chans)])
        for over in range(1, chans)
    ]
    head, tail = features[:, :HALO], features[:, sites - HALO :]
    lefts = [hop(tail, 1, over) for over in range(chans)]
    rights = [hop(head, -1, over) for over in range(chans)]
    rest = jnp.concatenate(others, axis=0)
    rest_left = jnp.concatenate(lefts[1:], axis=0)
    rest_right = jnp.concatenate(rights[1:], axis=0)

    ring = lax.dynamic_slice_in_dim(
        jnp.concatenate([conv_weight, conv_weight], axis=1), chan * share, total, axis=1
    )
    by_out = jnp.transpose(ring, (2, 0, 1))
    own_weights = by_out[:, :, :share].reshape(share, TAPS * share)
    rest_weights = by_out[:, :, share:].reshape(share, TAPS * (total - share))
    by_in = jnp.transpose(ring, (1, 0, 2)).reshape(total, TAPS * share)

    begun = call(
        functools.partial(own_body, width),
        shape((share, sites), f32),
        [pltpu.VMEM((9, share, length), bf16)],
        flops * share,
        4 * share * sites,
        "forward_own",
    )(lefts[0], features, rights[0], own_weights, neighbours)
    output, grad, first, last = call(
        functools.partial(rest_body, width),
        (
            shape((share, sites), bf16),
            shape((share, sites), bf16),
            shape((share, HALO), bf16),
            shape((share, HALO), bf16),
        ),
        [pltpu.VMEM((9, total - share, length), bf16)],
        flops * (total - share),
        4 * share * sites,
        "forward_rest",
    )(rest_left, rest, rest_right, rest_weights, neighbours, begun, features, cotangent)

    grad_left, grad_right = hop(last, 1, 0), hop(first, -1, 0)

    piece = -(-TAPS * share // (reps * bricks * ROWS)) * ROWS
    half = piece * bricks
    kept, sent = call(
        functools.partial(weight_body, width, half),
        (shape((half, total), f32), shape((half, total), bf16)),
        [pltpu.VMEM((9, share, length), bf16), pltpu.VMEM((reps * half, total), f32)],
        flops * total,
        4 * share * sites,
        "grad_weight",
        scalars=1,
    )(rep[None], grad_left, grad, grad_right, neighbours, features, rest)
    swap = [(0, 1), (1, 0)]
    arrived = lax.ppermute(sent, "rep", swap)

    own_part, rest_part = call(
        functools.partial(feature_body, width),
        (shape((share, sites), f32), shape((total - share, sites), bf16)),
        [pltpu.VMEM((9, share, length), bf16)],
        flops * total,
        4 * share * sites,
        "grad_features",
    )(grad_left, grad, grad_right, neighbours, by_in)
    terms = [
        lax.ppermute(
            rest_part[(over - 1) * share : over * share],
            "chan",
            [(i, (i + over) % chans) for i in range(chans)],
        )
        for over in range(1, chans)
    ]

    mine, *pieces = call(
        functools.partial(split_body, bricks),
        (shape((piece, total), f32),) + (shape((piece, total), bf16),) * (bricks - 1),
        [],
        0,
        6 * half * total,
        "split",
        scalars=1,
    )(brick[None], kept, arrived)
    turns = [[(i, (i + d) % bricks) for i in range(bricks)] for d in range(1, bricks)]
    pieces = [lax.ppermute(x, "brick", turn) for x, turn in zip(pieces, turns)]
    done = call(
        merge_body,
        shape((piece, total), bf16),
        [],
        0,
        2 * half * total,
        "merge",
    )(mine, *pieces)
    pieces = [done] + [lax.ppermute(done, "brick", turn) for turn in turns]
    side = call(
        functools.partial(gather_body, bricks),
        shape((half, total), bf16),
        [],
        0,
        4 * half * total,
        "gather",
        scalars=1,
    )(brick[None], *pieces)
    other = lax.ppermute(side, "rep", swap)
    grad_weight = call(
        functools.partial(join_body, half),
        shape((TAPS * share, total), f32),
        [pltpu.VMEM((reps * half, total), bf16)],
        0,
        12 * half * total,
        "join",
        scalars=2,
    )(rep[None], (chan * share)[None], side, other)

    grad_features = cotangent.astype(f32) + own_part
    for term in terms:
        grad_features = grad_features + term.astype(f32)
    grad_weight = jnp.transpose(grad_weight.reshape(TAPS, share, total), (0, 2, 1))
    return output, grad_features.astype(bf16), grad_weight


def solution(mesh):
    return jax.shard_map(
        local,
        mesh=mesh,
        in_specs=(
            P("chan", ("scene", "brick", "rep")),
            P(None, None, "chan"),
            P(None, ("scene", "brick", "rep")),
            P("chan", ("scene", "brick", "rep")),
        ),
        out_specs=(
            P("chan", ("scene", "brick", "rep")),
            P("chan", ("scene", "brick", "rep")),
            P("scene", None, "chan"),
        ),
        check_vma=False,
    )
```

```python
import functools

import jax
import jax.numpy as jnp
from jax import lax
from jax.experimental import pallas as pl
from jax.experimental.pallas import tpu as pltpu
from jax.sharding import PartitionSpec as P

EDGE = 16
FACE = EDGE * EDGE
TAPS = 27
HALO = 384
FAR = 2 * HALO
ROWS = 16
GROUP = 4
WIDTH = 768
BACK = 512
LINE = ("brick", "chan", "rep")
MIB = 1024 * 1024
F32, BF16 = jnp.float32, jnp.bfloat16

STEPS = [(k // 3 - 1) * EDGE + k % 3 - 1 for k in range(9)]

HERE = pl.BlockSpec(memory_space=pltpu.VMEM)
SCALAR = pl.BlockSpec(memory_space=pltpu.SMEM)


def kernel(body, name, outs, args, scalars=(), scratch=(), out_specs=None, limit=8, flops=0, moved=MIB):
    single = not isinstance(outs, (tuple, list))
    specs = out_specs or [HERE] * (1 if single else len(outs))
    return pl.pallas_call(
        body,
        out_shape=outs,
        in_specs=[SCALAR] * len(scalars) + [HERE] * len(args),
        out_specs=specs[0] if single else specs,
        scratch_shapes=list(scratch),
        compiler_params=pltpu.CompilerParams(vmem_limit_bytes=limit * MIB),
        cost_estimate=pl.CostEstimate(flops=flops, bytes_accessed=moved, transcendentals=0),
        name=name,
    )(*(x[None] for x in scalars), *args)


def shape(dims, kind=BF16):
    return jax.ShapeDtypeStruct(dims, kind)


def shift(shifts):
    length = shifts.shape[2]
    for at in range(0, shifts.shape[1], ROWS):
        rows = pl.ds(at, ROWS)
        for j, step in enumerate(STEPS):
            if j != 4:
                shifts[j, rows, 128 : length - 128] = shifts[4, rows, 128 + step : length - 128 + step]


def masked(shifts, valid, tap, at_shift, at_valid, width):
    keep = valid[tap, :, pl.ds(at_valid, width)]
    begin = pl.multiple_of(at_shift + (tap // 9 - 1) * FACE, 128)
    return [
        shifts[tap % 9, at : at + ROWS, pl.ds(begin, width)] * keep
        for at in range(0, shifts.shape[1], ROWS)
    ]


def groups():
    return [range(first, min(first + GROUP, TAPS)) for first in range(0, TAPS, GROUP)]


def product(weights, shifts, valid, at_shift, at_valid, width, taps_of):
    channels = shifts.shape[1]
    total = None
    for group in groups():
        rows = []
        for tap in group:
            rows += masked(shifts, valid, taps_of(tap), at_shift, at_valid, width)
        part = jnp.dot(
            weights[:, group[0] * channels : (group[-1] + 1) * channels],
            jnp.concatenate(rows, axis=0),
            preferred_element_type=F32,
        )
        total = part if total is None else total + part
    return total


def pack_body(*refs):
    ends, outs = refs[:6], refs[6:]
    for (features, cotangent, neighbours), out in zip((ends[:3], ends[3:]), outs):
        share = features.shape[0]
        out[...] = jnp.zeros_like(out)
        out[:share, :] = features[...]
        out[share : 2 * share, :HALO] = cotangent[...]
        kept = (neighbours[...] >= 0).astype(F32)
        kept = jnp.concatenate([kept, jnp.zeros((32 - TAPS, HALO), F32)], axis=0)
        out[share : share + 32, HALO:] = kept.astype(BF16)


def pack(features, cotangent, neighbours):
    share, sites = features.shape

    def end(rows, width, at):
        return pl.BlockSpec((rows, width), lambda i: (0, at * (sites // width - 1)))

    rows = share + max(share, 32)
    return pl.pallas_call(
        pack_body,
        grid=(1,),
        out_shape=[shape((rows, FAR))] * 2,
        in_specs=[
            spec
            for at in (1, 0)
            for spec in (end(share, FAR, at), end(share, HALO, at), end(TAPS, HALO, at))
        ],
        out_specs=[pl.BlockSpec((rows, FAR), lambda i: (0, 0))] * 2,
        cost_estimate=pl.CostEstimate(flops=0, bytes_accessed=MIB, transcendentals=0),
        name="pack",
    )(*(features, cotangent, neighbours) * 2)


def weights_body(share, turn, by_out, own, rest, by_in, flat):
    total = by_out.shape[2]
    flat[...] = jnp.zeros_like(flat)
    for group in groups():
        taps = []
        for tap in group:
            ring = pltpu.roll(by_out[tap].astype(F32), turn[0], 1)
            flat[tap * share : (tap + 1) * share, :] = ring
            taps.append(ring)
        first, last = group[0], group[-1] + 1
        own[:, first * share : last * share] = jnp.concatenate(
            [x[:, :share] for x in taps], axis=1
        ).astype(BF16)
        left = total - share
        rest[:, first * left : last * left] = jnp.concatenate(
            [x[:, share:] for x in taps], axis=1
        ).astype(BF16)
    by_in[...] = flat[...].T.astype(BF16)


def own_body(left, middle, right, weights, neighbours, begun, valid, shifts, kept):
    share, sites = middle.shape
    shifts[4, :, :FAR] = left[:share, :]
    shifts[4, :, FAR : FAR + sites] = middle[...]
    shifts[4, :, FAR + sites :] = right[:share, :]
    shift(shifts)
    kept[:, :HALO] = left[share : share + 32, HALO:].astype(F32)
    kept[:TAPS, HALO : HALO + sites] = (neighbours[...] >= 0).astype(F32)
    kept[:, HALO + sites :] = right[share : share + 32, HALO:].astype(F32)
    for tap in range(TAPS):
        valid[tap] = jnp.broadcast_to(kept[tap : tap + 1, :], (ROWS, kept.shape[1])).astype(BF16)

    def block(j, carry):
        start = pl.multiple_of(j * WIDTH, 128)
        begun[:, pl.ds(start, WIDTH)] = product(
            weights, shifts, valid, start + HALO, start, WIDTH, lambda tap: tap
        )
        return carry

    lax.fori_loop(0, begun.shape[1] // WIDTH, block, 0)


def rest_body(
    ends, middle, weights, valid, begun, left, features, right, cotangent, output, grad, shifts, kept
):
    share, sites = features.shape
    shifts[4, :, :FAR] = ends[:, :FAR]
    shifts[4, :, FAR : FAR + sites] = middle[...]
    shifts[4, :, FAR + sites :] = ends[:, FAR:]
    shift(shifts)
    grad[:, :HALO] = left[share : 2 * share, :HALO]
    grad[:, HALO : HALO + sites] = cotangent[...]
    grad[:, HALO + sites :] = right[share : 2 * share, :HALO]
    kept[:, HALO : HALO + sites] = features[...]

    def block(j, carry):
        start = pl.multiple_of(j * WIDTH, 128)
        here = pl.ds(start, WIDTH)
        hidden = begun[:, here] + product(
            weights, shifts, valid, start + HALO, start, WIDTH, lambda tap: tap
        )
        sigma = jax.nn.sigmoid(hidden)
        kept[:, here] = (kept[:, here].astype(F32) + hidden * sigma).astype(BF16)
        grad[:, here] = (
            grad[:, here].astype(F32) * sigma * (1.0 + hidden * (1.0 - sigma))
        ).astype(BF16)
        return carry

    lax.fori_loop(0, begun.shape[1] // WIDTH, block, 0)
    output[...] = kept[:, HALO : HALO + sites]


def weight_body(half, rep, grad, valid, own, rest, kept, sent, shifts, total):
    share, sites = own.shape
    shifts[4] = grad[...]
    shift(shifts)
    total[...] = jnp.zeros_like(total)

    def block(j, carry):
        start = pl.multiple_of(j * BACK, 128)
        here = pl.ds(start, BACK)
        features = jnp.concatenate([own[:, here], rest[:, here]], axis=0)
        for group in groups():
            rows = []
            for tap in group:
                rows += masked(shifts, valid, TAPS - 1 - tap, start + HALO, start + HALO, BACK)
            total[group[0] * share : (group[-1] + 1) * share, :] += lax.dot_general(
                jnp.concatenate(rows, axis=0),
                features,
                (((1,), (1,)), ((), ())),
                preferred_element_type=F32,
            )
        return carry

    lax.fori_loop(0, sites // BACK, block, 0)
    mine = rep[0]
    kept[...] = total[pl.ds(pl.multiple_of(mine * half, ROWS), half), :]
    sent[...] = total[pl.ds(pl.multiple_of((1 - mine) * half, ROWS), half), :].astype(BF16)


def feature_body(shifts, valid, weights, own, rest):
    share, sites = own.shape

    def block(j, carry):
        start = pl.multiple_of(j * BACK, 128)
        here = pl.ds(start, BACK)
        total = product(
            weights, shifts, valid, start + HALO, start + HALO, BACK, lambda tap: TAPS - 1 - tap
        )
        own[:, here] = total[:share]
        rest[:, here] = total[share:].astype(BF16)
        return carry

    lax.fori_loop(0, sites // BACK, block, 0)


def split_body(bricks, brick, kept, arrived, mine, *pieces):
    size = mine.shape[0]
    for d in range(bricks):
        rows = pl.ds(pl.multiple_of((brick[0] + d) % bricks * size, ROWS), size)
        summed = kept[rows, :] + arrived[rows, :].astype(F32)
        if d == 0:
            mine[...] = summed
        else:
            pieces[d - 1][...] = summed.astype(BF16)


def merge_body(mine, *rest):
    *pieces, done = rest
    total = mine[...]
    for piece in pieces:
        total += piece[...].astype(F32)
    done[...] = total.astype(BF16)


def gather_body(bricks, brick, *rest):
    *pieces, side = rest
    size = pieces[0].shape[0]
    for d, piece in enumerate(pieces):
        at = (brick[0] + bricks - d) % bricks * size
        side[pl.ds(pl.multiple_of(at, ROWS), size), :] = piece[...]


def join_body(half, rep, turn, side, other, out, both):
    mine = rep[0]
    both[pl.ds(pl.multiple_of(mine * half, ROWS), half), :] = side[...]
    both[pl.ds(pl.multiple_of((1 - mine) * half, ROWS), half), :] = other[...]
    out[...] = pltpu.roll(both[: out.shape[0], :].astype(F32), turn[0], 1)


def add_body(cotangent, own, *rest):
    *terms, out = rest
    total = cotangent[...].astype(F32) + own[...]
    for term in terms:
        total += term[...].astype(F32)
    out[...] = total.astype(BF16)


def hop(x, step):
    count = lax.axis_size(("brick", "rep"))
    pairs = [(i, i + step) for i in range(count) if 0 <= i + step < count]
    return lax.ppermute(x, ("brick", "rep"), pairs)


def local(features, conv_weight, neighbours, cotangent):
    share, sites = features.shape
    total = conv_weight.shape[1]
    left = total - share
    chans, bricks, reps = (lax.axis_size(axis) for axis in ("chan", "brick", "rep"))
    chan, brick, rep = (lax.axis_index(axis) for axis in ("chan", "brick", "rep"))
    margin = sites + 2 * HALO
    flops = 2 * TAPS * share * sites

    def around(x):
        return [
            lax.ppermute(x, "chan", [((i + over) % chans, i) for i in range(chans)])
            for over in range(1, chans)
        ]

    def stack(parts):
        return parts[0] if len(parts) == 1 else jnp.concatenate(parts, axis=0)

    rest = stack(around(features))
    to_next, to_last = pack(features, cotangent, neighbours)
    before, behind = hop(to_next, 1), hop(to_last, -1)
    ends = stack(around(jnp.concatenate([before[:share], behind[:share]], axis=1)))

    lanes = -(-TAPS * share // 128) * 128
    own_weights, rest_weights, by_in = kernel(
        functools.partial(weights_body, share),
        "weights",
        [shape((share, TAPS * share)), shape((share, TAPS * left)), shape((total, lanes))],
        [jnp.transpose(conv_weight, (0, 2, 1))],
        scalars=[(total - chan * share) % total],
        scratch=[pltpu.VMEM((lanes, total), F32)],
    )
    begun, valid = kernel(
        own_body,
        "forward_own",
        [shape((share, margin), F32), shape((TAPS, ROWS, margin))],
        [before, features, behind, own_weights, neighbours],
        scratch=[pltpu.VMEM((9, share, sites + 2 * FAR), BF16), pltpu.VMEM((32, margin), F32)],
        limit=20,
        flops=flops * share,
    )
    output, grad = kernel(
        rest_body,
        "forward_rest",
        [shape((share, sites)), shape((share, margin))],
        [ends, rest, rest_weights, valid, begun, before, features, behind, cotangent],
        scratch=[
            pltpu.VMEM((9, left, sites + 2 * FAR), BF16),
            pltpu.VMEM((share, margin), BF16),
        ],
        limit=24,
        flops=flops * left,
    )

    piece = -(-TAPS * share // (reps * bricks * ROWS)) * ROWS
    half = piece * bricks
    kept, sent, shifts = kernel(
        functools.partial(weight_body, half),
        "grad_weight",
        [shape((half, total), F32), shape((half, total)), shape((9, share, margin))],
        [grad, valid, features, rest],
        scalars=[rep],
        scratch=[pltpu.VMEM((reps * half, total), F32)],
        limit=12,
        flops=flops * total,
    )
    swap = [(0, 1), (1, 0)]
    arrived = lax.ppermute(sent, "rep", swap)

    own_part, rest_part = kernel(
        feature_body,
        "grad_features",
        [shape((share, sites), F32), shape((left, sites))],
        [shifts, valid, by_in],
        limit=12,
        flops=flops * total,
    )
    terms = [
        lax.ppermute(
            rest_part if left == share else rest_part[(over - 1) * share : over * share],
            "chan",
            [(i, (i + over) % chans) for i in range(chans)],
        )
        for over in range(1, chans)
    ]

    mine, *pieces = kernel(
        functools.partial(split_body, bricks),
        "split",
        [shape((piece, total), F32)] + [shape((piece, total))] * (bricks - 1),
        [kept, arrived],
        scalars=[brick],
    )
    turns = [[(i, (i + d) % bricks) for i in range(bricks)] for d in range(1, bricks)]
    pieces = [lax.ppermute(x, "brick", turn) for x, turn in zip(pieces, turns)]
    done = kernel(merge_body, "merge", shape((piece, total)), [mine, *pieces])
    pieces = [done] + [lax.ppermute(done, "brick", turn) for turn in turns]
    side = kernel(
        functools.partial(gather_body, bricks),
        "gather",
        shape((half, total)),
        pieces,
        scalars=[brick],
    )
    other = lax.ppermute(side, "rep", swap)
    grad_weight = kernel(
        functools.partial(join_body, half),
        "join",
        shape((TAPS * share, total), F32),
        [side, other],
        scalars=[rep, chan * share],
        scratch=[pltpu.VMEM((reps * half, total), BF16)],
    )
    grad_features = kernel(
        add_body, "add", shape((share, sites)), [cotangent, own_part, *terms]
    )
    grad_weight = jnp.transpose(grad_weight.reshape(TAPS, share, total), (0, 2, 1))
    return output, grad_features, grad_weight


def solution(mesh):
    return jax.shard_map(
        local,
        mesh=mesh,
        in_specs=(
            P("chan", ("scene", "brick", "rep")),
            P(None, None, "chan"),
            P(None, ("scene", "brick", "rep")),
            P("chan", ("scene", "brick", "rep")),
        ),
        out_specs=(
            P("chan", ("scene", "brick", "rep")),
            P("chan", ("scene", "brick", "rep")),
            P("scene", None, "chan"),
        ),
        check_vma=False,
    )
```

```python
import functools

import jax
import jax.numpy as jnp
from jax import lax
from jax.experimental import pallas as pl
from jax.experimental.pallas import tpu as pltpu
from jax.sharding import PartitionSpec as P

EDGE = 16
FACE = EDGE * EDGE
TAPS = 27
HALO = 384
FAR = 2 * HALO
ROWS = 16
GROUP = 4
WIDTH = 768
LATER = 25 * 10**7
LINE = ("brick", "chan", "rep")
MIB = 1024 * 1024
F32, BF16 = jnp.float32, jnp.bfloat16

STEPS = [(k // 3 - 1) * EDGE + k % 3 - 1 for k in range(9)]

HERE = pl.BlockSpec(memory_space=pltpu.VMEM)
SCALAR = pl.BlockSpec(memory_space=pltpu.SMEM)


def kernel(body, name, outs, args, scalars=(), scratch=(), aliases={}, limit=8, flops=0):
    single = not isinstance(outs, (tuple, list))
    return pl.pallas_call(
        body,
        out_shape=outs,
        in_specs=[SCALAR] * len(scalars) + [HERE] * len(args),
        out_specs=HERE if single else [HERE] * len(outs),
        scratch_shapes=list(scratch),
        input_output_aliases={len(scalars) + i: o for i, o in aliases.items()},
        compiler_params=pltpu.CompilerParams(vmem_limit_bytes=limit * MIB),
        cost_estimate=pl.CostEstimate(flops=flops, bytes_accessed=MIB, transcendentals=0),
        name=name,
    )(*(x[None] for x in scalars), *args)


def after(body, at):
    def ordered(*refs):
        body(*refs[:at], *refs[at + 1 :])

    return ordered


def shape(dims, kind=BF16):
    return jax.ShapeDtypeStruct(dims, kind)


def shift(shifts, low, high):
    for at in range(0, shifts.shape[1], ROWS):
        rows = pl.ds(at, ROWS)
        for j, step in enumerate(STEPS):
            if j != 4:
                shifts[j, rows, low:high] = shifts[4, rows, low + step : high + step]


def masked(shifts, valid, tap, at_shift, at_valid, width):
    keep = valid[tap, :, pl.ds(at_valid, width)]
    begin = pl.multiple_of(at_shift + (tap // 9 - 1) * FACE, 128)
    return [
        shifts[tap % 9, at : at + ROWS, pl.ds(begin, width)] * keep
        for at in range(0, shifts.shape[1], ROWS)
    ]


def groups():
    return [range(first, min(first + GROUP, TAPS)) for first in range(0, TAPS, GROUP)]


def product(weights, shifts, valid, at_shift, at_valid, width, taps_of):
    channels = shifts.shape[1]
    total = None
    for group in groups():
        rows = []
        for tap in group:
            rows += masked(shifts, valid, taps_of(tap), at_shift, at_valid, width)
        part = jnp.dot(
            weights[:, group[0] * channels : (group[-1] + 1) * channels],
            jnp.concatenate(rows, axis=0),
            preferred_element_type=F32,
        )
        total = part if total is None else total + part
    return total


def pack_body(rep, *refs):
    ends, outs = refs[:6], refs[6:]
    for at, (features, cotangent, neighbours) in enumerate((ends[:3], ends[3:])):
        share = features.shape[0]
        kept = (neighbours[...] >= 0).astype(F32)
        kept = jnp.concatenate([kept, jnp.zeros((32 - TAPS, HALO), F32)], axis=0).astype(BF16)

        def fill(out):
            out[...] = jnp.zeros_like(out)
            out[:share, :] = features[...]
            out[share : 2 * share, :HALO] = cotangent[...]
            out[share : share + 32, HALO:] = kept

        pl.when(rep[0] == at)(functools.partial(fill, outs[0]))
        pl.when(rep[0] != at)(functools.partial(fill, outs[1]))


def pack(rep, features, cotangent, neighbours):
    share, sites = features.shape

    def end(rows, width, at):
        return pl.BlockSpec((rows, width), lambda i: (0, at * (sites // width - 1)))

    rows = share + max(share, 32)
    return pl.pallas_call(
        pack_body,
        grid=(1,),
        out_shape=[shape((rows, FAR))] * 2,
        in_specs=[SCALAR]
        + [
            spec
            for at in (1, 0)
            for spec in (end(share, FAR, at), end(share, HALO, at), end(TAPS, HALO, at))
        ],
        out_specs=[pl.BlockSpec((rows, FAR), lambda i: (0, 0))] * 2,
        cost_estimate=pl.CostEstimate(flops=0, bytes_accessed=MIB, transcendentals=0),
        name="pack",
    )(rep[None], *(features, cotangent, neighbours) * 2)


def ends_body(rep, core, line, before, behind, both):
    share = both.shape[0]

    def fill(first, second):
        before[...] = first[...]
        behind[...] = second[...]
        both[:, :FAR] = first[:share, :]
        both[:, FAR:] = second[:share, :]

    pl.when(rep[0] == 0)(functools.partial(fill, line, core))
    pl.when(rep[0] != 0)(functools.partial(fill, core, line))


def prepare_body(
    turn, by_out, features, neighbours, own, rest, by_in, shifts, valid, flat, kept
):
    total = by_out.shape[2]
    share, sites = features.shape
    flat[...] = jnp.zeros_like(flat)
    for group in groups():
        taps = []
        for tap in group:
            ring = pltpu.roll(by_out[tap].astype(F32), turn[0], 1)
            flat[tap * share : (tap + 1) * share, :] = ring
            taps.append(ring)
        first, last = group[0], group[-1] + 1
        own[:, first * share : last * share] = jnp.concatenate(
            [x[:, :share] for x in taps], axis=1
        ).astype(BF16)
        left = total - share
        rest[:, first * left : last * left] = jnp.concatenate(
            [x[:, share:] for x in taps], axis=1
        ).astype(BF16)
    by_in[...] = flat[...].T.astype(BF16)
    shifts[4, :, FAR : FAR + sites] = features[...]
    shift(shifts, FAR + 128, FAR + sites - 128)
    kept[...] = (neighbours[...] >= 0).astype(F32)
    for tap in range(TAPS):
        valid[tap, :, HALO : HALO + sites] = jnp.broadcast_to(
            kept[tap : tap + 1, :], (ROWS, sites)
        ).astype(BF16)


def own_body(left, right, weights, shifts_in, valid_in, begun, shifts, valid, kept):
    del shifts_in, valid_in
    share = begun.shape[0]
    far = shifts.shape[2] - FAR
    for side, at, start in ((left, 0, 128), (right, 1, far - 128)):
        shifts[4, :, at * far : at * far + FAR] = side[:share, :]
        shift(shifts, start, start + FAR)
        kept[...] = side[share : share + 32, HALO:].astype(F32)
        begin = at * (valid.shape[2] - HALO)
        for tap in range(TAPS):
            valid[tap, :, begin : begin + HALO] = jnp.broadcast_to(
                kept[tap : tap + 1, :], (ROWS, HALO)
            ).astype(BF16)

    def block(j, carry):
        start = pl.multiple_of(j * WIDTH, 128)
        begun[:, pl.ds(start, WIDTH)] = product(
            weights, shifts, valid, start + HALO, start, WIDTH, lambda tap: tap
        )
        return carry

    lax.fori_loop(0, begun.shape[1] // WIDTH, block, 0)


def rest_body(
    ends, middle, weights, valid, begun, left, features, right, cotangent, output, grad, shifts, kept
):
    share, sites = features.shape
    shifts[4, :, :FAR] = ends[:, :FAR]
    shifts[4, :, FAR : FAR + sites] = middle[...]
    shifts[4, :, FAR + sites :] = ends[:, FAR:]
    shift(shifts, 128, shifts.shape[2] - 128)
    grad[:, :HALO] = left[share : 2 * share, :HALO]
    grad[:, HALO : HALO + sites] = cotangent[...]
    grad[:, HALO + sites :] = right[share : 2 * share, :HALO]
    kept[:, HALO : HALO + sites] = features[...]

    def block(j, carry):
        start = pl.multiple_of(j * WIDTH, 128)
        here = pl.ds(start, WIDTH)
        hidden = begun[:, here] + product(
            weights, shifts, valid, start + HALO, start, WIDTH, lambda tap: tap
        )
        sigma = jax.nn.sigmoid(hidden)
        kept[:, here] = (kept[:, here].astype(F32) + hidden * sigma).astype(BF16)
        grad[:, here] = (
            grad[:, here].astype(F32) * sigma * (1.0 + hidden * (1.0 - sigma))
        ).astype(BF16)
        return carry

    lax.fori_loop(0, begun.shape[1] // WIDTH, block, 0)
    output[...] = kept[:, HALO : HALO + sites]


def weight_body(half, rep, grad, valid, own, rest, kept, sent, shifts, total):
    share, sites = own.shape
    shifts[4] = grad[...]
    shift(shifts, 128, shifts.shape[2] - 128)
    total[...] = jnp.zeros_like(total)

    def block(j, carry):
        start = pl.multiple_of(j * WIDTH, 128)
        here = pl.ds(start, WIDTH)
        features = jnp.concatenate([own[:, here], rest[:, here]], axis=0).T
        for group in groups():
            rows = []
            for tap in group:
                rows += masked(shifts, valid, TAPS - 1 - tap, start + HALO, start + HALO, WIDTH)
            total[group[0] * share : (group[-1] + 1) * share, :] += jnp.dot(
                jnp.concatenate(rows, axis=0), features, preferred_element_type=F32
            )
        return carry

    lax.fori_loop(0, sites // WIDTH, block, 0)
    mine = rep[0]
    kept[...] = total[pl.ds(pl.multiple_of(mine * half, ROWS), half), :]
    sent[...] = total[pl.ds(pl.multiple_of((1 - mine) * half, ROWS), half), :].astype(BF16)


def feature_body(part, shifts, valid, weights, *refs):
    own, rest = refs[-2:]
    share, sites = own.shape
    begin = part * sites // 2

    def block(j, carry):
        start = pl.multiple_of(begin + j * WIDTH, 128)
        here = pl.ds(start, WIDTH)
        at = pl.multiple_of(start + HALO, 128)
        total = product(weights, shifts, valid, at, at, WIDTH, lambda tap: TAPS - 1 - tap)
        own[:, here] = total[:share]
        rest[:, here] = total[share:].astype(BF16)
        return carry

    lax.fori_loop(0, sites // 2 // WIDTH, block, 0)


def split_body(brick, kept, arrived, mine, sent):
    size = mine.shape[0]
    at = brick[0] % 2
    mine_rows = pl.ds(pl.multiple_of(at * size, ROWS), size)
    sent_rows = pl.ds(pl.multiple_of((1 - at) * size, ROWS), size)
    mine[...] = kept[mine_rows, :] + arrived[mine_rows, :].astype(F32)
    sent[...] = (kept[sent_rows, :] + arrived[sent_rows, :].astype(F32)).astype(BF16)


def merge_body(mine, other, out):
    out[...] = (mine[...].astype(F32) + other[...].astype(F32)).astype(BF16)


def gather_body(brick, mine, other, side):
    size = mine.shape[0]
    at = brick[0] % 2
    side[pl.ds(pl.multiple_of(at * size, ROWS), size), :] = mine[...]
    side[pl.ds(pl.multiple_of((1 - at) * size, ROWS), size), :] = other[...]


def join_body(half, rep, turn, side, other, out, both):
    mine = rep[0]
    both[pl.ds(pl.multiple_of(mine * half, ROWS), half), :] = side[...]
    both[pl.ds(pl.multiple_of((1 - mine) * half, ROWS), half), :] = other[...]
    out[...] = pltpu.roll(both[: out.shape[0], :].astype(F32), turn[0], 1)


def add_body(cotangent, own, *rest):
    *terms, out = rest
    total = cotangent[...].astype(F32) + own[...]
    for term in terms:
        total += term[...].astype(F32)
    out[...] = total.astype(BF16)


def line_swap(x):
    count = lax.axis_size(("brick", "rep"))
    pairs = [p for i in range(1, count - 1, 2) for p in ((i, i + 1), (i + 1, i))]
    return lax.ppermute(x, ("brick", "rep"), pairs)


def local(features, conv_weight, neighbours, cotangent):
    share, sites = features.shape
    total = conv_weight.shape[1]
    left = total - share
    chans, bricks, reps = (lax.axis_size(axis) for axis in ("chan", "brick", "rep"))
    chan, brick, rep = (lax.axis_index(axis) for axis in ("chan", "brick", "rep"))
    margin = sites + 2 * HALO
    flops = 2 * TAPS * share * sites

    def around(x):
        return [
            lax.ppermute(x, "chan", [((i + over) % chans, i) for i in range(chans)])
            for over in range(1, chans)
        ]

    def stack(parts):
        return parts[0] if len(parts) == 1 else jnp.concatenate(parts, axis=0)

    assert reps == 2
    swap = [(0, 1), (1, 0)]
    rest = stack(around(features))
    to_core, to_line = pack(rep, features, cotangent, neighbours)
    line = line_swap(to_line)
    core = lax.ppermute(to_core, "rep", swap)
    lanes = -(-TAPS * share // 128) * 128
    own_weights, rest_weights, by_in, shifts, valid = kernel(
        prepare_body,
        "prepare",
        [
            shape((share, TAPS * share)),
            shape((share, TAPS * left)),
            shape((total, lanes)),
            shape((9, share, sites + 2 * FAR)),
            shape((TAPS, ROWS, margin)),
        ],
        [jnp.transpose(conv_weight, (0, 2, 1)), features, neighbours],
        scalars=[(total - chan * share) % total],
        scratch=[pltpu.VMEM((lanes, total), F32), pltpu.VMEM((TAPS, sites), F32)],
    )
    before, behind, both = kernel(
        after(ends_body, 1),
        "ends",
        [shape(core.shape), shape(core.shape), shape((share, 2 * FAR))],
        [own_weights, core, line],
        scalars=[rep],
    )
    ends = stack(around(both))

    begun, _, valid = kernel(
        own_body,
        "forward_own",
        [shape((share, margin), F32), shape(shifts.shape), shape(valid.shape)],
        [before, behind, own_weights, shifts, valid],
        scratch=[pltpu.VMEM((32, HALO), F32)],
        aliases={3: 1, 4: 2},
    )
    output, grad = kernel(
        rest_body,
        "forward_rest",
        [shape((share, sites)), shape((share, margin))],
        [ends, rest, rest_weights, valid, begun, before, features, behind, cotangent],
        scratch=[
            pltpu.VMEM((9, left, sites + 2 * FAR), BF16),
            pltpu.VMEM((share, margin), BF16),
        ],
        limit=24,
        flops=flops * left,
    )

    piece = -(-TAPS * share // (reps * bricks * ROWS)) * ROWS
    half = piece * bricks
    kept, sent, shifts = kernel(
        functools.partial(weight_body, half),
        "grad_weight",
        [shape((half, total), F32), shape((half, total)), shape((9, share, margin))],
        [grad, valid, features, rest],
        scalars=[rep],
        scratch=[pltpu.VMEM((reps * half, total), F32)],
        limit=12,
        flops=flops * total,
    )
    arrived = lax.ppermute(sent, "rep", swap)

    def feature_part(part, first, so_far):
        return kernel(
            after(functools.partial(feature_body, part), 0),
            "grad_features_%d" % part,
            [shape((share, sites), F32), shape((left, sites))],
            [first, shifts, valid, by_in, *so_far],
            aliases={4 + i: i for i in range(len(so_far))},
            limit=12,
            flops=flops * total // 2,
        )

    parts = feature_part(0, kept, [])
    size = half // 2
    mine, sent = kernel(
        after(split_body, 1),
        "split",
        [shape((size, total), F32), shape((size, total))],
        [parts[0], kept, arrived],
        scalars=[brick],
        flops=LATER,
    )
    pairs = [(i, i ^ 1) for i in range(bricks)]
    arrived = lax.ppermute(sent, "brick", pairs)
    own, other = feature_part(1, mine, parts)
    terms = [
        lax.ppermute(
            other if left == share else other[(over - 1) * share : over * share],
            "chan",
            [(i, (i + over) % chans) for i in range(chans)],
        )
        for over in range(1, chans)
    ]
    mine = kernel(
        after(merge_body, 0),
        "merge_1",
        shape((size, total)),
        [own, mine, arrived],
        flops=LATER,
    )
    step = 2
    while step < bricks:
        other = lax.ppermute(mine, "brick", [(i, i ^ step) for i in range(bricks)])
        step *= 2
        mine = kernel(
            merge_body, "merge_%d" % step, shape((size, total)), [mine, other], flops=LATER
        )
    other = lax.ppermute(mine, "brick", pairs)
    side = kernel(
        gather_body, "gather", shape((half, total)), [mine, other], scalars=[brick], flops=LATER
    )
    other = lax.ppermute(side, "rep", swap)
    grad_weight = kernel(
        functools.partial(join_body, half),
        "join",
        shape((TAPS * share, total), F32),
        [side, other],
        scalars=[rep, chan * share],
        scratch=[pltpu.VMEM((reps * half, total), BF16)],
        flops=LATER,
    )
    grad_features = kernel(add_body, "add", shape((share, sites)), [cotangent, own, *terms])
    grad_weight = jnp.transpose(grad_weight.reshape(TAPS, share, total), (0, 2, 1))
    return output, grad_features, grad_weight


def solution(mesh):
    return jax.shard_map(
        local,
        mesh=mesh,
        in_specs=(
            P("chan", ("scene", "brick", "rep")),
            P(None, None, "chan"),
            P(None, ("scene", "brick", "rep")),
            P("chan", ("scene", "brick", "rep")),
        ),
        out_specs=(
            P("chan", ("scene", "brick", "rep")),
            P("chan", ("scene", "brick", "rep")),
            P("scene", None, "chan"),
        ),
        check_vma=False,
    )
```

```python
import functools

import jax
import jax.numpy as jnp
from jax import lax
from jax.experimental import pallas as pl
from jax.experimental.pallas import tpu as pltpu
from jax.sharding import PartitionSpec as P

EDGE = 16
FACE = EDGE * EDGE
TAPS = 27
HALO = 384
FAR = 2 * HALO
NEAR = 640
LEAD = 896
NINE = 9
ROWS = 16
GROUP = 4
WIDTH = 768
LATER = 25 * 10**7
LINE = ("brick", "chan", "rep")
MIB = 1024 * 1024
F32, BF16 = jnp.float32, jnp.bfloat16

STEPS = [(k // 3 - 1) * EDGE + k % 3 - 1 for k in range(9)]

HERE = pl.BlockSpec(memory_space=pltpu.VMEM)
SCALAR = pl.BlockSpec(memory_space=pltpu.SMEM)


def kernel(body, name, outs, args, scalars=(), scratch=(), aliases={}, limit=8, flops=0, space=HERE):
    single = not isinstance(outs, (tuple, list))
    return pl.pallas_call(
        body,
        out_shape=outs,
        in_specs=[SCALAR] * len(scalars) + [space] * len(args),
        out_specs=HERE if single else [HERE] * len(outs),
        scratch_shapes=list(scratch),
        input_output_aliases={len(scalars) + i: o for i, o in aliases.items()},
        compiler_params=pltpu.CompilerParams(vmem_limit_bytes=limit * MIB),
        cost_estimate=pl.CostEstimate(flops=flops, bytes_accessed=MIB, transcendentals=0),
        name=name,
    )(*(x[None] for x in scalars), *args)


def after(body, at):
    def ordered(*refs):
        body(*refs[:at], *refs[at + 1 :])

    return ordered


def shape(dims, kind=BF16):
    return jax.ShapeDtypeStruct(dims, kind)


def shift(shifts, low, high):
    for at in range(0, shifts.shape[1], ROWS):
        rows = pl.ds(at, ROWS)
        for j, step in enumerate(STEPS):
            if j != 4:
                shifts[j, rows, low:high] = shifts[4, rows, low + step : high + step]


def masked(shifts, valid, tap, at_shift, at_valid, width):
    keep = valid[tap, :, pl.ds(at_valid, width)]
    begin = pl.multiple_of(at_shift + (tap // 9 - 1) * FACE, 128)
    return [
        shifts[tap % 9, at : at + ROWS, pl.ds(begin, width)] * keep
        for at in range(0, shifts.shape[1], ROWS)
    ]


def groups(count=GROUP):
    return [range(first, min(first + count, TAPS)) for first in range(0, TAPS, count)]


def product(weights, shifts, valid, at_shift, at_valid, width, taps_of):
    channels = shifts.shape[1]
    total = None
    for group in groups():
        rows = []
        for tap in group:
            rows += masked(shifts, valid, taps_of(tap), at_shift, at_valid, width)
        part = jnp.dot(
            weights[:, group[0] * channels : (group[-1] + 1) * channels],
            jnp.concatenate(rows, axis=0),
            preferred_element_type=F32,
        )
        total = part if total is None else total + part
    return total


def pack_body(rep, *refs):
    ends, outs = refs[:6], refs[6:]
    for at, (features, cotangent, neighbours) in enumerate((ends[:3], ends[3:])):
        share = features.shape[0]
        kept = (neighbours[...] >= 0).astype(F32)
        kept = jnp.concatenate([kept, jnp.zeros((32 - TAPS, HALO), F32)], axis=0).astype(BF16)

        def fill(out):
            out[...] = jnp.zeros_like(out)
            out[:share, :] = features[...]
            out[share : 2 * share, :HALO] = cotangent[...]
            out[share : share + 32, HALO:] = kept

        pl.when(rep[0] == at)(functools.partial(fill, outs[0]))
        pl.when(rep[0] != at)(functools.partial(fill, outs[1]))


def pack(rep, features, cotangent, neighbours):
    share, sites = features.shape

    def end(rows, width, at):
        return pl.BlockSpec((rows, width), lambda i: (0, at * (sites // width - 1)))

    rows = share + max(share, 32)
    return pl.pallas_call(
        pack_body,
        grid=(1,),
        out_shape=[shape((rows, FAR))] * 2,
        in_specs=[SCALAR]
        + [
            spec
            for at in (1, 0)
            for spec in (end(share, FAR, at), end(share, HALO, at), end(TAPS, HALO, at))
        ],
        out_specs=[pl.BlockSpec((rows, FAR), lambda i: (0, 0))] * 2,
        cost_estimate=pl.CostEstimate(flops=0, bytes_accessed=MIB, transcendentals=0),
        name="pack",
    )(rep[None], *(features, cotangent, neighbours) * 2)


def ends_body(rep, core, line, before, behind, both):
    share = both.shape[0]

    def fill(first, second):
        before[...] = first[...]
        behind[...] = second[...]
        both[:, :NEAR] = first[:share, FAR - NEAR :]
        both[:, NEAR:] = second[:share, :NEAR]

    pl.when(rep[0] == 0)(functools.partial(fill, line, core))
    pl.when(rep[0] != 0)(functools.partial(fill, core, line))


def prepare_body(
    turn, by_out, features, neighbours, own, rest, by_in, shifts, valid, flat, kept, taken, near, done
):
    total = by_out.shape[2]
    share, sites = features.shape
    copies = [
        pltpu.make_async_copy(source, target, done.at[i])
        for i, (source, target) in enumerate(
            [
                (by_out, taken),
                (features, shifts.at[4, :, pl.ds(FAR, sites)]),
                (neighbours, near),
            ]
        )
    ]
    for copy in copies:
        copy.start()
    copies[0].wait()
    flat[...] = jnp.zeros_like(flat)
    for group in groups():
        taps = []
        for tap in group:
            ring = pltpu.roll(taken[tap].astype(F32), turn[0], 1)
            flat[tap * share : (tap + 1) * share, :] = ring
            taps.append(ring)
        first, last = group[0], group[-1] + 1
        own[:, first * share : last * share] = jnp.concatenate(
            [x[:, :share] for x in taps], axis=1
        ).astype(BF16)
        left = total - share
        rest[:, first * left : last * left] = jnp.concatenate(
            [x[:, share:] for x in taps], axis=1
        ).astype(BF16)
    by_in[...] = flat[...].T.astype(BF16)
    copies[1].wait()
    shift(shifts, FAR + 128, FAR + sites - 128)
    copies[2].wait()
    kept[...] = (near[...] >= 0).astype(F32)
    for tap in range(TAPS):
        valid[tap, :, HALO : HALO + sites] = jnp.broadcast_to(
            kept[tap : tap + 1, :], (ROWS, sites)
        ).astype(BF16)


def own_body(left, right, weights, shifts_in, valid_in, begun, shifts, valid, kept):
    del shifts_in, valid_in
    share = begun.shape[0]
    far = shifts.shape[2] - FAR
    for side, at, start in ((left, 0, 128), (right, 1, far - 128)):
        shifts[4, :, at * far : at * far + FAR] = side[:share, :]
        shift(shifts, start, start + FAR)
        kept[...] = side[share : share + 32, HALO:].astype(F32)
        begin = at * (valid.shape[2] - HALO)
        for tap in range(TAPS):
            valid[tap, :, begin : begin + HALO] = jnp.broadcast_to(
                kept[tap : tap + 1, :], (ROWS, HALO)
            ).astype(BF16)

    def block(j, carry):
        start = pl.multiple_of(j * WIDTH, 128)
        begun[:, pl.ds(start, WIDTH)] = product(
            weights, shifts, valid, start + HALO, start, WIDTH, lambda tap: tap
        )
        return carry

    lax.fori_loop(0, begun.shape[1] // WIDTH, block, 0)


def arrive_body(rest, own_in, shifts, across, own):
    del own_in
    sites = rest.shape[1]
    shifts[4, :, FAR : FAR + sites] = rest[...]
    shift(shifts, FAR + 128, FAR + sites - 128)

    def block(j, carry):
        start = pl.multiple_of(j * WIDTH, 128)
        here = pl.ds(pl.multiple_of(start + FAR, 128), WIDTH)
        across[pl.ds(start, WIDTH), :] = jnp.concatenate(
            [own[4, :, here], shifts[4, :, here]], axis=0
        ).T
        return carry

    lax.fori_loop(0, sites // WIDTH, block, 0)


def rest_body(
    ends,
    shifts_in,
    weights,
    valid_in,
    begun,
    left,
    right,
    own,
    cotangent,
    output,
    grads,
    valid,
    shifts,
    grad,
    kept,
):
    del shifts_in, valid_in
    share, sites = cotangent.shape
    far = shifts.shape[2] - FAR
    shifts[4, :, : FAR - NEAR] = jnp.zeros((shifts.shape[1], FAR - NEAR), BF16)
    shifts[4, :, FAR - NEAR : FAR] = ends[:, :NEAR]
    shifts[4, :, far : far + NEAR] = ends[:, NEAR:]
    shifts[4, :, far + NEAR :] = jnp.zeros((shifts.shape[1], FAR - NEAR), BF16)
    shift(shifts, 128, 128 + FAR)
    shift(shifts, far - 128, far + FAR - 128)
    lead = LEAD + 128
    grad[:, lead : lead + HALO] = left[share : 2 * share, :HALO]
    grad[:, lead + HALO : lead + HALO + sites] = cotangent[...]
    grad[:, lead + HALO + sites :] = right[share : 2 * share, :HALO]

    def spread(start):
        for at in range(0, share, ROWS):
            rows = pl.ds(at, ROWS)
            window = grad[rows, pl.ds(start, WIDTH + 256)]
            for j, step in enumerate(STEPS):
                grads[j, rows, pl.ds(start, WIDTH)] = window[:, 128 + step : 128 + step + WIDTH]

    def block(j, carry):
        start = pl.multiple_of(j * WIDTH, 128)
        spread(start)
        here = pl.ds(start, WIDTH)
        there = pl.ds(pl.multiple_of(start + lead, 128), WIDTH)
        hidden = begun[:, here] + product(
            weights, shifts, valid, start + HALO, start, WIDTH, lambda tap: tap
        )
        sigma = jax.nn.sigmoid(hidden)
        features = own[4, :, pl.ds(pl.multiple_of(start + HALO, 128), WIDTH)]
        kept[:, here] = (features.astype(F32) + hidden * sigma).astype(BF16)
        grad[:, there] = (
            grad[:, there].astype(F32) * sigma * (1.0 + hidden * (1.0 - sigma))
        ).astype(BF16)
        return carry

    count = begun.shape[1] // WIDTH
    lax.fori_loop(0, count, block, 0)
    spread(count * WIDTH)
    output[...] = kept[:, HALO : HALO + sites]


def weight_body(half, rep, across, valid_in, grads_in, kept, sent, valid, grads, total):
    del valid_in, grads_in
    share, sites = grads.shape[1], across.shape[0]
    total[...] = jnp.zeros_like(total)

    def block(j, carry):
        start = pl.multiple_of(j * WIDTH, 128)
        features = across[pl.ds(start, WIDTH), :]
        for group in groups(NINE):
            rows = []
            for tap in group:
                rows += masked(
                    grads, valid, TAPS - 1 - tap, start + HALO + LEAD, start + HALO, WIDTH
                )
            total[group[0] * share : (group[-1] + 1) * share, :] += jnp.dot(
                jnp.concatenate(rows, axis=0), features, preferred_element_type=F32
            )
        return carry

    lax.fori_loop(0, sites // WIDTH, block, 0)
    mine = rep[0]
    kept[...] = total[pl.ds(pl.multiple_of(mine * half, ROWS), half), :]
    sent[...] = total[pl.ds(pl.multiple_of((1 - mine) * half, ROWS), half), :].astype(BF16)


def feature_body(part, weights, valid, grads, *refs):
    own, rest = refs[-2:]
    share, sites = own.shape
    begin = part * sites // 2

    def block(j, carry):
        start = pl.multiple_of(begin + j * WIDTH, 128)
        here = pl.ds(start, WIDTH)
        total = product(
            weights,
            grads,
            valid,
            start + HALO + LEAD,
            start + HALO,
            WIDTH,
            lambda tap: TAPS - 1 - tap,
        )
        own[:, here] = total[:share]
        rest[:, here] = total[share:].astype(BF16)
        return carry

    lax.fori_loop(0, sites // 2 // WIDTH, block, 0)


def split_body(brick, kept, arrived, mine, sent):
    size = mine.shape[0]
    at = brick[0] % 2
    mine_rows = pl.ds(pl.multiple_of(at * size, ROWS), size)
    sent_rows = pl.ds(pl.multiple_of((1 - at) * size, ROWS), size)
    mine[...] = kept[mine_rows, :] + arrived[mine_rows, :].astype(F32)
    sent[...] = (kept[sent_rows, :] + arrived[sent_rows, :].astype(F32)).astype(BF16)


def merge_body(mine, other, out):
    out[...] = (mine[...].astype(F32) + other[...].astype(F32)).astype(BF16)


def gather_body(brick, mine, other, side):
    size = mine.shape[0]
    at = brick[0] % 2
    side[pl.ds(pl.multiple_of(at * size, ROWS), size), :] = mine[...]
    side[pl.ds(pl.multiple_of((1 - at) * size, ROWS), size), :] = other[...]


def join_body(half, rep, turn, side, other, out, both):
    mine = rep[0]
    both[pl.ds(pl.multiple_of(mine * half, ROWS), half), :] = side[...]
    both[pl.ds(pl.multiple_of((1 - mine) * half, ROWS), half), :] = other[...]
    out[...] = pltpu.roll(both[: out.shape[0], :].astype(F32), turn[0], 1)


def add_body(cotangent, own, *rest):
    *terms, out = rest
    total = cotangent[...].astype(F32) + own[...]
    for term in terms:
        total += term[...].astype(F32)
    out[...] = total.astype(BF16)


def line_swap(x):
    count = lax.axis_size(("brick", "rep"))
    pairs = [p for i in range(1, count - 1, 2) for p in ((i, i + 1), (i + 1, i))]
    return lax.ppermute(x, ("brick", "rep"), pairs)


def local(features, conv_weight, neighbours, cotangent):
    share, sites = features.shape
    total = conv_weight.shape[1]
    left = total - share
    chans, bricks, reps = (lax.axis_size(axis) for axis in ("chan", "brick", "rep"))
    chan, brick, rep = (lax.axis_index(axis) for axis in ("chan", "brick", "rep"))
    margin = sites + 2 * HALO
    flops = 2 * TAPS * share * sites

    def around(x):
        return [
            lax.ppermute(x, "chan", [((i + over) % chans, i) for i in range(chans)])
            for over in range(1, chans)
        ]

    def stack(parts):
        return parts[0] if len(parts) == 1 else jnp.concatenate(parts, axis=0)

    assert reps == 2
    swap = [(0, 1), (1, 0)]
    rest = stack(around(features))
    to_core, to_line = pack(rep, features, cotangent, neighbours)
    line = line_swap(to_line)
    core = lax.ppermute(to_core, "rep", swap)
    lanes = -(-TAPS * share // 128) * 128
    own_weights, rest_weights, by_in, shifts, valid = kernel(
        prepare_body,
        "prepare",
        [
            shape((share, TAPS * share)),
            shape((share, TAPS * left)),
            shape((total, lanes)),
            shape((9, share, sites + 2 * FAR)),
            shape((TAPS, ROWS, margin)),
        ],
        [jnp.transpose(conv_weight, (0, 2, 1)), features, neighbours],
        scalars=[(total - chan * share) % total],
        scratch=[
            pltpu.VMEM((lanes, total), F32),
            pltpu.VMEM((TAPS, sites), F32),
            pltpu.VMEM((TAPS, share, total), BF16),
            pltpu.VMEM((TAPS, sites), jnp.int32),
            pltpu.SemaphoreType.DMA((3,)),
        ],
        space=pl.BlockSpec(memory_space=pl.ANY),
    )
    before, behind, both = kernel(
        after(ends_body, 1),
        "ends",
        [shape(core.shape), shape(core.shape), shape((share, 2 * NEAR))],
        [own_weights, core, line],
        scalars=[rep],
    )
    ends = stack(around(both))
    begun, own_shifts, valid = kernel(
        own_body,
        "forward_own",
        [shape((share, margin), F32), shape(shifts.shape), shape(valid.shape)],
        [before, behind, own_weights, shifts, valid],
        scratch=[pltpu.VMEM((32, HALO), F32)],
        aliases={3: 1, 4: 2},
    )
    rest_shifts, across, own_shifts = kernel(
        arrive_body,
        "arrive",
        [shape((9, left, sites + 2 * FAR)), shape((sites, total)), shape(own_shifts.shape)],
        [rest, own_shifts],
        aliases={1: 2},
    )
    output, grads, valid, _ = kernel(
        rest_body,
        "forward_rest",
        [
            shape((share, sites)),
            shape((9, share, margin + WIDTH)),
            shape(valid.shape),
            shape(rest_shifts.shape),
        ],
        [ends, rest_shifts, rest_weights, valid, begun, before, behind, own_shifts, cotangent],
        scratch=[
            pltpu.VMEM((share, LEAD + 128 + margin), BF16),
            pltpu.VMEM((share, margin), BF16),
        ],
        aliases={1: 3, 3: 2},
        flops=flops * left,
    )

    piece = -(-TAPS * share // (reps * bricks * ROWS)) * ROWS
    half = piece * bricks
    kept, sent, valid, grads = kernel(
        functools.partial(weight_body, half),
        "grad_weight",
        [shape((half, total), F32), shape((half, total)), shape(valid.shape), shape(grads.shape)],
        [across, valid, grads],
        scalars=[rep],
        scratch=[pltpu.VMEM((reps * half, total), F32)],
        aliases={1: 2, 2: 3},
        flops=flops * total,
    )
    arrived = lax.ppermute(sent, "rep", swap)

    def feature_part(part, body, args, kept):
        outs = [shape((share, sites), F32), shape((left, sites))]
        return kernel(
            body,
            "grad_features_%d" % part,
            [shape(x.shape) for x in kept] + outs,
            args,
            aliases={len(args) - len(kept) + i: i for i in range(len(kept))}
            if part == 0
            else {len(args) - 2 + i: i for i in range(2)},
            flops=flops * total // 2,
        )

    valid, grads, *parts = feature_part(
        0, functools.partial(feature_body, 0), [by_in, valid, grads], [valid, grads]
    )
    size = half // 2
    mine, sent = kernel(
        after(split_body, 1),
        "split",
        [shape((size, total), F32), shape((size, total))],
        [parts[0], kept, arrived],
        scalars=[brick],
        flops=LATER,
    )
    pairs = [(i, i ^ 1) for i in range(bricks)]
    arrived = lax.ppermute(sent, "brick", pairs)
    own, other = feature_part(
        1, after(functools.partial(feature_body, 1), 0), [mine, by_in, valid, grads, *parts], []
    )
    terms = [
        lax.ppermute(
            other if left == share else other[(over - 1) * share : over * share],
            "chan",
            [(i, (i + over) % chans) for i in range(chans)],
        )
        for over in range(1, chans)
    ]
    mine = kernel(
        after(merge_body, 0),
        "merge_1",
        shape((size, total)),
        [own, mine, arrived],
        flops=LATER,
    )
    step = 2
    while step < bricks:
        other = lax.ppermute(mine, "brick", [(i, i ^ step) for i in range(bricks)])
        step *= 2
        mine = kernel(
            merge_body, "merge_%d" % step, shape((size, total)), [mine, other], flops=LATER
        )
    other = lax.ppermute(mine, "brick", pairs)
    side = kernel(
        gather_body, "gather", shape((half, total)), [mine, other], scalars=[brick], flops=LATER
    )
    other = lax.ppermute(side, "rep", swap)
    grad_weight = kernel(
        functools.partial(join_body, half),
        "join",
        shape((TAPS * share, total), F32),
        [side, other],
        scalars=[rep, chan * share],
        scratch=[pltpu.VMEM((reps * half, total), BF16)],
        flops=LATER,
    )
    grad_features = kernel(add_body, "add", shape((share, sites)), [cotangent, own, *terms])
    grad_weight = jnp.transpose(grad_weight.reshape(TAPS, share, total), (0, 2, 1))
    return output, grad_features, grad_weight


def solution(mesh):
    return jax.shard_map(
        local,
        mesh=mesh,
        in_specs=(
            P("chan", ("scene", "brick", "rep")),
            P(None, None, "chan"),
            P(None, ("scene", "brick", "rep")),
            P("chan", ("scene", "brick", "rep")),
        ),
        out_specs=(
            P("chan", ("scene", "brick", "rep")),
            P("chan", ("scene", "brick", "rep")),
            P("scene", None, "chan"),
        ),
        check_vma=False,
    )
```

```python
import functools

import jax
import jax.numpy as jnp
from jax import lax
from jax.experimental import pallas as pl
from jax.experimental.pallas import tpu as pltpu
from jax.sharding import PartitionSpec as P

EDGE = 16
FACE = EDGE * EDGE
TAPS = 27
HALO = 384
FAR = 2 * HALO
NEAR = 640
LEAD = 896
NINE = 9
ROWS = 16
GROUP = 4
WIDTH = 768
LATER = 25 * 10**7
LINE = ("brick", "chan", "rep")
MIB = 1024 * 1024
F32, BF16 = jnp.float32, jnp.bfloat16

STEPS = [(k // 3 - 1) * EDGE + k % 3 - 1 for k in range(9)]

HERE = pl.BlockSpec(memory_space=pltpu.VMEM)
FAR_OFF = pl.BlockSpec(memory_space=pltpu.HBM)
SCALAR = pl.BlockSpec(memory_space=pltpu.SMEM)


def kernel(body, name, outs, args, scalars=(), scratch=(), aliases={}, limit=8, flops=0, space=HERE):
    single = not isinstance(outs, (tuple, list))
    return pl.pallas_call(
        body,
        out_shape=outs,
        in_specs=[SCALAR] * len(scalars) + [space] * len(args),
        out_specs=HERE if single else [HERE] * len(outs),
        scratch_shapes=list(scratch),
        input_output_aliases={len(scalars) + i: o for i, o in aliases.items()},
        compiler_params=pltpu.CompilerParams(vmem_limit_bytes=limit * MIB),
        cost_estimate=pl.CostEstimate(flops=flops, bytes_accessed=MIB, transcendentals=0),
        name=name,
    )(*scalars, *args)


def after(body, at):
    def ordered(*refs):
        body(*refs[:at], *refs[at + 1 :])

    return ordered


def shape(dims, kind=BF16):
    return jax.ShapeDtypeStruct(dims, kind)


def shift(shifts, low, high):
    for at in range(0, shifts.shape[1], ROWS):
        rows = pl.ds(at, ROWS)
        for j, step in enumerate(STEPS):
            if j != 4:
                shifts[j, rows, low:high] = shifts[4, rows, low + step : high + step]


def masked(shifts, valid, tap, at_shift, at_valid, width):
    keep = valid[tap, :, pl.ds(at_valid, width)]
    begin = pl.multiple_of(at_shift + (tap // 9 - 1) * FACE, 128)
    return [
        shifts[tap % 9, at : at + ROWS, pl.ds(begin, width)] * keep
        for at in range(0, shifts.shape[1], ROWS)
    ]


def groups(count=GROUP):
    return [range(first, min(first + count, TAPS)) for first in range(0, TAPS, count)]


def product(weights, shifts, valid, at_shift, at_valid, width, taps_of):
    channels = shifts.shape[1]
    total = None
    for group in groups():
        rows = []
        for tap in group:
            rows += masked(shifts, valid, taps_of(tap), at_shift, at_valid, width)
        part = jnp.dot(
            weights[:, group[0] * channels : (group[-1] + 1) * channels],
            jnp.concatenate(rows, axis=0),
            preferred_element_type=F32,
        )
        total = part if total is None else total + part
    return total


def pack_body(brick, chan, rep, features, cotangent, neighbours, to_core, to_line, near, done):
    share, sites = features.shape
    copies = []
    for i, (out, last) in enumerate(((to_core, 1 - rep[0]), (to_line, rep[0]))):
        far = pl.ds(pl.multiple_of(last * (sites - FAR), 128), FAR)
        close = pl.ds(pl.multiple_of(last * (sites - HALO), 128), HALO)
        copies += [
            pltpu.make_async_copy(source, target, done.at[3 * i + j])
            for j, (source, target) in enumerate(
                [
                    (neighbours.at[:, close], near.at[i]),
                    (features.at[:, far], out.at[pl.ds(0, share), :]),
                    (cotangent.at[:, close], out.at[pl.ds(share, share), pl.ds(0, HALO)]),
                ]
            )
        ]
    for copy in copies:
        copy.start()
    for i, out in enumerate((to_core, to_line)):
        copies[3 * i].wait()
        kept = (near[i] >= 0).astype(F32)
        kept = jnp.concatenate([kept, jnp.zeros((32 - TAPS, HALO), F32)], axis=0)
        out[share : share + 32, HALO:] = kept.astype(BF16)
        copies[3 * i + 1].wait()
        copies[3 * i + 2].wait()


def ends_body(brick, chan, rep, core, line, before, behind, both):
    share = both.shape[0]

    def fill(first, second):
        before[...] = first[...]
        behind[...] = second[...]
        both[:, :NEAR] = first[:share, FAR - NEAR :]
        both[:, NEAR:] = second[:share, :NEAR]

    pl.when(rep[0] == 0)(functools.partial(fill, line, core))
    pl.when(rep[0] != 0)(functools.partial(fill, core, line))


def prepare_body(
    brick, chan, rep, by_out, features, neighbours, own, rest, by_in, shifts, valid, flat, kept, taken, near, done
):
    total = by_out.shape[2]
    share, sites = features.shape
    turn = lax.rem(total - chan[0] * share, total)
    copies = [
        pltpu.make_async_copy(source, target, done.at[i])
        for i, (source, target) in enumerate(
            [
                (by_out, taken),
                (features, shifts.at[4, :, pl.ds(FAR, sites)]),
                (neighbours, near),
            ]
        )
    ]
    for copy in copies:
        copy.start()
    copies[0].wait()
    flat[...] = jnp.zeros_like(flat)
    for group in groups():
        taps = []
        for tap in group:
            ring = pltpu.roll(taken[tap].astype(F32), turn, 1)
            flat[tap * share : (tap + 1) * share, :] = ring
            taps.append(ring)
        first, last = group[0], group[-1] + 1
        own[:, first * share : last * share] = jnp.concatenate(
            [x[:, :share] for x in taps], axis=1
        ).astype(BF16)
        left = total - share
        rest[:, first * left : last * left] = jnp.concatenate(
            [x[:, share:] for x in taps], axis=1
        ).astype(BF16)
    by_in[...] = flat[...].T.astype(BF16)
    copies[1].wait()
    shift(shifts, FAR + 128, FAR + sites - 128)
    copies[2].wait()
    kept[...] = (near[...] >= 0).astype(F32)
    for tap in range(TAPS):
        valid[tap, :, HALO : HALO + sites] = jnp.broadcast_to(
            kept[tap : tap + 1, :], (ROWS, sites)
        ).astype(BF16)


def own_body(left, right, weights, shifts_in, valid_in, begun, shifts, valid, kept):
    del shifts_in, valid_in
    share = begun.shape[0]
    far = shifts.shape[2] - FAR
    for side, at, start in ((left, 0, 128), (right, 1, far - 128)):
        shifts[4, :, at * far : at * far + FAR] = side[:share, :]
        shift(shifts, start, start + FAR)
        kept[...] = side[share : share + 32, HALO:].astype(F32)
        begin = at * (valid.shape[2] - HALO)
        for tap in range(TAPS):
            valid[tap, :, begin : begin + HALO] = jnp.broadcast_to(
                kept[tap : tap + 1, :], (ROWS, HALO)
            ).astype(BF16)

    def block(j, carry):
        start = pl.multiple_of(j * WIDTH, 128)
        begun[:, pl.ds(start, WIDTH)] = product(
            weights, shifts, valid, start + HALO, start, WIDTH, lambda tap: tap
        )
        return carry

    lax.fori_loop(0, begun.shape[1] // WIDTH, block, 0)


def arrive_body(rest, own_in, shifts, across, own):
    del own_in
    sites = rest.shape[1]
    shifts[4, :, FAR : FAR + sites] = rest[...]
    shift(shifts, FAR + 128, FAR + sites - 128)

    def block(j, carry):
        start = pl.multiple_of(j * WIDTH, 128)
        here = pl.ds(pl.multiple_of(start + FAR, 128), WIDTH)
        across[pl.ds(start, WIDTH), :] = jnp.concatenate(
            [own[4, :, here], shifts[4, :, here]], axis=0
        ).T
        return carry

    lax.fori_loop(0, sites // WIDTH, block, 0)


def rest_body(
    ends,
    shifts_in,
    weights,
    valid_in,
    begun,
    left,
    right,
    own,
    cotangent,
    output,
    grads,
    valid,
    shifts,
    grad,
    kept,
):
    del shifts_in, valid_in
    share, sites = cotangent.shape
    far = shifts.shape[2] - FAR
    shifts[4, :, : FAR - NEAR] = jnp.zeros((shifts.shape[1], FAR - NEAR), BF16)
    shifts[4, :, FAR - NEAR : FAR] = ends[:, :NEAR]
    shifts[4, :, far : far + NEAR] = ends[:, NEAR:]
    shifts[4, :, far + NEAR :] = jnp.zeros((shifts.shape[1], FAR - NEAR), BF16)
    shift(shifts, 128, 128 + FAR)
    shift(shifts, far - 128, far + FAR - 128)
    lead = LEAD + 128
    grad[:, lead : lead + HALO] = left[share : 2 * share, :HALO]
    grad[:, lead + HALO : lead + HALO + sites] = cotangent[...]
    grad[:, lead + HALO + sites :] = right[share : 2 * share, :HALO]

    def spread(start):
        for at in range(0, share, ROWS):
            rows = pl.ds(at, ROWS)
            window = grad[rows, pl.ds(start, WIDTH + 256)]
            for j, step in enumerate(STEPS):
                grads[j, rows, pl.ds(start, WIDTH)] = window[:, 128 + step : 128 + step + WIDTH]

    def block(j, carry):
        start = pl.multiple_of(j * WIDTH, 128)
        spread(start)
        here = pl.ds(start, WIDTH)
        there = pl.ds(pl.multiple_of(start + lead, 128), WIDTH)
        hidden = begun[:, here] + product(
            weights, shifts, valid, start + HALO, start, WIDTH, lambda tap: tap
        )
        sigma = jax.nn.sigmoid(hidden)
        features = own[4, :, pl.ds(pl.multiple_of(start + HALO, 128), WIDTH)]
        kept[:, here] = (features.astype(F32) + hidden * sigma).astype(BF16)
        grad[:, there] = (
            grad[:, there].astype(F32) * sigma * (1.0 + hidden * (1.0 - sigma))
        ).astype(BF16)
        return carry

    count = begun.shape[1] // WIDTH
    lax.fori_loop(0, count, block, 0)
    spread(count * WIDTH)
    output[...] = kept[:, HALO : HALO + sites]


def weight_body(half, brick, chan, rep, across, valid_in, grads_in, kept, sent, valid, grads, total):
    del valid_in, grads_in
    share, sites = grads.shape[1], across.shape[0]
    total[...] = jnp.zeros_like(total)

    def block(j, carry):
        start = pl.multiple_of(j * WIDTH, 128)
        features = across[pl.ds(start, WIDTH), :]
        for group in groups(NINE):
            rows = []
            for tap in group:
                rows += masked(
                    grads, valid, TAPS - 1 - tap, start + HALO + LEAD, start + HALO, WIDTH
                )
            total[group[0] * share : (group[-1] + 1) * share, :] += jnp.dot(
                jnp.concatenate(rows, axis=0), features, preferred_element_type=F32
            )
        return carry

    lax.fori_loop(0, sites // WIDTH, block, 0)
    mine = rep[0]
    kept[...] = total[pl.ds(pl.multiple_of(mine * half, ROWS), half), :]
    sent[...] = total[pl.ds(pl.multiple_of((1 - mine) * half, ROWS), half), :].astype(BF16)


def feature_body(part, weights, valid, grads, *refs):
    own, rest = refs[-2:]
    share, sites = own.shape
    begin = part * sites // 2

    def block(j, carry):
        start = pl.multiple_of(begin + j * WIDTH, 128)
        here = pl.ds(start, WIDTH)
        total = product(
            weights,
            grads,
            valid,
            start + HALO + LEAD,
            start + HALO,
            WIDTH,
            lambda tap: TAPS - 1 - tap,
        )
        own[:, here] = total[:share]
        rest[:, here] = total[share:].astype(BF16)
        return carry

    lax.fori_loop(0, sites // 2 // WIDTH, block, 0)


def split_body(brick, chan, rep, kept, arrived, mine, sent):
    size = mine.shape[0]
    at = brick[0] % 2
    mine_rows = pl.ds(pl.multiple_of(at * size, ROWS), size)
    sent_rows = pl.ds(pl.multiple_of((1 - at) * size, ROWS), size)
    mine[...] = kept[mine_rows, :] + arrived[mine_rows, :].astype(F32)
    sent[...] = (kept[sent_rows, :] + arrived[sent_rows, :].astype(F32)).astype(BF16)


def merge_body(mine, other, out):
    out[...] = (mine[...].astype(F32) + other[...].astype(F32)).astype(BF16)


def gather_body(brick, chan, rep, mine, other, side):
    size = mine.shape[0]
    at = brick[0] % 2
    side[pl.ds(pl.multiple_of(at * size, ROWS), size), :] = mine[...]
    side[pl.ds(pl.multiple_of((1 - at) * size, ROWS), size), :] = other[...]


def join_body(half, share, brick, chan, rep, side, other, out, both):
    mine = rep[0]
    both[pl.ds(pl.multiple_of(mine * half, ROWS), half), :] = side[...]
    both[pl.ds(pl.multiple_of((1 - mine) * half, ROWS), half), :] = other[...]
    out[...] = pltpu.roll(both[: out.shape[0], :].astype(F32), chan[0] * share, 1)


def add_body(cotangent, own, *rest):
    *terms, out = rest
    total = cotangent[...].astype(F32) + own[...]
    for term in terms:
        total += term[...].astype(F32)
    out[...] = total.astype(BF16)


def line_swap(x):
    count = lax.axis_size(("brick", "rep"))
    pairs = [p for i in range(1, count - 1, 2) for p in ((i, i + 1), (i + 1, i))]
    return lax.ppermute(x, ("brick", "rep"), pairs)


def local(features, conv_weight, neighbours, cotangent):
    share, sites = features.shape
    total = conv_weight.shape[1]
    left = total - share
    chans, bricks, reps = (lax.axis_size(axis) for axis in ("chan", "brick", "rep"))
    place = [lax.axis_index(axis)[None] for axis in LINE]
    margin = sites + 2 * HALO
    flops = 2 * TAPS * share * sites

    def around(x):
        return [
            lax.ppermute(x, "chan", [((i + over) % chans, i) for i in range(chans)])
            for over in range(1, chans)
        ]

    def stack(parts):
        return parts[0] if len(parts) == 1 else jnp.concatenate(parts, axis=0)

    assert reps == 2
    swap = [(0, 1), (1, 0)]
    rest = stack(around(features))
    to_core, to_line = kernel(
        pack_body,
        "pack",
        [shape((share + max(share, 32), FAR))] * 2,
        [features, cotangent, neighbours],
        scalars=place,
        scratch=[pltpu.VMEM((2, TAPS, HALO), jnp.int32), pltpu.SemaphoreType.DMA((6,))],
        limit=58,
        space=FAR_OFF,
    )
    line = line_swap(to_line)
    core = lax.ppermute(to_core, "rep", swap)
    lanes = -(-TAPS * share // 128) * 128
    own_weights, rest_weights, by_in, shifts, valid = kernel(
        prepare_body,
        "prepare",
        [
            shape((share, TAPS * share)),
            shape((share, TAPS * left)),
            shape((total, lanes)),
            shape((9, share, sites + 2 * FAR)),
            shape((TAPS, ROWS, margin)),
        ],
        [jnp.transpose(conv_weight, (0, 2, 1)), features, neighbours],
        scalars=place,
        scratch=[
            pltpu.VMEM((lanes, total), F32),
            pltpu.VMEM((TAPS, sites), F32),
            pltpu.VMEM((TAPS, share, total), BF16),
            pltpu.VMEM((TAPS, sites), jnp.int32),
            pltpu.SemaphoreType.DMA((3,)),
        ],
        space=FAR_OFF,
    )
    before, behind, both = kernel(
        after(ends_body, 3),
        "ends",
        [shape(core.shape), shape(core.shape), shape((share, 2 * NEAR))],
        [own_weights, core, line],
        scalars=place,
    )
    ends = stack(around(both))
    begun, own_shifts, valid = kernel(
        own_body,
        "forward_own",
        [shape((share, margin), F32), shape(shifts.shape), shape(valid.shape)],
        [before, behind, own_weights, shifts, valid],
        scratch=[pltpu.VMEM((32, HALO), F32)],
        aliases={3: 1, 4: 2},
    )
    rest_shifts, across, own_shifts = kernel(
        arrive_body,
        "arrive",
        [shape((9, left, sites + 2 * FAR)), shape((sites, total)), shape(own_shifts.shape)],
        [rest, own_shifts],
        aliases={1: 2},
    )
    output, grads, valid, _ = kernel(
        rest_body,
        "forward_rest",
        [
            shape((share, sites)),
            shape((9, share, margin + WIDTH)),
            shape(valid.shape),
            shape(rest_shifts.shape),
        ],
        [ends, rest_shifts, rest_weights, valid, begun, before, behind, own_shifts, cotangent],
        scratch=[
            pltpu.VMEM((share, LEAD + 128 + margin), BF16),
            pltpu.VMEM((share, margin), BF16),
        ],
        aliases={1: 3, 3: 2},
        flops=flops * left,
    )

    piece = -(-TAPS * share // (reps * bricks * ROWS)) * ROWS
    half = piece * bricks
    kept, sent, valid, grads = kernel(
        functools.partial(weight_body, half),
        "grad_weight",
        [shape((half, total), F32), shape((half, total)), shape(valid.shape), shape(grads.shape)],
        [across, valid, grads],
        scalars=place,
        scratch=[pltpu.VMEM((reps * half, total), F32)],
        aliases={1: 2, 2: 3},
        flops=flops * total,
    )
    arrived = lax.ppermute(sent, "rep", swap)

    def feature_part(part, body, args, kept):
        outs = [shape((share, sites), F32), shape((left, sites))]
        return kernel(
            body,
            "grad_features_%d" % part,
            [shape(x.shape) for x in kept] + outs,
            args,
            aliases={len(args) - len(kept) + i: i for i in range(len(kept))}
            if part == 0
            else {len(args) - 2 + i: i for i in range(2)},
            flops=flops * total // 2,
        )

    valid, grads, *parts = feature_part(
        0, functools.partial(feature_body, 0), [by_in, valid, grads], [valid, grads]
    )
    size = half // 2
    mine, sent = kernel(
        after(split_body, 3),
        "split",
        [shape((size, total), F32), shape((size, total))],
        [parts[0], kept, arrived],
        scalars=place,
        flops=LATER,
    )
    pairs = [(i, i ^ 1) for i in range(bricks)]
    arrived = lax.ppermute(sent, "brick", pairs)
    own, other = feature_part(
        1, after(functools.partial(feature_body, 1), 0), [mine, by_in, valid, grads, *parts], []
    )
    terms = [
        lax.ppermute(
            other if left == share else other[(over - 1) * share : over * share],
            "chan",
            [(i, (i + over) % chans) for i in range(chans)],
        )
        for over in range(1, chans)
    ]
    mine = kernel(
        after(merge_body, 0),
        "merge_1",
        shape((size, total)),
        [own, mine, arrived],
        flops=LATER,
    )
    step = 2
    while step < bricks:
        other = lax.ppermute(mine, "brick", [(i, i ^ step) for i in range(bricks)])
        step *= 2
        mine = kernel(
            merge_body, "merge_%d" % step, shape((size, total)), [mine, other], flops=LATER
        )
    other = lax.ppermute(mine, "brick", pairs)
    side = kernel(
        gather_body, "gather", shape((half, total)), [mine, other], scalars=place, flops=LATER
    )
    other = lax.ppermute(side, "rep", swap)
    grad_weight = kernel(
        functools.partial(join_body, half, share),
        "join",
        shape((TAPS * share, total), F32),
        [side, other],
        scalars=place,
        scratch=[pltpu.VMEM((reps * half, total), BF16)],
        flops=LATER,
    )
    grad_features = kernel(add_body, "add", shape((share, sites)), [cotangent, own, *terms])
    grad_weight = jnp.transpose(grad_weight.reshape(TAPS, share, total), (0, 2, 1))
    return output, grad_features, grad_weight


def solution(mesh):
    return jax.shard_map(
        local,
        mesh=mesh,
        in_specs=(
            P("chan", ("scene", "brick", "rep")),
            P(None, None, "chan"),
            P(None, ("scene", "brick", "rep")),
            P("chan", ("scene", "brick", "rep")),
        ),
        out_specs=(
            P("chan", ("scene", "brick", "rep")),
            P("chan", ("scene", "brick", "rep")),
            P("scene", None, "chan"),
        ),
        check_vma=False,
    )
```

```python
import functools

import jax
import jax.numpy as jnp
from jax import lax
from jax.experimental import pallas as pl
from jax.experimental.pallas import tpu as pltpu
from jax.sharding import PartitionSpec as P

EDGE = 16
FACE = EDGE * EDGE
TAPS = 27
HALO = 384
FAR = 2 * HALO
NEAR = 640
LEAD = 896
NINE = 9
ROWS = 16
GROUP = 4
WIDTH = 768
LATER = 25 * 10**7
LINE = ("brick", "chan", "rep")
MIB = 1024 * 1024
F32, BF16 = jnp.float32, jnp.bfloat16

STEPS = [(k // 3 - 1) * EDGE + k % 3 - 1 for k in range(9)]

HERE = pl.BlockSpec(memory_space=pltpu.VMEM)
FAR_OFF = pl.BlockSpec(memory_space=pltpu.HBM)
SCALAR = pl.BlockSpec(memory_space=pltpu.SMEM)


def kernel(body, name, outs, args, scalars=(), scratch=(), aliases={}, limit=8, flops=0, space=HERE):
    single = not isinstance(outs, (tuple, list))
    return pl.pallas_call(
        body,
        out_shape=outs,
        in_specs=[SCALAR] * len(scalars) + [space] * len(args),
        out_specs=HERE if single else [HERE] * len(outs),
        scratch_shapes=list(scratch),
        input_output_aliases={len(scalars) + i: o for i, o in aliases.items()},
        compiler_params=pltpu.CompilerParams(vmem_limit_bytes=limit * MIB),
        cost_estimate=pl.CostEstimate(flops=flops, bytes_accessed=MIB, transcendentals=0),
        name=name,
    )(*scalars, *args)


def after(body, at):
    def ordered(*refs):
        body(*refs[:at], *refs[at + 1 :])

    return ordered


def shape(dims, kind=BF16):
    return jax.ShapeDtypeStruct(dims, kind)


def shift(shifts, low, high):
    for at in range(0, shifts.shape[1], ROWS):
        rows = pl.ds(at, ROWS)
        for j, step in enumerate(STEPS):
            if j != 4:
                shifts[j, rows, low:high] = shifts[4, rows, low + step : high + step]


def masked(shifts, valid, tap, at_shift, at_valid, width):
    keep = valid[tap, :, pl.ds(at_valid, width)]
    begin = pl.multiple_of(at_shift + (tap // 9 - 1) * FACE, 128)
    return [
        shifts[tap % 9, at : at + ROWS, pl.ds(begin, width)] * keep
        for at in range(0, shifts.shape[1], ROWS)
    ]


def groups(count=GROUP):
    return [range(first, min(first + count, TAPS)) for first in range(0, TAPS, count)]


def product(weights, shifts, valid, at_shift, at_valid, width, taps_of):
    channels = shifts.shape[1]
    total = None
    for group in groups():
        rows = []
        for tap in group:
            rows += masked(shifts, valid, taps_of(tap), at_shift, at_valid, width)
        part = jnp.dot(
            weights[:, group[0] * channels : (group[-1] + 1) * channels],
            jnp.concatenate(rows, axis=0),
            preferred_element_type=F32,
        )
        total = part if total is None else total + part
    return total


def pack_body(brick, chan, rep, features, cotangent, neighbours, to_core, to_line, near, done):
    share, sites = features.shape
    copies = []
    for i, (out, last) in enumerate(((to_core, 1 - rep[0]), (to_line, rep[0]))):
        far = pl.ds(pl.multiple_of(last * (sites - FAR), 128), FAR)
        close = pl.ds(pl.multiple_of(last * (sites - HALO), 128), HALO)
        copies += [
            pltpu.make_async_copy(source, target, done.at[3 * i + j])
            for j, (source, target) in enumerate(
                [
                    (neighbours.at[:, close], near.at[i]),
                    (features.at[:, far], out.at[pl.ds(0, share), :]),
                    (cotangent.at[:, close], out.at[pl.ds(share, share), pl.ds(0, HALO)]),
                ]
            )
        ]
    for copy in copies:
        copy.start()
    for i, out in enumerate((to_core, to_line)):
        copies[3 * i].wait()
        kept = (near[i] >= 0).astype(F32)
        kept = jnp.concatenate([kept, jnp.zeros((32 - TAPS, HALO), F32)], axis=0)
        out[share : share + 32, HALO:] = kept.astype(BF16)
        copies[3 * i + 1].wait()
        copies[3 * i + 2].wait()


def ends_body(brick, chan, rep, core, line, before, behind, both):
    share = both.shape[0]

    def fill(first, second):
        before[...] = first[...]
        behind[...] = second[...]
        both[:, :NEAR] = first[:share, FAR - NEAR :]
        both[:, NEAR:] = second[:share, :NEAR]

    pl.when(rep[0] == 0)(functools.partial(fill, line, core))
    pl.when(rep[0] != 0)(functools.partial(fill, core, line))


def prepare_body(
    brick, chan, rep, by_out, features, neighbours, own, rest, by_in, shifts, valid, flat, kept, taken, near, done
):
    total = by_out.shape[2]
    share, sites = features.shape
    turn = lax.rem(total - chan[0] * share, total)
    copies = [
        pltpu.make_async_copy(source, target, done.at[i])
        for i, (source, target) in enumerate(
            [
                (by_out, taken),
                (features, shifts.at[4, :, pl.ds(FAR, sites)]),
                (neighbours, near),
            ]
        )
    ]
    for copy in copies:
        copy.start()
    copies[0].wait()
    flat[...] = jnp.zeros_like(flat)
    for group in groups():
        taps = []
        for tap in group:
            ring = pltpu.roll(taken[tap].astype(F32), turn, 1)
            flat[tap * share : (tap + 1) * share, :] = ring
            taps.append(ring)
        first, last = group[0], group[-1] + 1
        own[:, first * share : last * share] = jnp.concatenate(
            [x[:, :share] for x in taps], axis=1
        ).astype(BF16)
        left = total - share
        rest[:, first * left : last * left] = jnp.concatenate(
            [x[:, share:] for x in taps], axis=1
        ).astype(BF16)
    by_in[...] = flat[...].T.astype(BF16)
    copies[1].wait()
    shift(shifts, FAR + 128, FAR + sites - 128)
    copies[2].wait()
    kept[...] = (near[...] >= 0).astype(F32)
    for tap in range(TAPS):
        valid[tap, :, HALO : HALO + sites] = jnp.broadcast_to(
            kept[tap : tap + 1, :], (ROWS, sites)
        ).astype(BF16)


def own_body(left, right, weights, shifts_in, valid_in, begun, shifts, valid, kept):
    del shifts_in, valid_in
    share = begun.shape[0]
    far = shifts.shape[2] - FAR
    for side, at, start in ((left, 0, 128), (right, 1, far - 128)):
        shifts[4, :, at * far : at * far + FAR] = side[:share, :]
        shift(shifts, start, start + FAR)
        kept[...] = side[share : share + 32, HALO:].astype(F32)
        begin = at * (valid.shape[2] - HALO)
        for tap in range(TAPS):
            valid[tap, :, begin : begin + HALO] = jnp.broadcast_to(
                kept[tap : tap + 1, :], (ROWS, HALO)
            ).astype(BF16)

    def block(j, carry):
        start = pl.multiple_of(j * WIDTH, 128)
        begun[:, pl.ds(start, WIDTH)] = product(
            weights, shifts, valid, start + HALO, start, WIDTH, lambda tap: tap
        )
        return carry

    lax.fori_loop(0, begun.shape[1] // WIDTH, block, 0)


def arrive_body(rest, own_in, shifts, across, own):
    del own_in
    sites = rest.shape[1]
    shifts[4, :, FAR : FAR + sites] = rest[...]
    shift(shifts, FAR + 128, FAR + sites - 128)

    def block(j, carry):
        start = pl.multiple_of(j * WIDTH, 128)
        here = pl.ds(pl.multiple_of(start + FAR, 128), WIDTH)
        across[pl.ds(start, WIDTH), :] = jnp.concatenate(
            [own[4, :, here], shifts[4, :, here]], axis=0
        ).T
        return carry

    lax.fori_loop(0, sites // WIDTH, block, 0)


def rest_body(
    ends,
    shifts_in,
    weights,
    valid_in,
    begun,
    left,
    right,
    own,
    cotangent,
    output,
    grads,
    valid,
    shifts,
    grad,
    kept,
):
    del shifts_in, valid_in
    share, sites = cotangent.shape
    far = shifts.shape[2] - FAR
    shifts[4, :, : FAR - NEAR] = jnp.zeros((shifts.shape[1], FAR - NEAR), BF16)
    shifts[4, :, FAR - NEAR : FAR] = ends[:, :NEAR]
    shifts[4, :, far : far + NEAR] = ends[:, NEAR:]
    shifts[4, :, far + NEAR :] = jnp.zeros((shifts.shape[1], FAR - NEAR), BF16)
    shift(shifts, 128, 128 + FAR)
    shift(shifts, far - 128, far + FAR - 128)
    lead = LEAD + 128
    grad[:, lead : lead + HALO] = left[share : 2 * share, :HALO]
    grad[:, lead + HALO : lead + HALO + sites] = cotangent[...]
    grad[:, lead + HALO + sites :] = right[share : 2 * share, :HALO]

    def spread(start):
        for at in range(0, share, ROWS):
            rows = pl.ds(at, ROWS)
            window = grad[rows, pl.ds(start, WIDTH + 256)]
            for j, step in enumerate(STEPS):
                grads[j, rows, pl.ds(start, WIDTH)] = window[:, 128 + step : 128 + step + WIDTH]

    def block(j, carry):
        start = pl.multiple_of(j * WIDTH, 128)
        spread(start)
        here = pl.ds(start, WIDTH)
        there = pl.ds(pl.multiple_of(start + lead, 128), WIDTH)
        hidden = begun[:, here] + product(
            weights, shifts, valid, start + HALO, start, WIDTH, lambda tap: tap
        )
        sigma = jax.nn.sigmoid(hidden)
        features = own[4, :, pl.ds(pl.multiple_of(start + HALO, 128), WIDTH)]
        kept[:, here] = (features.astype(F32) + hidden * sigma).astype(BF16)
        grad[:, there] = (
            grad[:, there].astype(F32) * sigma * (1.0 + hidden * (1.0 - sigma))
        ).astype(BF16)
        return carry

    count = begun.shape[1] // WIDTH
    lax.fori_loop(0, count, block, 0)
    spread(count * WIDTH)
    output[...] = kept[:, HALO : HALO + sites]


def weight_body(half, brick, chan, rep, across, valid_in, grads_in, kept, sent, valid, grads, total):
    del valid_in, grads_in
    share, sites = grads.shape[1], across.shape[0]
    total[...] = jnp.zeros_like(total)

    def block(j, carry):
        start = pl.multiple_of(j * WIDTH, 128)
        features = across[pl.ds(start, WIDTH), :]
        for group in groups(NINE):
            rows = []
            for tap in group:
                rows += masked(
                    grads, valid, TAPS - 1 - tap, start + HALO + LEAD, start + HALO, WIDTH
                )
            total[group[0] * share : (group[-1] + 1) * share, :] += jnp.dot(
                jnp.concatenate(rows, axis=0), features, preferred_element_type=F32
            )
        return carry

    lax.fori_loop(0, sites // WIDTH, block, 0)
    mine = rep[0]
    kept[...] = total[pl.ds(pl.multiple_of(mine * half, ROWS), half), :]
    sent[...] = total[pl.ds(pl.multiple_of((1 - mine) * half, ROWS), half), :].astype(BF16)


def feature_body(weights, valid, grads, own, rest):
    def block(j, carry):
        start = pl.multiple_of(j * WIDTH, 128)
        here = pl.ds(start, WIDTH)
        total = product(
            weights,
            grads,
            valid,
            start + HALO + LEAD,
            start + HALO,
            WIDTH,
            lambda tap: TAPS - 1 - tap,
        )
        own[:, here] = total[: own.shape[0]]
        rest[:, here] = total[own.shape[0] :].astype(BF16)
        return carry

    lax.fori_loop(0, own.shape[1] // WIDTH, block, 0)


def split_body(brick, chan, rep, kept, arrived, mine, sent):
    size = mine.shape[0]
    rows = pl.ds(pl.multiple_of(brick[0] * size, ROWS), size)
    mine[...] = kept[rows, :] + arrived[rows, :].astype(F32)
    sent[...] = (kept[...] + arrived[...].astype(F32)).astype(BF16)


def merge_body(brick, chan, rep, mine, others, out):
    size = mine.shape[0]
    count = others.shape[0] // size
    total = mine[...]
    for at in range(count):
        part = others[at * size : (at + 1) * size, :].astype(F32)
        total += jnp.where(brick[0] == at, 0.0, part)
    for at in range(count):
        out[at * size : (at + 1) * size, :] = total.astype(BF16)


def join_body(half, share, brick, chan, rep, side, other, out, both):
    mine = rep[0]
    both[pl.ds(pl.multiple_of(mine * half, ROWS), half), :] = side[...]
    both[pl.ds(pl.multiple_of((1 - mine) * half, ROWS), half), :] = other[...]
    out[...] = pltpu.roll(both[: out.shape[0], :].astype(F32), chan[0] * share, 1)


def add_body(cotangent, own, *rest):
    *terms, out = rest
    total = cotangent[...].astype(F32) + own[...]
    for term in terms:
        total += term[...].astype(F32)
    out[...] = total.astype(BF16)


def line_swap(x):
    count = lax.axis_size(("brick", "rep"))
    pairs = [p for i in range(1, count - 1, 2) for p in ((i, i + 1), (i + 1, i))]
    return lax.ppermute(x, ("brick", "rep"), pairs)


def local(features, conv_weight, neighbours, cotangent):
    share, sites = features.shape
    total = conv_weight.shape[1]
    left = total - share
    chans, bricks, reps = (lax.axis_size(axis) for axis in ("chan", "brick", "rep"))
    place = [lax.axis_index(axis)[None] for axis in LINE]
    margin = sites + 2 * HALO
    flops = 2 * TAPS * share * sites

    def around(x):
        return [
            lax.ppermute(x, "chan", [((i + over) % chans, i) for i in range(chans)])
            for over in range(1, chans)
        ]

    def stack(parts):
        return parts[0] if len(parts) == 1 else jnp.concatenate(parts, axis=0)

    assert reps == 2
    swap = [(0, 1), (1, 0)]
    rest = stack(around(features))
    to_core, to_line = kernel(
        pack_body,
        "pack",
        [shape((share + max(share, 32), FAR))] * 2,
        [features, cotangent, neighbours],
        scalars=place,
        scratch=[pltpu.VMEM((2, TAPS, HALO), jnp.int32), pltpu.SemaphoreType.DMA((6,))],
        limit=58,
        space=FAR_OFF,
    )
    line = line_swap(to_line)
    core = lax.ppermute(to_core, "rep", swap)
    lanes = -(-TAPS * share // 128) * 128
    own_weights, rest_weights, by_in, shifts, valid = kernel(
        prepare_body,
        "prepare",
        [
            shape((share, TAPS * share)),
            shape((share, TAPS * left)),
            shape((total, lanes)),
            shape((9, share, sites + 2 * FAR)),
            shape((TAPS, ROWS, margin)),
        ],
        [jnp.transpose(conv_weight, (0, 2, 1)), features, neighbours],
        scalars=place,
        scratch=[
            pltpu.VMEM((lanes, total), F32),
            pltpu.VMEM((TAPS, sites), F32),
            pltpu.VMEM((TAPS, share, total), BF16),
            pltpu.VMEM((TAPS, sites), jnp.int32),
            pltpu.SemaphoreType.DMA((3,)),
        ],
        space=FAR_OFF,
    )
    before, behind, both = kernel(
        after(ends_body, 3),
        "ends",
        [shape(core.shape), shape(core.shape), shape((share, 2 * NEAR))],
        [own_weights, core, line],
        scalars=place,
    )
    ends = stack(around(both))
    begun, own_shifts, valid = kernel(
        own_body,
        "forward_own",
        [shape((share, margin), F32), shape(shifts.shape), shape(valid.shape)],
        [before, behind, own_weights, shifts, valid],
        scratch=[pltpu.VMEM((32, HALO), F32)],
        aliases={3: 1, 4: 2},
    )
    rest_shifts, across, own_shifts = kernel(
        arrive_body,
        "arrive",
        [shape((9, left, sites + 2 * FAR)), shape((sites, total)), shape(own_shifts.shape)],
        [rest, own_shifts],
        aliases={1: 2},
    )
    output, grads, valid, _ = kernel(
        rest_body,
        "forward_rest",
        [
            shape((share, sites)),
            shape((9, share, margin + WIDTH)),
            shape(valid.shape),
            shape(rest_shifts.shape),
        ],
        [ends, rest_shifts, rest_weights, valid, begun, before, behind, own_shifts, cotangent],
        scratch=[
            pltpu.VMEM((share, LEAD + 128 + margin), BF16),
            pltpu.VMEM((share, margin), BF16),
        ],
        aliases={1: 3, 3: 2},
        flops=flops * left,
    )

    piece = -(-TAPS * share // (reps * bricks * ROWS)) * ROWS
    half = piece * bricks
    kept, sent, valid, grads = kernel(
        functools.partial(weight_body, half),
        "grad_weight",
        [shape((half, total), F32), shape((half, total)), shape(valid.shape), shape(grads.shape)],
        [across, valid, grads],
        scalars=place,
        scratch=[pltpu.VMEM((reps * half, total), F32)],
        aliases={1: 2, 2: 3},
        flops=flops * total,
    )
    arrived = lax.ppermute(sent, "rep", swap)

    own, other = kernel(
        feature_body,
        "grad_features",
        [shape((share, sites), F32), shape((left, sites))],
        [by_in, valid, grads],
        flops=flops * total,
    )
    terms = [
        lax.ppermute(
            other if left == share else other[(over - 1) * share : over * share],
            "chan",
            [(i, (i + over) % chans) for i in range(chans)],
        )
        for over in range(1, chans)
    ]

    mine, sent = kernel(
        after(split_body, 3),
        "split",
        [shape((piece, total), F32), shape((half, total))],
        [own, kept, arrived],
        scalars=place,
        flops=LATER,
    )

    def across_bricks(x):
        return lax.all_to_all(x, "brick", split_axis=0, concat_axis=0, tiled=True)

    arrived = across_bricks(sent)
    done = kernel(
        merge_body,
        "merge",
        shape((half, total)),
        [mine, arrived],
        scalars=place,
        flops=LATER,
    )
    side = across_bricks(done)
    other = lax.ppermute(side, "rep", swap)
    grad_weight = kernel(
        functools.partial(join_body, half, share),
        "join",
        shape((TAPS * share, total), F32),
        [side, other],
        scalars=place,
        scratch=[pltpu.VMEM((reps * half, total), BF16)],
        flops=LATER,
    )
    grad_features = kernel(add_body, "add", shape((share, sites)), [cotangent, own, *terms])
    grad_weight = jnp.transpose(grad_weight.reshape(TAPS, share, total), (0, 2, 1))
    return output, grad_features, grad_weight


def solution(mesh):
    return jax.shard_map(
        local,
        mesh=mesh,
        in_specs=(
            P("chan", ("scene", "brick", "rep")),
            P(None, None, "chan"),
            P(None, ("scene", "brick", "rep")),
            P("chan", ("scene", "brick", "rep")),
        ),
        out_specs=(
            P("chan", ("scene", "brick", "rep")),
            P("chan", ("scene", "brick", "rep")),
            P("scene", None, "chan"),
        ),
        check_vma=False,
    )
```

```python
import functools

import jax
import jax.numpy as jnp
from jax import lax
from jax.experimental import pallas as pl
from jax.experimental.pallas import tpu as pltpu
from jax.sharding import PartitionSpec as P

EDGE = 16
FACE = EDGE * EDGE
TAPS = 27
HALO = 384
FAR = 2 * HALO
NEAR = 640
LEAD = 896
MANY = 14
ROWS = 16
GROUP = 4
WIDTH = 768
LATER = 25 * 10**7
LINE = ("brick", "chan", "rep")
MIB = 1024 * 1024
F32, BF16 = jnp.float32, jnp.bfloat16

STEPS = [(k // 3 - 1) * EDGE + k % 3 - 1 for k in range(9)]

HERE = pl.BlockSpec(memory_space=pltpu.VMEM)
FAR_OFF = pl.BlockSpec(memory_space=pltpu.HBM)
SCALAR = pl.BlockSpec(memory_space=pltpu.SMEM)


def kernel(body, name, outs, args, scalars=(), scratch=(), aliases={}, limit=8, flops=0, held=False):
    if held:
        args = [pltpu.with_memory_space_constraint(x, pltpu.HBM) for x in args]
    single = not isinstance(outs, (tuple, list))
    return pl.pallas_call(
        body,
        out_shape=outs,
        in_specs=[SCALAR] * len(scalars) + [FAR_OFF if held else HERE] * len(args),
        out_specs=HERE if single else [HERE] * len(outs),
        scratch_shapes=list(scratch),
        input_output_aliases={len(scalars) + i: o for i, o in aliases.items()},
        compiler_params=pltpu.CompilerParams(vmem_limit_bytes=limit * MIB),
        cost_estimate=pl.CostEstimate(flops=flops, bytes_accessed=MIB, transcendentals=0),
        name=name,
    )(*scalars, *args)


def after(body, at):
    def ordered(*refs):
        body(*refs[:at], *refs[at + 1 :])

    return ordered


def shape(dims, kind=BF16):
    return jax.ShapeDtypeStruct(dims, kind)


def shift(shifts, low, high):
    for at in range(0, shifts.shape[1], ROWS):
        rows = pl.ds(at, ROWS)
        for j, step in enumerate(STEPS):
            if j != 4:
                shifts[j, rows, low:high] = shifts[4, rows, low + step : high + step]


def masked(shifts, valid, tap, at_shift, at_valid, width):
    keep = valid[tap, :, pl.ds(at_valid, width)]
    begin = pl.multiple_of(at_shift + (tap // 9 - 1) * FACE, 128)
    return [
        shifts[tap % 9, at : at + ROWS, pl.ds(begin, width)] * keep
        for at in range(0, shifts.shape[1], ROWS)
    ]


def groups(count=GROUP):
    return [range(first, min(first + count, TAPS)) for first in range(0, TAPS, count)]


def product(weights, shifts, valid, at_shift, at_valid, width, taps_of):
    channels = shifts.shape[1]
    total = None
    for group in groups():
        rows = []
        for tap in group:
            rows += masked(shifts, valid, taps_of(tap), at_shift, at_valid, width)
        part = jnp.dot(
            weights[:, group[0] * channels : (group[-1] + 1) * channels],
            jnp.concatenate(rows, axis=0),
            preferred_element_type=F32,
        )
        total = part if total is None else total + part
    return total


def pack_body(brick, chan, rep, features, cotangent, neighbours, to_core, to_line, near, done):
    share, sites = features.shape
    copies = []
    for i, (out, last) in enumerate(((to_core, 1 - rep[0]), (to_line, rep[0]))):
        far = pl.ds(pl.multiple_of(last * (sites - FAR), 128), FAR)
        close = pl.ds(pl.multiple_of(last * (sites - HALO), 128), HALO)
        copies += [
            pltpu.make_async_copy(source, target, done.at[3 * i + j])
            for j, (source, target) in enumerate(
                [
                    (neighbours.at[:, close], near.at[i]),
                    (features.at[:, far], out.at[pl.ds(0, share), :]),
                    (cotangent.at[:, close], out.at[pl.ds(share, share), pl.ds(0, HALO)]),
                ]
            )
        ]
    for copy in copies:
        copy.start()
    for i, out in enumerate((to_core, to_line)):
        copies[3 * i].wait()
        kept = (near[i] >= 0).astype(F32)
        kept = jnp.concatenate([kept, jnp.zeros((32 - TAPS, HALO), F32)], axis=0)
        out[share : share + 32, HALO:] = kept.astype(BF16)
        copies[3 * i + 1].wait()
        copies[3 * i + 2].wait()


def ends_body(brick, chan, rep, core, line, before, behind, both):
    share = both.shape[0]

    def fill(first, second):
        before[...] = first[...]
        behind[...] = second[...]
        both[:, :NEAR] = first[:share, FAR - NEAR :]
        both[:, NEAR:] = second[:share, :NEAR]

    pl.when(rep[0] == 0)(functools.partial(fill, line, core))
    pl.when(rep[0] != 0)(functools.partial(fill, core, line))


def prepare_body(
    brick, chan, rep, by_out, features, neighbours, own, rest, by_in, shifts, valid, flat, kept, taken, near, done
):
    total = by_out.shape[2]
    share, sites = features.shape
    turn = lax.rem(total - chan[0] * share, total)
    copies = [
        pltpu.make_async_copy(source, target, done.at[i])
        for i, (source, target) in enumerate(
            [
                (by_out, taken),
                (features, shifts.at[4, :, pl.ds(FAR, sites)]),
                (neighbours, near),
            ]
        )
    ]
    for copy in copies:
        copy.start()
    copies[0].wait()
    flat[...] = jnp.zeros_like(flat)
    for group in groups():
        taps = []
        for tap in group:
            ring = pltpu.roll(taken[tap].astype(F32), turn, 1)
            flat[tap * share : (tap + 1) * share, :] = ring
            taps.append(ring)
        first, last = group[0], group[-1] + 1
        own[:, first * share : last * share] = jnp.concatenate(
            [x[:, :share] for x in taps], axis=1
        ).astype(BF16)
        left = total - share
        rest[:, first * left : last * left] = jnp.concatenate(
            [x[:, share:] for x in taps], axis=1
        ).astype(BF16)
    by_in[...] = flat[...].T.astype(BF16)
    copies[1].wait()
    shift(shifts, FAR + 128, FAR + sites - 128)
    copies[2].wait()
    kept[...] = (near[...] >= 0).astype(F32)
    for tap in range(TAPS):
        valid[tap, :, HALO : HALO + sites] = jnp.broadcast_to(
            kept[tap : tap + 1, :], (ROWS, sites)
        ).astype(BF16)


def own_body(left, right, weights, shifts_in, valid_in, begun, shifts, valid, kept):
    del shifts_in, valid_in
    share = begun.shape[0]
    far = shifts.shape[2] - FAR
    for side, at, start in ((left, 0, 128), (right, 1, far - 128)):
        shifts[4, :, at * far : at * far + FAR] = side[:share, :]
        shift(shifts, start, start + FAR)
        kept[...] = side[share : share + 32, HALO:].astype(F32)
        begin = at * (valid.shape[2] - HALO)
        for tap in range(TAPS):
            valid[tap, :, begin : begin + HALO] = jnp.broadcast_to(
                kept[tap : tap + 1, :], (ROWS, HALO)
            ).astype(BF16)

    def block(j, carry):
        start = pl.multiple_of(j * WIDTH, 128)
        begun[:, pl.ds(start, WIDTH)] = product(
            weights, shifts, valid, start + HALO, start, WIDTH, lambda tap: tap
        )
        return carry

    lax.fori_loop(0, begun.shape[1] // WIDTH, block, 0)


def arrive_body(rest, own_in, shifts, across, own):
    del own_in
    sites = rest.shape[1]
    shifts[4, :, FAR : FAR + sites] = rest[...]
    shift(shifts, FAR + 128, FAR + sites - 128)

    def block(j, carry):
        start = pl.multiple_of(j * WIDTH, 128)
        here = pl.ds(pl.multiple_of(start + FAR, 128), WIDTH)
        across[pl.ds(start, WIDTH), :] = jnp.concatenate(
            [own[4, :, here], shifts[4, :, here]], axis=0
        ).T
        return carry

    lax.fori_loop(0, sites // WIDTH, block, 0)


def rest_body(
    ends,
    shifts_in,
    weights,
    valid_in,
    begun,
    left,
    right,
    own,
    cotangent,
    output,
    grads,
    valid,
    shifts,
    grad,
    kept,
):
    del shifts_in, valid_in
    share, sites = cotangent.shape
    far = shifts.shape[2] - FAR
    shifts[4, :, : FAR - NEAR] = jnp.zeros((shifts.shape[1], FAR - NEAR), BF16)
    shifts[4, :, FAR - NEAR : FAR] = ends[:, :NEAR]
    shifts[4, :, far : far + NEAR] = ends[:, NEAR:]
    shifts[4, :, far + NEAR :] = jnp.zeros((shifts.shape[1], FAR - NEAR), BF16)
    shift(shifts, 128, 128 + FAR)
    shift(shifts, far - 128, far + FAR - 128)
    lead = LEAD + 128
    grad[:, lead : lead + HALO] = left[share : 2 * share, :HALO]
    grad[:, lead + HALO : lead + HALO + sites] = cotangent[...]
    grad[:, lead + HALO + sites :] = right[share : 2 * share, :HALO]

    def spread(start):
        for at in range(0, share, ROWS):
            rows = pl.ds(at, ROWS)
            window = grad[rows, pl.ds(start, WIDTH + 256)]
            for j, step in enumerate(STEPS):
                grads[j, rows, pl.ds(start, WIDTH)] = window[:, 128 + step : 128 + step + WIDTH]

    def block(j, carry):
        start = pl.multiple_of(j * WIDTH, 128)
        spread(start)
        here = pl.ds(start, WIDTH)
        there = pl.ds(pl.multiple_of(start + lead, 128), WIDTH)
        hidden = begun[:, here] + product(
            weights, shifts, valid, start + HALO, start, WIDTH, lambda tap: tap
        )
        sigma = 0.5 * jnp.tanh(0.5 * hidden) + 0.5
        features = own[4, :, pl.ds(pl.multiple_of(start + HALO, 128), WIDTH)]
        kept[:, here] = (features.astype(F32) + hidden * sigma).astype(BF16)
        grad[:, there] = (
            grad[:, there].astype(F32) * sigma * (1.0 + hidden * (1.0 - sigma))
        ).astype(BF16)
        return carry

    count = begun.shape[1] // WIDTH
    lax.fori_loop(0, count, block, 0)
    spread(count * WIDTH)
    output[...] = kept[:, HALO : HALO + sites]


def weight_body(half, brick, chan, rep, across, valid_in, grads_in, kept, sent, valid, grads, total):
    del valid_in, grads_in
    share, sites = grads.shape[1], across.shape[0]
    total[...] = jnp.zeros_like(total)

    def block(j, carry):
        start = pl.multiple_of(j * WIDTH, 128)
        features = across[pl.ds(start, WIDTH), :]
        for group in groups(MANY):
            rows = []
            for tap in group:
                rows += masked(
                    grads, valid, TAPS - 1 - tap, start + HALO + LEAD, start + HALO, WIDTH
                )
            total[group[0] * share : (group[-1] + 1) * share, :] += jnp.dot(
                jnp.concatenate(rows, axis=0), features, preferred_element_type=F32
            )
        return carry

    lax.fori_loop(0, sites // WIDTH, block, 0)
    mine = rep[0]
    kept[...] = total[pl.ds(pl.multiple_of(mine * half, ROWS), half), :]
    sent[...] = total[pl.ds(pl.multiple_of((1 - mine) * half, ROWS), half), :].astype(BF16)


def feature_body(part, weights, valid, grads, *refs):
    own, rest = refs[-2:]
    share, sites = own.shape
    begin = part * sites // 2

    def block(j, carry):
        start = pl.multiple_of(begin + j * WIDTH, 128)
        here = pl.ds(start, WIDTH)
        total = product(
            weights,
            grads,
            valid,
            start + HALO + LEAD,
            start + HALO,
            WIDTH,
            lambda tap: TAPS - 1 - tap,
        )
        own[:, here] = total[:share]
        rest[:, here] = total[share:].astype(BF16)
        return carry

    lax.fori_loop(0, sites // 2 // WIDTH, block, 0)


def split_body(brick, chan, rep, kept, arrived, mine, sent):
    size = mine.shape[0]
    at = brick[0] % 2
    mine_rows = pl.ds(pl.multiple_of(at * size, ROWS), size)
    sent_rows = pl.ds(pl.multiple_of((1 - at) * size, ROWS), size)
    mine[...] = kept[mine_rows, :] + arrived[mine_rows, :].astype(F32)
    sent[...] = (kept[sent_rows, :] + arrived[sent_rows, :].astype(F32)).astype(BF16)


def merge_body(mine, other, out):
    out[...] = (mine[...].astype(F32) + other[...].astype(F32)).astype(BF16)


def gather_body(brick, chan, rep, mine, other, side):
    size = mine.shape[0]
    at = brick[0] % 2
    side[pl.ds(pl.multiple_of(at * size, ROWS), size), :] = mine[...]
    side[pl.ds(pl.multiple_of((1 - at) * size, ROWS), size), :] = other[...]


def join_body(half, share, brick, chan, rep, side, other, out, both):
    mine = rep[0]
    both[pl.ds(pl.multiple_of(mine * half, ROWS), half), :] = side[...]
    both[pl.ds(pl.multiple_of((1 - mine) * half, ROWS), half), :] = other[...]
    out[...] = pltpu.roll(both[: out.shape[0], :].astype(F32), chan[0] * share, 1)


def add_body(cotangent, own, *rest):
    *terms, out, token = rest
    token[...] = jnp.zeros_like(token)
    total = cotangent[...].astype(F32) + own[...]
    for term in terms:
        total += term[...].astype(F32)
    out[...] = total.astype(BF16)


def line_swap(x):
    count = lax.axis_size(("brick", "rep"))
    pairs = [p for i in range(1, count - 1, 2) for p in ((i, i + 1), (i + 1, i))]
    return lax.ppermute(x, ("brick", "rep"), pairs)


def local(features, conv_weight, neighbours, cotangent):
    share, sites = features.shape
    total = conv_weight.shape[1]
    left = total - share
    chans, bricks, reps = (lax.axis_size(axis) for axis in ("chan", "brick", "rep"))
    place = [lax.axis_index(axis)[None] for axis in LINE]
    margin = sites + 2 * HALO
    flops = 2 * TAPS * share * sites

    def around(x):
        return [
            lax.ppermute(x, "chan", [((i + over) % chans, i) for i in range(chans)])
            for over in range(1, chans)
        ]

    def stack(parts):
        return parts[0] if len(parts) == 1 else jnp.concatenate(parts, axis=0)

    assert reps == 2
    swap = [(0, 1), (1, 0)]
    rest = stack(around(features))
    to_core, to_line = kernel(
        pack_body,
        "pack",
        [shape((share + max(share, 32), FAR))] * 2,
        [features, cotangent, neighbours],
        scalars=place,
        scratch=[pltpu.VMEM((2, TAPS, HALO), jnp.int32), pltpu.SemaphoreType.DMA((6,))],
        held=True,
    )
    line = line_swap(to_line)
    core = lax.ppermute(to_core, "rep", swap)
    lanes = -(-TAPS * share // 128) * 128
    own_weights, rest_weights, by_in, shifts, valid = kernel(
        prepare_body,
        "prepare",
        [
            shape((share, TAPS * share)),
            shape((share, TAPS * left)),
            shape((total, lanes)),
            shape((9, share, sites + 2 * FAR)),
            shape((TAPS, ROWS, margin)),
        ],
        [jnp.transpose(conv_weight, (0, 2, 1)), features, neighbours],
        scalars=place,
        scratch=[
            pltpu.VMEM((lanes, total), F32),
            pltpu.VMEM((TAPS, sites), F32),
            pltpu.VMEM((TAPS, share, total), BF16),
            pltpu.VMEM((TAPS, sites), jnp.int32),
            pltpu.SemaphoreType.DMA((3,)),
        ],
        held=True,
    )
    before, behind, both = kernel(
        after(ends_body, 3),
        "ends",
        [shape(core.shape), shape(core.shape), shape((share, 2 * NEAR))],
        [own_weights, core, line],
        scalars=place,
    )
    ends = stack(around(both))
    begun, own_shifts, valid = kernel(
        own_body,
        "forward_own",
        [shape((share, margin), F32), shape(shifts.shape), shape(valid.shape)],
        [before, behind, own_weights, shifts, valid],
        scratch=[pltpu.VMEM((32, HALO), F32)],
        aliases={3: 1, 4: 2},
    )
    rest_shifts, across, own_shifts = kernel(
        arrive_body,
        "arrive",
        [shape((9, left, sites + 2 * FAR)), shape((sites, total)), shape(own_shifts.shape)],
        [rest, own_shifts],
        aliases={1: 2},
    )
    output, grads, valid, _ = kernel(
        rest_body,
        "forward_rest",
        [
            shape((share, sites)),
            shape((9, share, margin + WIDTH)),
            shape(valid.shape),
            shape(rest_shifts.shape),
        ],
        [ends, rest_shifts, rest_weights, valid, begun, before, behind, own_shifts, cotangent],
        scratch=[
            pltpu.VMEM((share, LEAD + 128 + margin), BF16),
            pltpu.VMEM((share, margin), BF16),
        ],
        aliases={1: 3, 3: 2},
        flops=flops * left,
    )

    piece = -(-TAPS * share // (reps * bricks * ROWS)) * ROWS
    half = piece * bricks
    kept, sent, valid, grads = kernel(
        functools.partial(weight_body, half),
        "grad_weight",
        [shape((half, total), F32), shape((half, total)), shape(valid.shape), shape(grads.shape)],
        [across, valid, grads],
        scalars=place,
        scratch=[pltpu.VMEM((reps * half, total), F32)],
        aliases={1: 2, 2: 3},
        flops=flops * total,
    )
    arrived = lax.ppermute(sent, "rep", swap)

    def feature_part(part, body, args, kept):
        outs = [shape((share, sites), F32), shape((left, sites))]
        return kernel(
            body,
            "grad_features_%d" % part,
            [shape(x.shape) for x in kept] + outs,
            args,
            aliases={len(args) - len(kept) + i: i for i in range(len(kept))}
            if part == 0
            else {len(args) - 2 + i: i for i in range(2)},
            flops=flops * total // 2,
        )

    valid, grads, *parts = feature_part(
        0, functools.partial(feature_body, 0), [by_in, valid, grads], [valid, grads]
    )
    size = half // 2
    mine, sent = kernel(
        after(split_body, 3),
        "split",
        [shape((size, total), F32), shape((size, total))],
        [parts[0], kept, arrived],
        scalars=place,
        flops=LATER,
    )
    pairs = [(i, i ^ 1) for i in range(bricks)]
    arrived = lax.ppermute(sent, "brick", pairs)
    own, other = feature_part(
        1, after(functools.partial(feature_body, 1), 0), [mine, by_in, valid, grads, *parts], []
    )
    terms = [
        lax.ppermute(
            other if left == share else other[(over - 1) * share : over * share],
            "chan",
            [(i, (i + over) % chans) for i in range(chans)],
        )
        for over in range(1, chans)
    ]
    mine = kernel(
        after(merge_body, 0),
        "merge_1",
        shape((size, total)),
        [own, mine, arrived],
        flops=LATER,
    )
    step = 2
    while step < bricks:
        other = lax.ppermute(mine, "brick", [(i, i ^ step) for i in range(bricks)])
        step *= 2
        mine = kernel(
            merge_body, "merge_%d" % step, shape((size, total)), [mine, other], flops=LATER
        )
    other = lax.ppermute(mine, "brick", pairs)
    side = kernel(
        gather_body, "gather", shape((half, total)), [mine, other], scalars=place, flops=LATER
    )
    other = lax.ppermute(side, "rep", swap)
    grad_features, token = kernel(
        add_body,
        "add",
        [shape((share, sites)), shape((8, 128), F32)],
        [cotangent, own, *terms],
    )
    grad_weight = kernel(
        after(functools.partial(join_body, half, share), 3),
        "join",
        shape((TAPS * share, total), F32),
        [token, side, other],
        scalars=place,
        scratch=[pltpu.VMEM((reps * half, total), BF16)],
        flops=LATER,
    )
    grad_weight = jnp.transpose(grad_weight.reshape(TAPS, share, total), (0, 2, 1))
    return output, grad_features, grad_weight


def solution(mesh):
    return jax.shard_map(
        local,
        mesh=mesh,
        in_specs=(
            P("chan", ("scene", "brick", "rep")),
            P(None, None, "chan"),
            P(None, ("scene", "brick", "rep")),
            P("chan", ("scene", "brick", "rep")),
        ),
        out_specs=(
            P("chan", ("scene", "brick", "rep")),
            P("chan", ("scene", "brick", "rep")),
            P("scene", None, "chan"),
        ),
        check_vma=False,
    )
```

```python
import functools

import jax
import jax.numpy as jnp
from jax import lax
from jax.experimental import pallas as pl
from jax.experimental.pallas import tpu as pltpu
from jax.sharding import PartitionSpec as P

EDGE = 16
FACE = EDGE * EDGE
TAPS = 27
HALO = 384
FAR = 2 * HALO
NEAR = 640
LEAD = 896
MANY = 14
ROWS = 16
GROUP = 4
WIDTH = 768
LATER = 25 * 10**7
LINE = ("brick", "chan", "rep")
MIB = 1024 * 1024
F32, BF16 = jnp.float32, jnp.bfloat16

STEPS = [(k // 3 - 1) * EDGE + k % 3 - 1 for k in range(9)]

HERE = pl.BlockSpec(memory_space=pltpu.VMEM)
FAR_OFF = pl.BlockSpec(memory_space=pltpu.HBM)
SCALAR = pl.BlockSpec(memory_space=pltpu.SMEM)


def kernel(body, name, outs, args, scalars=(), scratch=(), aliases={}, limit=8, flops=0, held=False):
    if held:
        args = [pltpu.with_memory_space_constraint(x, pltpu.HBM) for x in args]
    single = not isinstance(outs, (tuple, list))
    return pl.pallas_call(
        body,
        out_shape=outs,
        in_specs=[SCALAR] * len(scalars) + [FAR_OFF if held else HERE] * len(args),
        out_specs=HERE if single else [HERE] * len(outs),
        scratch_shapes=list(scratch),
        input_output_aliases={len(scalars) + i: o for i, o in aliases.items()},
        compiler_params=pltpu.CompilerParams(vmem_limit_bytes=limit * MIB),
        cost_estimate=pl.CostEstimate(flops=flops, bytes_accessed=MIB, transcendentals=0),
        name=name,
    )(*scalars, *args)


def after(body, at):
    def ordered(*refs):
        body(*refs[:at], *refs[at + 1 :])

    return ordered


def shape(dims, kind=BF16):
    return jax.ShapeDtypeStruct(dims, kind)


def spread(window, target, rows, lanes):
    width = window.shape[1]
    for j, step in enumerate(STEPS):
        moved = pltpu.roll(window, -step % width, 1) if step else window
        target[j, rows, lanes] = moved[:, 128 : width - 128]


def shift(shifts, low, high):
    for at in range(0, shifts.shape[1], ROWS):
        rows = pl.ds(at, ROWS)
        spread(shifts[4, rows, low - 128 : high + 128], shifts, rows, slice(low, high))


def masked(shifts, valid, tap, at_shift, at_valid, width):
    keep = valid[tap, :, pl.ds(at_valid, width)]
    begin = pl.multiple_of(at_shift + (tap // 9 - 1) * FACE, 128)
    return [
        shifts[tap % 9, at : at + ROWS, pl.ds(begin, width)] * keep
        for at in range(0, shifts.shape[1], ROWS)
    ]


def groups(count=GROUP):
    return [range(first, min(first + count, TAPS)) for first in range(0, TAPS, count)]


def product(weights, shifts, valid, at_shift, at_valid, width, taps_of):
    channels = shifts.shape[1]
    total = None
    for group in groups():
        rows = []
        for tap in group:
            rows += masked(shifts, valid, taps_of(tap), at_shift, at_valid, width)
        part = jnp.dot(
            weights[:, group[0] * channels : (group[-1] + 1) * channels],
            jnp.concatenate(rows, axis=0),
            preferred_element_type=F32,
        )
        total = part if total is None else total + part
    return total


def pack_body(brick, chan, rep, features, cotangent, neighbours, to_core, to_line, near, done):
    share, sites = features.shape
    copies = []
    for i, (out, last) in enumerate(((to_core, 1 - rep[0]), (to_line, rep[0]))):
        far = pl.ds(pl.multiple_of(last * (sites - FAR), 128), FAR)
        close = pl.ds(pl.multiple_of(last * (sites - HALO), 128), HALO)
        copies += [
            pltpu.make_async_copy(source, target, done.at[3 * i + j])
            for j, (source, target) in enumerate(
                [
                    (neighbours.at[:, close], near.at[i]),
                    (features.at[:, far], out.at[pl.ds(0, share), :]),
                    (cotangent.at[:, close], out.at[pl.ds(share, share), pl.ds(0, HALO)]),
                ]
            )
        ]
    for copy in copies:
        copy.start()
    for i, out in enumerate((to_core, to_line)):
        copies[3 * i].wait()
        kept = (near[i] >= 0).astype(F32)
        kept = jnp.concatenate([kept, jnp.zeros((32 - TAPS, HALO), F32)], axis=0)
        out[share : share + 32, HALO:] = kept.astype(BF16)
        copies[3 * i + 1].wait()
        copies[3 * i + 2].wait()


def ends_body(brick, chan, rep, core, line, before, behind, both):
    share = both.shape[0]

    def fill(first, second):
        before[...] = first[...]
        behind[...] = second[...]
        both[:, :NEAR] = first[:share, FAR - NEAR :]
        both[:, NEAR:] = second[:share, :NEAR]

    pl.when(rep[0] == 0)(functools.partial(fill, line, core))
    pl.when(rep[0] != 0)(functools.partial(fill, core, line))


def prepare_body(
    brick, chan, rep, by_out, features, neighbours, own, rest, by_in, shifts, valid, flat, kept, taken, near, done
):
    total = by_out.shape[2]
    share, sites = features.shape
    turn = lax.rem(total - chan[0] * share, total)
    copies = [
        pltpu.make_async_copy(source, target, done.at[i])
        for i, (source, target) in enumerate(
            [
                (by_out, taken),
                (features, shifts.at[4, :, pl.ds(FAR, sites)]),
                (neighbours, near),
            ]
        )
    ]
    for copy in copies:
        copy.start()
    copies[0].wait()
    flat[...] = jnp.zeros_like(flat)
    for group in groups():
        taps = []
        for tap in group:
            ring = pltpu.roll(taken[tap].astype(F32), turn, 1)
            flat[tap * share : (tap + 1) * share, :] = ring.astype(BF16)
            taps.append(ring)
        first, last = group[0], group[-1] + 1
        own[:, first * share : last * share] = jnp.concatenate(
            [x[:, :share] for x in taps], axis=1
        ).astype(BF16)
        left = total - share
        rest[:, first * left : last * left] = jnp.concatenate(
            [x[:, share:] for x in taps], axis=1
        ).astype(BF16)
    by_in[...] = flat[...].T
    copies[1].wait()
    shift(shifts, FAR + 128, FAR + sites - 128)
    copies[2].wait()
    kept[...] = (near[...] >= 0).astype(F32)
    for tap in range(TAPS):
        valid[tap, :, HALO : HALO + sites] = jnp.broadcast_to(
            kept[tap : tap + 1, :], (ROWS, sites)
        ).astype(BF16)


def own_body(left, right, weights, shifts_in, valid_in, begun, shifts, valid, kept):
    del shifts_in, valid_in
    share = begun.shape[0]
    far = shifts.shape[2] - FAR
    for side, at, start in ((left, 0, 128), (right, 1, far - 128)):
        shifts[4, :, at * far : at * far + FAR] = side[:share, :]
        shift(shifts, start, start + FAR)
        kept[...] = side[share : share + 32, HALO:].astype(F32)
        begin = at * (valid.shape[2] - HALO)
        for tap in range(TAPS):
            valid[tap, :, begin : begin + HALO] = jnp.broadcast_to(
                kept[tap : tap + 1, :], (ROWS, HALO)
            ).astype(BF16)

    def block(j, carry):
        start = pl.multiple_of(j * WIDTH, 128)
        begun[:, pl.ds(start, WIDTH)] = product(
            weights, shifts, valid, start + HALO, start, WIDTH, lambda tap: tap
        )
        return carry

    lax.fori_loop(0, begun.shape[1] // WIDTH, block, 0)


def arrive_body(rest, own_in, shifts, across, own):
    del own_in
    sites = rest.shape[1]
    shifts[4, :, FAR : FAR + sites] = rest[...]
    shift(shifts, FAR + 128, FAR + sites - 128)

    def block(j, carry):
        start = pl.multiple_of(j * WIDTH, 128)
        here = pl.ds(pl.multiple_of(start + FAR, 128), WIDTH)
        across[pl.ds(start, WIDTH), :] = jnp.concatenate(
            [own[4, :, here], shifts[4, :, here]], axis=0
        ).T
        return carry

    lax.fori_loop(0, sites // WIDTH, block, 0)


def rest_body(
    ends,
    shifts_in,
    weights,
    valid_in,
    begun,
    left,
    right,
    own,
    cotangent,
    output,
    grads,
    valid,
    shifts,
    grad,
    kept,
    hidden,
):
    del shifts_in, valid_in
    share, sites = cotangent.shape
    far = shifts.shape[2] - FAR
    shifts[4, :, : FAR - NEAR] = jnp.zeros((shifts.shape[1], FAR - NEAR), BF16)
    shifts[4, :, FAR - NEAR : FAR] = ends[:, :NEAR]
    shifts[4, :, far : far + NEAR] = ends[:, NEAR:]
    shifts[4, :, far + NEAR :] = jnp.zeros((shifts.shape[1], FAR - NEAR), BF16)
    shift(shifts, 128, 128 + FAR)
    shift(shifts, far - 128, far + FAR - 128)
    lead = LEAD + 128
    grad[:, lead : lead + HALO] = left[share : 2 * share, :HALO]
    grad[:, lead + HALO : lead + HALO + sites] = cotangent[...]
    grad[:, lead + HALO + sites :] = right[share : 2 * share, :HALO]

    def finish(before, start):
        previous = pl.multiple_of(jnp.maximum(start - WIDTH, 0) + HALO, 128)
        there = pl.ds(pl.multiple_of(start - WIDTH + lead, 128), WIDTH)
        value = hidden[before]
        sigma = 0.5 * jnp.tanh(0.5 * value) + 0.5
        features = own[4, :, pl.ds(previous, WIDTH)]
        kept[:, pl.ds(start, WIDTH)] = (features.astype(F32) + value * sigma).astype(BF16)
        grad[:, there] = (
            grad[:, there].astype(F32) * sigma * (1.0 + value * (1.0 - sigma))
        ).astype(BF16)
        for at in range(0, share, ROWS):
            rows = pl.ds(at, ROWS)
            window = grad[rows, pl.ds(start, WIDTH + 256)]
            spread(window, grads, rows, pl.ds(start, WIDTH))

    def block(j, carry):
        start = pl.multiple_of(j * WIDTH, 128)
        finish((j + 1) % 2, start)
        hidden[j % 2] = begun[:, pl.ds(start, WIDTH)] + product(
            weights, shifts, valid, start + HALO, start, WIDTH, lambda tap: tap
        )
        return carry

    count = begun.shape[1] // WIDTH
    lax.fori_loop(0, count, block, 0)
    finish((count + 1) % 2, count * WIDTH)
    output[...] = kept[:, WIDTH + HALO : WIDTH + HALO + sites]


def weight_body(half, brick, chan, rep, across, valid_in, grads_in, kept, sent, valid, grads, total):
    del valid_in, grads_in
    share, sites = grads.shape[1], across.shape[0]
    total[...] = jnp.zeros_like(total)

    def block(j, carry):
        start = pl.multiple_of(j * WIDTH, 128)
        features = across[pl.ds(start, WIDTH), :]
        for group in groups(MANY):
            rows = []
            for tap in group:
                rows += masked(
                    grads, valid, TAPS - 1 - tap, start + HALO + LEAD, start + HALO, WIDTH
                )
            total[group[0] * share : (group[-1] + 1) * share, :] += jnp.dot(
                jnp.concatenate(rows, axis=0), features, preferred_element_type=F32
            )
        return carry

    lax.fori_loop(0, sites // WIDTH, block, 0)
    mine = rep[0]
    kept[...] = total[pl.ds(pl.multiple_of(mine * half, ROWS), half), :]
    sent[...] = total[pl.ds(pl.multiple_of((1 - mine) * half, ROWS), half), :].astype(BF16)


def feature_body(part, weights, valid, grads, *refs):
    own, rest = refs[-2:]
    share, sites = own.shape
    begin = part * sites // 2

    def block(j, carry):
        start = pl.multiple_of(begin + j * WIDTH, 128)
        here = pl.ds(start, WIDTH)
        total = product(
            weights,
            grads,
            valid,
            start + HALO + LEAD,
            start + HALO,
            WIDTH,
            lambda tap: TAPS - 1 - tap,
        )
        own[:, here] = total[:share]
        rest[:, here] = total[share:].astype(BF16)
        return carry

    lax.fori_loop(0, sites // 2 // WIDTH, block, 0)


def split_body(brick, chan, rep, kept, arrived, mine, sent):
    size = mine.shape[0]
    at = brick[0] % 2
    mine_rows = pl.ds(pl.multiple_of(at * size, ROWS), size)
    sent_rows = pl.ds(pl.multiple_of((1 - at) * size, ROWS), size)
    mine[...] = kept[mine_rows, :] + arrived[mine_rows, :].astype(F32)
    sent[...] = (kept[sent_rows, :] + arrived[sent_rows, :].astype(F32)).astype(BF16)


def merge_body(mine, other, out):
    out[...] = (mine[...].astype(F32) + other[...].astype(F32)).astype(BF16)


def gather_body(brick, chan, rep, mine, other, side):
    size = mine.shape[0]
    at = brick[0] % 2
    side[pl.ds(pl.multiple_of(at * size, ROWS), size), :] = mine[...]
    side[pl.ds(pl.multiple_of((1 - at) * size, ROWS), size), :] = other[...]


def join_body(half, share, brick, chan, rep, side, other, out, both):
    mine = rep[0]
    both[pl.ds(pl.multiple_of(mine * half, ROWS), half), :] = side[...]
    both[pl.ds(pl.multiple_of((1 - mine) * half, ROWS), half), :] = other[...]
    out[...] = pltpu.roll(both[: out.shape[0], :].astype(F32), chan[0] * share, 1)


def add_body(cotangent, own, *rest):
    *terms, out, token = rest
    token[...] = jnp.zeros_like(token)
    total = cotangent[...].astype(F32) + own[...]
    for term in terms:
        total += term[...].astype(F32)
    out[...] = total.astype(BF16)


def line_swap(x):
    count = lax.axis_size(("brick", "rep"))
    pairs = [p for i in range(1, count - 1, 2) for p in ((i, i + 1), (i + 1, i))]
    return lax.ppermute(x, ("brick", "rep"), pairs)


def local(features, conv_weight, neighbours, cotangent):
    share, sites = features.shape
    total = conv_weight.shape[1]
    left = total - share
    chans, bricks, reps = (lax.axis_size(axis) for axis in ("chan", "brick", "rep"))
    place = [lax.axis_index(axis)[None] for axis in LINE]
    margin = sites + 2 * HALO
    flops = 2 * TAPS * share * sites

    def around(x):
        return [
            lax.ppermute(x, "chan", [((i + over) % chans, i) for i in range(chans)])
            for over in range(1, chans)
        ]

    def stack(parts):
        return parts[0] if len(parts) == 1 else jnp.concatenate(parts, axis=0)

    assert reps == 2
    swap = [(0, 1), (1, 0)]
    rest = stack(around(features))
    to_core, to_line = kernel(
        pack_body,
        "pack",
        [shape((share + max(share, 32), FAR))] * 2,
        [features, cotangent, neighbours],
        scalars=place,
        scratch=[pltpu.VMEM((2, TAPS, HALO), jnp.int32), pltpu.SemaphoreType.DMA((6,))],
        held=True,
    )
    line = line_swap(to_line)
    core = lax.ppermute(to_core, "rep", swap)
    lanes = -(-TAPS * share // 128) * 128
    own_weights, rest_weights, by_in, shifts, valid = kernel(
        prepare_body,
        "prepare",
        [
            shape((share, TAPS * share)),
            shape((share, TAPS * left)),
            shape((total, lanes)),
            shape((9, share, sites + 2 * FAR)),
            shape((TAPS, ROWS, margin)),
        ],
        [jnp.transpose(conv_weight, (0, 2, 1)), features, neighbours],
        scalars=place,
        scratch=[
            pltpu.VMEM((lanes, total), BF16),
            pltpu.VMEM((TAPS, sites), F32),
            pltpu.VMEM((TAPS, share, total), BF16),
            pltpu.VMEM((TAPS, sites), jnp.int32),
            pltpu.SemaphoreType.DMA((3,)),
        ],
        held=True,
    )
    before, behind, both = kernel(
        after(ends_body, 3),
        "ends",
        [shape(core.shape), shape(core.shape), shape((share, 2 * NEAR))],
        [own_weights, core, line],
        scalars=place,
    )
    ends = stack(around(both))
    begun, own_shifts, valid = kernel(
        own_body,
        "forward_own",
        [shape((share, margin), F32), shape(shifts.shape), shape(valid.shape)],
        [before, behind, own_weights, shifts, valid],
        scratch=[pltpu.VMEM((32, HALO), F32)],
        aliases={3: 1, 4: 2},
    )
    rest_shifts, across, own_shifts = kernel(
        arrive_body,
        "arrive",
        [shape((9, left, sites + 2 * FAR)), shape((sites, total)), shape(own_shifts.shape)],
        [rest, own_shifts],
        aliases={1: 2},
    )
    output, grads, valid, _ = kernel(
        rest_body,
        "forward_rest",
        [
            shape((share, sites)),
            shape((9, share, margin + WIDTH)),
            shape(valid.shape),
            shape(rest_shifts.shape),
        ],
        [ends, rest_shifts, rest_weights, valid, begun, before, behind, own_shifts, cotangent],
        scratch=[
            pltpu.VMEM((share, LEAD + 128 + margin), BF16),
            pltpu.VMEM((share, WIDTH + margin), BF16),
            pltpu.VMEM((2, share, WIDTH), F32),
        ],
        aliases={1: 3, 3: 2},
        flops=flops * left,
    )

    piece = -(-TAPS * share // (reps * bricks * ROWS)) * ROWS
    half = piece * bricks
    kept, sent, valid, grads = kernel(
        functools.partial(weight_body, half),
        "grad_weight",
        [shape((half, total), F32), shape((half, total)), shape(valid.shape), shape(grads.shape)],
        [across, valid, grads],
        scalars=place,
        scratch=[pltpu.VMEM((reps * half, total), F32)],
        aliases={1: 2, 2: 3},
        flops=flops * total,
    )
    arrived = lax.ppermute(sent, "rep", swap)

    def feature_part(part, body, args, kept):
        outs = [shape((share, sites), F32), shape((left, sites))]
        return kernel(
            body,
            "grad_features_%d" % part,
            [shape(x.shape) for x in kept] + outs,
            args,
            aliases={len(args) - len(kept) + i: i for i in range(len(kept))}
            if part == 0
            else {len(args) - 2 + i: i for i in range(2)},
            flops=flops * total // 2,
        )

    valid, grads, *parts = feature_part(
        0, functools.partial(feature_body, 0), [by_in, valid, grads], [valid, grads]
    )
    size = half // 2
    mine, sent = kernel(
        after(split_body, 3),
        "split",
        [shape((size, total), F32), shape((size, total))],
        [parts[0], kept, arrived],
        scalars=place,
        flops=LATER,
    )
    pairs = [(i, i ^ 1) for i in range(bricks)]
    arrived = lax.ppermute(sent, "brick", pairs)
    own, other = feature_part(
        1, after(functools.partial(feature_body, 1), 0), [mine, by_in, valid, grads, *parts], []
    )
    terms = [
        lax.ppermute(
            other if left == share else other[(over - 1) * share : over * share],
            "chan",
            [(i, (i + over) % chans) for i in range(chans)],
        )
        for over in range(1, chans)
    ]
    mine = kernel(
        after(merge_body, 0),
        "merge_1",
        shape((size, total)),
        [own, mine, arrived],
        flops=LATER,
    )
    step = 2
    while step < bricks:
        other = lax.ppermute(mine, "brick", [(i, i ^ step) for i in range(bricks)])
        step *= 2
        mine = kernel(
            merge_body, "merge_%d" % step, shape((size, total)), [mine, other], flops=LATER
        )
    other = lax.ppermute(mine, "brick", pairs)
    side = kernel(
        gather_body, "gather", shape((half, total)), [mine, other], scalars=place, flops=LATER
    )
    other = lax.ppermute(side, "rep", swap)
    grad_features, token = kernel(
        add_body,
        "add",
        [shape((share, sites)), shape((8, 128), F32)],
        [cotangent, own, *terms],
    )
    grad_weight = kernel(
        after(functools.partial(join_body, half, share), 3),
        "join",
        shape((TAPS * share, total), F32),
        [token, side, other],
        scalars=place,
        scratch=[pltpu.VMEM((reps * half, total), BF16)],
        flops=LATER,
    )
    grad_weight = jnp.transpose(grad_weight.reshape(TAPS, share, total), (0, 2, 1))
    return output, grad_features, grad_weight


def solution(mesh):
    return jax.shard_map(
        local,
        mesh=mesh,
        in_specs=(
            P("chan", ("scene", "brick", "rep")),
            P(None, None, "chan"),
            P(None, ("scene", "brick", "rep")),
            P("chan", ("scene", "brick", "rep")),
        ),
        out_specs=(
            P("chan", ("scene", "brick", "rep")),
            P("chan", ("scene", "brick", "rep")),
            P("scene", None, "chan"),
        ),
        check_vma=False,
    )
```

```python
import functools

import jax
import jax.numpy as jnp
from jax import lax
from jax.experimental import pallas as pl
from jax.experimental.pallas import tpu as pltpu
from jax.sharding import PartitionSpec as P

EDGE = 16
FACE = EDGE * EDGE
TAPS = 27
HALO = 384
FAR = 2 * HALO
NEAR = 640
LEAD = 896
MANY = 14
ROWS = 16
GROUP = 4
WIDTH = 768
LATER = 25 * 10**7
LINE = ("brick", "chan", "rep")
MIB = 1024 * 1024
F32, BF16 = jnp.float32, jnp.bfloat16

STEPS = [(k // 3 - 1) * EDGE + k % 3 - 1 for k in range(9)]

HERE = pl.BlockSpec(memory_space=pltpu.VMEM)
FAR_OFF = pl.BlockSpec(memory_space=pltpu.HBM)
SCALAR = pl.BlockSpec(memory_space=pltpu.SMEM)


def kernel(body, name, outs, args, scalars=(), scratch=(), aliases={}, limit=8, flops=0, held=False):
    if held:
        args = [pltpu.with_memory_space_constraint(x, pltpu.HBM) for x in args]
    single = not isinstance(outs, (tuple, list))
    return pl.pallas_call(
        body,
        out_shape=outs,
        in_specs=[SCALAR] * len(scalars) + [FAR_OFF if held else HERE] * len(args),
        out_specs=HERE if single else [HERE] * len(outs),
        scratch_shapes=list(scratch),
        input_output_aliases={len(scalars) + i: o for i, o in aliases.items()},
        compiler_params=pltpu.CompilerParams(vmem_limit_bytes=limit * MIB),
        cost_estimate=pl.CostEstimate(flops=flops, bytes_accessed=MIB, transcendentals=0),
        name=name,
    )(*scalars, *args)


def after(body, at):
    def ordered(*refs):
        body(*refs[:at], *refs[at + 1 :])

    return ordered


def shape(dims, kind=BF16):
    return jax.ShapeDtypeStruct(dims, kind)


def spread(window, target, rows, lanes):
    width = window.shape[1]
    for j, step in enumerate(STEPS):
        moved = pltpu.roll(window, -step % width, 1) if step else window
        target[j, rows, lanes] = moved[:, 128 : width - 128]


def shift(shifts, low, high):
    for at in range(0, shifts.shape[1], ROWS):
        rows = pl.ds(at, ROWS)
        spread(shifts[4, rows, low - 128 : high + 128], shifts, rows, slice(low, high))


def masked(shifts, valid, tap, at_shift, at_valid, width):
    keep = valid[tap, :, pl.ds(at_valid, width)]
    begin = pl.multiple_of(at_shift + (tap // 9 - 1) * FACE, 128)
    return [
        shifts[tap % 9, at : at + ROWS, pl.ds(begin, width)] * keep
        for at in range(0, shifts.shape[1], ROWS)
    ]


def groups(count=GROUP):
    return [range(first, min(first + count, TAPS)) for first in range(0, TAPS, count)]


def product(weights, shifts, valid, at_shift, at_valid, width, taps_of, between=()):
    channels = shifts.shape[1]
    total = None
    for at, group in enumerate(groups()):
        for piece in between[at :: len(groups())]:
            piece()
        rows = []
        for tap in group:
            rows += masked(shifts, valid, taps_of(tap), at_shift, at_valid, width)
        part = jnp.dot(
            weights[:, group[0] * channels : (group[-1] + 1) * channels],
            jnp.concatenate(rows, axis=0),
            preferred_element_type=F32,
        )
        total = part if total is None else total + part
    return total


def pack_body(brick, chan, rep, features, cotangent, neighbours, to_core, to_line, near, done):
    share, sites = features.shape
    copies = []
    for i, (out, last) in enumerate(((to_core, 1 - rep[0]), (to_line, rep[0]))):
        far = pl.ds(pl.multiple_of(last * (sites - FAR), 128), FAR)
        close = pl.ds(pl.multiple_of(last * (sites - HALO), 128), HALO)
        copies += [
            pltpu.make_async_copy(source, target, done.at[3 * i + j])
            for j, (source, target) in enumerate(
                [
                    (neighbours.at[:, close], near.at[i]),
                    (features.at[:, far], out.at[pl.ds(0, share), :]),
                    (cotangent.at[:, close], out.at[pl.ds(share, share), pl.ds(0, HALO)]),
                ]
            )
        ]
    for copy in copies:
        copy.start()
    for i, out in enumerate((to_core, to_line)):
        copies[3 * i].wait()
        kept = (near[i] >= 0).astype(F32)
        kept = jnp.concatenate([kept, jnp.zeros((32 - TAPS, HALO), F32)], axis=0)
        out[share : share + 32, HALO:] = kept.astype(BF16)
        copies[3 * i + 1].wait()
        copies[3 * i + 2].wait()


def ends_body(brick, chan, rep, core, line, before, behind, both):
    share = both.shape[0]

    def fill(first, second):
        before[...] = first[...]
        behind[...] = second[...]
        both[:, :NEAR] = first[:share, FAR - NEAR :]
        both[:, NEAR:] = second[:share, :NEAR]

    pl.when(rep[0] == 0)(functools.partial(fill, line, core))
    pl.when(rep[0] != 0)(functools.partial(fill, core, line))


def prepare_body(
    brick, chan, rep, by_out, features, neighbours, own, rest, by_in, shifts, valid, flat, kept, taken, near, done
):
    total = by_out.shape[2]
    share, sites = features.shape
    turn = lax.rem(total - chan[0] * share, total)
    copies = [
        pltpu.make_async_copy(source, target, done.at[i])
        for i, (source, target) in enumerate(
            [
                (by_out, taken),
                (features, shifts.at[4, :, pl.ds(FAR, sites)]),
                (neighbours, near),
            ]
        )
    ]
    for copy in copies:
        copy.start()
    copies[0].wait()
    flat[...] = jnp.zeros_like(flat)
    for group in groups():
        taps = []
        for tap in group:
            ring = pltpu.roll(taken[tap].astype(F32), turn, 1)
            flat[tap * share : (tap + 1) * share, :] = ring.astype(BF16)
            taps.append(ring)
        first, last = group[0], group[-1] + 1
        own[:, first * share : last * share] = jnp.concatenate(
            [x[:, :share] for x in taps], axis=1
        ).astype(BF16)
        left = total - share
        rest[:, first * left : last * left] = jnp.concatenate(
            [x[:, share:] for x in taps], axis=1
        ).astype(BF16)
    by_in[...] = flat[...].T
    copies[1].wait()
    shift(shifts, FAR + 128, FAR + sites - 128)
    copies[2].wait()
    kept[...] = (near[...] >= 0).astype(F32)
    for tap in range(TAPS):
        valid[tap, :, HALO : HALO + sites] = jnp.broadcast_to(
            kept[tap : tap + 1, :], (ROWS, sites)
        ).astype(BF16)


def own_body(left, right, weights, shifts_in, valid_in, begun, shifts, valid, kept):
    del shifts_in, valid_in
    share = begun.shape[0]
    far = shifts.shape[2] - FAR
    for side, at, start in ((left, 0, 128), (right, 1, far - 128)):
        shifts[4, :, at * far : at * far + FAR] = side[:share, :]
        shift(shifts, start, start + FAR)
        kept[...] = side[share : share + 32, HALO:].astype(F32)
        begin = at * (valid.shape[2] - HALO)
        for tap in range(TAPS):
            valid[tap, :, begin : begin + HALO] = jnp.broadcast_to(
                kept[tap : tap + 1, :], (ROWS, HALO)
            ).astype(BF16)

    def block(j, carry):
        start = pl.multiple_of(j * WIDTH, 128)
        begun[:, pl.ds(start, WIDTH)] = product(
            weights, shifts, valid, start + HALO, start, WIDTH, lambda tap: tap
        )
        return carry

    lax.fori_loop(0, begun.shape[1] // WIDTH, block, 0)


def arrive_body(rest, own_in, shifts, across, own):
    del own_in
    sites = rest.shape[1]
    shifts[4, :, FAR : FAR + sites] = rest[...]
    shift(shifts, FAR + 128, FAR + sites - 128)

    def block(j, carry):
        start = pl.multiple_of(j * WIDTH, 128)
        here = pl.ds(pl.multiple_of(start + FAR, 128), WIDTH)
        across[pl.ds(start, WIDTH), :] = jnp.concatenate(
            [own[4, :, here], shifts[4, :, here]], axis=0
        ).T
        return carry

    lax.fori_loop(0, sites // WIDTH, block, 0)


def rest_body(
    ends,
    shifts_in,
    weights,
    valid_in,
    begun,
    left,
    right,
    own,
    cotangent,
    output,
    grads,
    valid,
    shifts,
    grad,
    kept,
    hidden,
):
    del shifts_in, valid_in
    share, sites = cotangent.shape
    far = shifts.shape[2] - FAR
    shifts[4, :, : FAR - NEAR] = jnp.zeros((shifts.shape[1], FAR - NEAR), BF16)
    shifts[4, :, FAR - NEAR : FAR] = ends[:, :NEAR]
    shifts[4, :, far : far + NEAR] = ends[:, NEAR:]
    shifts[4, :, far + NEAR :] = jnp.zeros((shifts.shape[1], FAR - NEAR), BF16)
    shift(shifts, 128, 128 + FAR)
    shift(shifts, far - 128, far + FAR - 128)
    lead = LEAD + 128
    grad[:, lead : lead + HALO] = left[share : 2 * share, :HALO]
    grad[:, lead + HALO : lead + HALO + sites] = cotangent[...]
    grad[:, lead + HALO + sites :] = right[share : 2 * share, :HALO]

    def finish(before, start, at):
        rows = pl.ds(at, ROWS)
        previous = pl.multiple_of(jnp.maximum(start - WIDTH, 0) + HALO, 128)
        there = pl.ds(pl.multiple_of(start - WIDTH + lead, 128), WIDTH)
        value = hidden[before, rows, :]
        sigma = 0.5 * jnp.tanh(0.5 * value) + 0.5
        features = own[4, rows, pl.ds(previous, WIDTH)]
        kept[rows, pl.ds(start, WIDTH)] = (features.astype(F32) + value * sigma).astype(BF16)
        grad[rows, there] = (
            grad[rows, there].astype(F32) * sigma * (1.0 + value * (1.0 - sigma))
        ).astype(BF16)
        window = grad[rows, pl.ds(start, WIDTH + 256)]
        spread(window, grads, rows, pl.ds(start, WIDTH))

    def finishes(before, start):
        return [functools.partial(finish, before, start, at) for at in range(0, share, ROWS)]

    def block(j, carry):
        start = pl.multiple_of(j * WIDTH, 128)
        hidden[j % 2] = begun[:, pl.ds(start, WIDTH)] + product(
            weights,
            shifts,
            valid,
            start + HALO,
            start,
            WIDTH,
            lambda tap: tap,
            [lambda: None, *finishes((j + 1) % 2, start)],
        )
        return carry

    count = begun.shape[1] // WIDTH
    lax.fori_loop(0, count, block, 0)
    for piece in finishes((count + 1) % 2, count * WIDTH):
        piece()
    output[...] = kept[:, WIDTH + HALO : WIDTH + HALO + sites]


def weight_body(half, brick, chan, rep, across, valid_in, grads_in, kept, sent, valid, grads, total):
    del valid_in, grads_in
    share, sites = grads.shape[1], across.shape[0]
    total[...] = jnp.zeros_like(total)

    def block(j, carry):
        start = pl.multiple_of(j * WIDTH, 128)
        features = across[pl.ds(start, WIDTH), :]
        for group in groups(MANY):
            rows = []
            for tap in group:
                rows += masked(
                    grads, valid, TAPS - 1 - tap, start + HALO + LEAD, start + HALO, WIDTH
                )
            total[group[0] * share : (group[-1] + 1) * share, :] += jnp.dot(
                jnp.concatenate(rows, axis=0), features, preferred_element_type=F32
            )
        return carry

    lax.fori_loop(0, sites // WIDTH, block, 0)
    mine = rep[0]
    kept[...] = total[pl.ds(pl.multiple_of(mine * half, ROWS), half), :]
    sent[...] = total[pl.ds(pl.multiple_of((1 - mine) * half, ROWS), half), :].astype(BF16)


def feature_body(part, weights, valid, grads, *refs):
    own, rest = refs[-2:]
    share, sites = own.shape
    begin = part * sites // 2

    def block(j, carry):
        start = pl.multiple_of(begin + j * WIDTH, 128)
        here = pl.ds(start, WIDTH)
        total = product(
            weights,
            grads,
            valid,
            start + HALO + LEAD,
            start + HALO,
            WIDTH,
            lambda tap: TAPS - 1 - tap,
        )
        own[:, here] = total[:share]
        rest[:, here] = total[share:].astype(BF16)
        return carry

    lax.fori_loop(0, sites // 2 // WIDTH, block, 0)


def split_body(brick, chan, rep, kept, arrived, mine, sent):
    size = mine.shape[0]
    at = brick[0] % 2
    mine_rows = pl.ds(pl.multiple_of(at * size, ROWS), size)
    sent_rows = pl.ds(pl.multiple_of((1 - at) * size, ROWS), size)
    mine[...] = kept[mine_rows, :] + arrived[mine_rows, :].astype(F32)
    sent[...] = (kept[sent_rows, :] + arrived[sent_rows, :].astype(F32)).astype(BF16)


def merge_body(mine, other, out):
    out[...] = (mine[...].astype(F32) + other[...].astype(F32)).astype(BF16)


def gather_body(brick, chan, rep, mine, other, side):
    size = mine.shape[0]
    at = brick[0] % 2
    side[pl.ds(pl.multiple_of(at * size, ROWS), size), :] = mine[...]
    side[pl.ds(pl.multiple_of((1 - at) * size, ROWS), size), :] = other[...]


def join_body(half, share, brick, chan, rep, side, other, out, both):
    mine = rep[0]
    both[pl.ds(pl.multiple_of(mine * half, ROWS), half), :] = side[...]
    both[pl.ds(pl.multiple_of((1 - mine) * half, ROWS), half), :] = other[...]
    out[...] = pltpu.roll(both[: out.shape[0], :].astype(F32), chan[0] * share, 1)


def add_body(cotangent, own, *rest):
    *terms, out, token = rest
    token[...] = jnp.zeros_like(token)
    total = cotangent[...].astype(F32) + own[...]
    for term in terms:
        total += term[...].astype(F32)
    out[...] = total.astype(BF16)


def line_swap(x):
    count = lax.axis_size(("brick", "rep"))
    pairs = [p for i in range(1, count - 1, 2) for p in ((i, i + 1), (i + 1, i))]
    return lax.ppermute(x, ("brick", "rep"), pairs)


def local(features, conv_weight, neighbours, cotangent):
    share, sites = features.shape
    total = conv_weight.shape[1]
    left = total - share
    chans, bricks, reps = (lax.axis_size(axis) for axis in ("chan", "brick", "rep"))
    place = [lax.axis_index(axis)[None] for axis in LINE]
    margin = sites + 2 * HALO
    flops = 2 * TAPS * share * sites

    def around(x):
        return [
            lax.ppermute(x, "chan", [((i + over) % chans, i) for i in range(chans)])
            for over in range(1, chans)
        ]

    def stack(parts):
        return parts[0] if len(parts) == 1 else jnp.concatenate(parts, axis=0)

    assert reps == 2
    swap = [(0, 1), (1, 0)]
    rest = stack(around(features))
    to_core, to_line = kernel(
        pack_body,
        "pack",
        [shape((share + max(share, 32), FAR))] * 2,
        [features, cotangent, neighbours],
        scalars=place,
        scratch=[pltpu.VMEM((2, TAPS, HALO), jnp.int32), pltpu.SemaphoreType.DMA((6,))],
        held=True,
    )
    line = line_swap(to_line)
    core = lax.ppermute(to_core, "rep", swap)
    lanes = -(-TAPS * share // 128) * 128
    own_weights, rest_weights, by_in, shifts, valid = kernel(
        prepare_body,
        "prepare",
        [
            shape((share, TAPS * share)),
            shape((share, TAPS * left)),
            shape((total, lanes)),
            shape((9, share, sites + 2 * FAR)),
            shape((TAPS, ROWS, margin)),
        ],
        [jnp.transpose(conv_weight, (0, 2, 1)), features, neighbours],
        scalars=place,
        scratch=[
            pltpu.VMEM((lanes, total), BF16),
            pltpu.VMEM((TAPS, sites), F32),
            pltpu.VMEM((TAPS, share, total), BF16),
            pltpu.VMEM((TAPS, sites), jnp.int32),
            pltpu.SemaphoreType.DMA((3,)),
        ],
        held=True,
    )
    before, behind, both = kernel(
        after(ends_body, 3),
        "ends",
        [shape(core.shape), shape(core.shape), shape((share, 2 * NEAR))],
        [own_weights, core, line],
        scalars=place,
    )
    ends = stack(around(both))
    begun, own_shifts, valid = kernel(
        own_body,
        "forward_own",
        [shape((share, margin), F32), shape(shifts.shape), shape(valid.shape)],
        [before, behind, own_weights, shifts, valid],
        scratch=[pltpu.VMEM((32, HALO), F32)],
        aliases={3: 1, 4: 2},
    )
    rest_shifts, across, own_shifts = kernel(
        arrive_body,
        "arrive",
        [shape((9, left, sites + 2 * FAR)), shape((sites, total)), shape(own_shifts.shape)],
        [rest, own_shifts],
        aliases={1: 2},
    )
    output, grads, valid, _ = kernel(
        rest_body,
        "forward_rest",
        [
            shape((share, sites)),
            shape((9, share, margin + WIDTH)),
            shape(valid.shape),
            shape(rest_shifts.shape),
        ],
        [ends, rest_shifts, rest_weights, valid, begun, before, behind, own_shifts, cotangent],
        scratch=[
            pltpu.VMEM((share, LEAD + 128 + margin), BF16),
            pltpu.VMEM((share, WIDTH + margin), BF16),
            pltpu.VMEM((2, share, WIDTH), F32),
        ],
        aliases={1: 3, 3: 2},
        flops=flops * left,
    )

    piece = -(-TAPS * share // (reps * bricks * ROWS)) * ROWS
    half = piece * bricks
    kept, sent, valid, grads = kernel(
        functools.partial(weight_body, half),
        "grad_weight",
        [shape((half, total), F32), shape((half, total)), shape(valid.shape), shape(grads.shape)],
        [across, valid, grads],
        scalars=place,
        scratch=[pltpu.VMEM((reps * half, total), F32)],
        aliases={1: 2, 2: 3},
        flops=flops * total,
    )
    arrived = lax.ppermute(sent, "rep", swap)

    def feature_part(part, body, args, kept):
        outs = [shape((share, sites), F32), shape((left, sites))]
        return kernel(
            body,
            "grad_features_%d" % part,
            [shape(x.shape) for x in kept] + outs,
            args,
            aliases={len(args) - len(kept) + i: i for i in range(len(kept))}
            if part == 0
            else {len(args) - 2 + i: i for i in range(2)},
            flops=flops * total // 2,
        )

    valid, grads, *parts = feature_part(
        0, functools.partial(feature_body, 0), [by_in, valid, grads], [valid, grads]
    )
    size = half // 2
    mine, sent = kernel(
        after(split_body, 3),
        "split",
        [shape((size, total), F32), shape((size, total))],
        [parts[0], kept, arrived],
        scalars=place,
        flops=LATER,
    )
    pairs = [(i, i ^ 1) for i in range(bricks)]
    arrived = lax.ppermute(sent, "brick", pairs)
    own, other = feature_part(
        1, after(functools.partial(feature_body, 1), 0), [mine, by_in, valid, grads, *parts], []
    )
    terms = [
        lax.ppermute(
            other if left == share else other[(over - 1) * share : over * share],
            "chan",
            [(i, (i + over) % chans) for i in range(chans)],
        )
        for over in range(1, chans)
    ]
    mine = kernel(
        after(merge_body, 0),
        "merge_1",
        shape((size, total)),
        [own, mine, arrived],
        flops=LATER,
    )
    step = 2
    while step < bricks:
        other = lax.ppermute(mine, "brick", [(i, i ^ step) for i in range(bricks)])
        step *= 2
        mine = kernel(
            merge_body, "merge_%d" % step, shape((size, total)), [mine, other], flops=LATER
        )
    other = lax.ppermute(mine, "brick", pairs)
    side = kernel(
        gather_body, "gather", shape((half, total)), [mine, other], scalars=place, flops=LATER
    )
    other = lax.ppermute(side, "rep", swap)
    grad_features, token = kernel(
        add_body,
        "add",
        [shape((share, sites)), shape((8, 128), F32)],
        [cotangent, own, *terms],
    )
    grad_weight = kernel(
        after(functools.partial(join_body, half, share), 3),
        "join",
        shape((TAPS * share, total), F32),
        [token, side, other],
        scalars=place,
        scratch=[pltpu.VMEM((reps * half, total), BF16)],
        flops=LATER,
    )
    grad_weight = jnp.transpose(grad_weight.reshape(TAPS, share, total), (0, 2, 1))
    return output, grad_features, grad_weight


def solution(mesh):
    return jax.shard_map(
        local,
        mesh=mesh,
        in_specs=(
            P("chan", ("scene", "brick", "rep")),
            P(None, None, "chan"),
            P(None, ("scene", "brick", "rep")),
            P("chan", ("scene", "brick", "rep")),
        ),
        out_specs=(
            P("chan", ("scene", "brick", "rep")),
            P("chan", ("scene", "brick", "rep")),
            P("scene", None, "chan"),
        ),
        check_vma=False,
    )
```

```python
import functools

import jax
import jax.numpy as jnp
from jax import lax
from jax.experimental import pallas as pl
from jax.experimental.pallas import tpu as pltpu
from jax.sharding import PartitionSpec as P

EDGE = 16
FACE = EDGE * EDGE
TAPS = 27
HALO = 384
FAR = 2 * HALO
NEAR = 640
LEAD = 896
MANY = 14
ROWS = 16
LANES = 128
GROUP = 4
TILES = 6
WIDTH = TILES * LANES
LATER = 25 * 10**7
LINE = ("brick", "chan", "rep")
MIB = 1024 * 1024
F32, BF16 = jnp.float32, jnp.bfloat16

STEPS = [(k // 3 - 1) * EDGE + k % 3 - 1 for k in range(9)]

HERE = pl.BlockSpec(memory_space=pltpu.VMEM)
FAR_OFF = pl.BlockSpec(memory_space=pltpu.HBM)
SCALAR = pl.BlockSpec(memory_space=pltpu.SMEM)


def kernel(body, name, outs, args, scalars=(), scratch=(), aliases={}, limit=8, flops=0, held=False):
    if held:
        args = [pltpu.with_memory_space_constraint(x, pltpu.HBM) for x in args]
    single = not isinstance(outs, (tuple, list))
    return pl.pallas_call(
        body,
        out_shape=outs,
        in_specs=[SCALAR] * len(scalars) + [FAR_OFF if held else HERE] * len(args),
        out_specs=HERE if single else [HERE] * len(outs),
        scratch_shapes=list(scratch),
        input_output_aliases={len(scalars) + i: o for i, o in aliases.items()},
        compiler_params=pltpu.CompilerParams(vmem_limit_bytes=limit * MIB),
        cost_estimate=pl.CostEstimate(flops=flops, bytes_accessed=MIB, transcendentals=0),
        name=name,
    )(*scalars, *args)


def after(body, at):
    def ordered(*refs):
        body(*refs[:at], *refs[at + 1 :])

    return ordered


def shape(dims, kind=BF16):
    return jax.ShapeDtypeStruct(dims, kind)


def wide(ref, first, count, *rows):
    return jnp.concatenate([ref[(first + i, *rows)] for i in range(count)], axis=1)


def lay(ref, first, value, *rows):
    for i in range(value.shape[1] // LANES):
        ref[(first + i, *rows)] = value[:, i * LANES : (i + 1) * LANES]


def spread(window, target, rows, first):
    width = window.shape[1]
    for j, step in enumerate(STEPS):
        moved = pltpu.roll(window, -step % width, 1) if step else window
        lay(target.at[j], first, moved[:, LANES : width - LANES], rows)


def shift(shifts, low, high):
    for at in range(0, shifts.shape[2], ROWS):
        rows = pl.ds(at, ROWS)
        spread(wide(shifts.at[4], low - 1, high - low + 2, rows), shifts, rows, low)


def masked(shifts, valid, tap, at_shift, at_valid):
    keep = wide(valid.at[tap], at_valid, TILES)
    begin = at_shift + (tap // 9 - 1) * FACE // LANES
    return [
        wide(shifts.at[tap % 9], begin, TILES, pl.ds(at, ROWS)) * keep
        for at in range(0, shifts.shape[2], ROWS)
    ]


def groups(count=GROUP):
    return [range(first, min(first + count, TAPS)) for first in range(0, TAPS, count)]


def product(weights, shifts, valid, at_shift, at_valid, taps_of, between=()):
    channels = shifts.shape[2]
    total = None
    for at, group in enumerate(groups()):
        for piece in between[at :: len(groups())]:
            piece()
        rows = []
        for tap in group:
            rows += masked(shifts, valid, taps_of(tap), at_shift, at_valid)
        part = jnp.dot(
            weights[:, group[0] * channels : (group[-1] + 1) * channels],
            jnp.concatenate(rows, axis=0),
            preferred_element_type=F32,
        )
        total = part if total is None else total + part
    return total


def pack_body(brick, chan, rep, features, cotangent, neighbours, to_core, to_line, near, done):
    share, sites = features.shape
    copies = []
    for i, (out, last) in enumerate(((to_core, 1 - rep[0]), (to_line, rep[0]))):
        far = pl.ds(pl.multiple_of(last * (sites - FAR), 128), FAR)
        close = pl.ds(pl.multiple_of(last * (sites - HALO), 128), HALO)
        copies += [
            pltpu.make_async_copy(source, target, done.at[3 * i + j])
            for j, (source, target) in enumerate(
                [
                    (neighbours.at[:, close], near.at[i]),
                    (features.at[:, far], out.at[pl.ds(0, share), :]),
                    (cotangent.at[:, close], out.at[pl.ds(share, share), pl.ds(0, HALO)]),
                ]
            )
        ]
    for copy in copies:
        copy.start()
    for i, out in enumerate((to_core, to_line)):
        copies[3 * i].wait()
        kept = (near[i] >= 0).astype(F32)
        kept = jnp.concatenate([kept, jnp.zeros((32 - TAPS, HALO), F32)], axis=0)
        out[share : share + 32, HALO:] = kept.astype(BF16)
        copies[3 * i + 1].wait()
        copies[3 * i + 2].wait()


def ends_body(brick, chan, rep, core, line, before, behind, both):
    share = both.shape[0]

    def fill(first, second):
        before[...] = first[...]
        behind[...] = second[...]
        both[:, :NEAR] = first[:share, FAR - NEAR :]
        both[:, NEAR:] = second[:share, :NEAR]

    pl.when(rep[0] == 0)(functools.partial(fill, line, core))
    pl.when(rep[0] != 0)(functools.partial(fill, core, line))


def expand(kept, valid, first):
    for tap in range(TAPS):
        row = jnp.broadcast_to(kept[tap : tap + 1, :], (ROWS, kept.shape[1]))
        lay(valid.at[tap], first, row.astype(BF16))


def prepare_body(
    brick, chan, rep, by_out, features, neighbours, own, rest, by_in, shifts, valid, flat, kept, taken, staged, near, done
):
    total = by_out.shape[2]
    share, sites = features.shape
    turn = lax.rem(total - chan[0] * share, total)
    copies = [
        pltpu.make_async_copy(source, target, done.at[i])
        for i, (source, target) in enumerate(
            [
                (by_out, taken),
                (features, staged),
                (neighbours, near),
            ]
        )
    ]
    for copy in copies:
        copy.start()
    copies[0].wait()
    flat[...] = jnp.zeros_like(flat)
    for group in groups():
        taps = []
        for tap in group:
            ring = pltpu.roll(taken[tap].astype(F32), turn, 1)
            flat[tap * share : (tap + 1) * share, :] = ring.astype(BF16)
            taps.append(ring)
        first, last = group[0], group[-1] + 1
        own[:, first * share : last * share] = jnp.concatenate(
            [x[:, :share] for x in taps], axis=1
        ).astype(BF16)
        left = total - share
        rest[:, first * left : last * left] = jnp.concatenate(
            [x[:, share:] for x in taps], axis=1
        ).astype(BF16)
    by_in[...] = flat[...].T
    copies[1].wait()
    lay(shifts.at[4], FAR // LANES, staged[...])
    shift(shifts, FAR // LANES + 1, (FAR + sites) // LANES - 1)
    copies[2].wait()
    kept[...] = (near[...] >= 0).astype(F32)
    expand(kept, valid, HALO // LANES)


def own_body(left, right, weights, shifts_in, valid_in, begun, shifts, valid, kept):
    del shifts_in, valid_in
    share = begun.shape[0]
    edge = FAR // LANES
    far = shifts.shape[1] - edge
    for side, at, start in ((left, 0, 1), (right, 1, far - 1)):
        lay(shifts.at[4], at * far, side[:share, :])
        shift(shifts, start, start + edge)
        kept[...] = side[share : share + 32, HALO:].astype(F32)
        expand(kept, valid, at * (valid.shape[1] - HALO // LANES))

    def block(j, carry):
        begun[:, pl.ds(pl.multiple_of(j * WIDTH, LANES), WIDTH)] = product(
            weights, shifts, valid, j * TILES + HALO // LANES, j * TILES, lambda tap: tap
        )
        return carry

    lax.fori_loop(0, begun.shape[1] // WIDTH, block, 0)


def arrive_body(rest, own_in, shifts, across, own):
    del own_in
    sites = rest.shape[1]
    edge = FAR // LANES
    lay(shifts.at[4], edge, rest[...])
    shift(shifts, edge + 1, edge + sites // LANES - 1)

    def block(j, carry):
        at = j * TILES + edge
        across[pl.ds(pl.multiple_of(j * WIDTH, LANES), WIDTH), :] = jnp.concatenate(
            [wide(own.at[4], at, TILES), wide(shifts.at[4], at, TILES)], axis=0
        ).T
        return carry

    lax.fori_loop(0, sites // WIDTH, block, 0)


def rest_body(
    ends,
    shifts_in,
    weights,
    valid_in,
    begun,
    left,
    right,
    own,
    cotangent,
    output,
    grads,
    valid,
    shifts,
    grad,
    kept,
    hidden,
):
    del shifts_in, valid_in
    share, sites = cotangent.shape
    edge, near, halo, lead = (n // LANES for n in (FAR, NEAR, HALO, LEAD + LANES))
    far = shifts.shape[1] - edge
    lay(shifts.at[4], 0, jnp.zeros((shifts.shape[2], FAR - NEAR), BF16))
    lay(shifts.at[4], edge - near, ends[:, :NEAR])
    lay(shifts.at[4], far, ends[:, NEAR:])
    lay(shifts.at[4], far + near, jnp.zeros((shifts.shape[2], FAR - NEAR), BF16))
    shift(shifts, 1, 1 + edge)
    shift(shifts, far - 1, far - 1 + edge)
    lay(grad, lead, left[share : 2 * share, :HALO])
    lay(grad, lead + halo, cotangent[...])
    lay(grad, lead + halo + sites // LANES, right[share : 2 * share, :HALO])

    def finish(before, start, at):
        rows = pl.ds(at, ROWS)
        value = hidden[before, rows, :]
        sigma = 0.5 * jnp.tanh(0.5 * value) + 0.5
        features = wide(own.at[4], jnp.maximum(start - TILES, 0) + halo, TILES, rows)
        kept[rows, pl.ds(pl.multiple_of(start * LANES, LANES), WIDTH)] = (
            features.astype(F32) + value * sigma
        ).astype(BF16)
        there = start - TILES + lead
        ready = (
            wide(grad, there, TILES, rows).astype(F32) * sigma * (1.0 + value * (1.0 - sigma))
        ).astype(BF16)
        lay(grad, there, ready, rows)
        spread(wide(grad, start, TILES + 2, rows), grads, rows, start)

    def finishes(before, start):
        return [functools.partial(finish, before, start, at) for at in range(0, share, ROWS)]

    def block(j, carry):
        start = j * TILES
        here = pl.ds(pl.multiple_of(j * WIDTH, LANES), WIDTH)
        hidden[j % 2] = begun[:, here] + product(
            weights,
            shifts,
            valid,
            start + halo,
            start,
            lambda tap: tap,
            [lambda: None, *finishes((j + 1) % 2, start)],
        )
        return carry

    count = begun.shape[1] // WIDTH
    lax.fori_loop(0, count, block, 0)
    for piece in finishes((count + 1) % 2, count * TILES):
        piece()
    output[...] = kept[:, WIDTH + HALO : WIDTH + HALO + sites]


def weight_body(half, brick, chan, rep, across, valid_in, grads_in, kept, sent, valid, grads, total):
    del valid_in, grads_in
    share, sites = grads.shape[2], across.shape[0]
    halo, lead = HALO // LANES, LEAD // LANES
    total[...] = jnp.zeros_like(total)

    def block(j, carry):
        start = j * TILES + halo
        features = across[pl.ds(pl.multiple_of(j * WIDTH, LANES), WIDTH), :]
        for group in groups(MANY):
            rows = []
            for tap in group:
                rows += masked(grads, valid, TAPS - 1 - tap, start + lead, start)
            total[group[0] * share : (group[-1] + 1) * share, :] += jnp.dot(
                jnp.concatenate(rows, axis=0), features, preferred_element_type=F32
            )
        return carry

    lax.fori_loop(0, sites // WIDTH, block, 0)
    mine = rep[0]
    kept[...] = total[pl.ds(pl.multiple_of(mine * half, ROWS), half), :]
    sent[...] = total[pl.ds(pl.multiple_of((1 - mine) * half, ROWS), half), :].astype(BF16)


def feature_body(part, weights, valid, grads, *refs):
    own, rest = refs[-2:]
    share, sites = own.shape
    blocks = sites // 2 // WIDTH

    def block(j, carry):
        at = part * blocks + j
        here = pl.ds(pl.multiple_of(at * WIDTH, LANES), WIDTH)
        start = at * TILES + HALO // LANES
        total = product(
            weights, grads, valid, start + LEAD // LANES, start, lambda tap: TAPS - 1 - tap
        )
        own[:, here] = total[:share]
        rest[:, here] = total[share:].astype(BF16)
        return carry

    lax.fori_loop(0, blocks, block, 0)


def split_body(brick, chan, rep, kept, arrived, mine, sent):
    size = mine.shape[0]
    at = brick[0] % 2
    mine_rows = pl.ds(pl.multiple_of(at * size, ROWS), size)
    sent_rows = pl.ds(pl.multiple_of((1 - at) * size, ROWS), size)
    mine[...] = kept[mine_rows, :] + arrived[mine_rows, :].astype(F32)
    sent[...] = (kept[sent_rows, :] + arrived[sent_rows, :].astype(F32)).astype(BF16)


def merge_body(mine, other, out):
    out[...] = (mine[...].astype(F32) + other[...].astype(F32)).astype(BF16)


def gather_body(brick, chan, rep, mine, other, side):
    size = mine.shape[0]
    at = brick[0] % 2
    side[pl.ds(pl.multiple_of(at * size, ROWS), size), :] = mine[...]
    side[pl.ds(pl.multiple_of((1 - at) * size, ROWS), size), :] = other[...]


def join_body(half, share, brick, chan, rep, side, other, out, both):
    mine = rep[0]
    both[pl.ds(pl.multiple_of(mine * half, ROWS), half), :] = side[...]
    both[pl.ds(pl.multiple_of((1 - mine) * half, ROWS), half), :] = other[...]
    out[...] = pltpu.roll(both[: out.shape[0], :].astype(F32), chan[0] * share, 1)


def add_body(cotangent, own, *rest):
    *terms, out, token = rest
    token[...] = jnp.zeros_like(token)
    total = cotangent[...].astype(F32) + own[...]
    for term in terms:
        total += term[...].astype(F32)
    out[...] = total.astype(BF16)


def line_swap(x):
    count = lax.axis_size(("brick", "rep"))
    pairs = [p for i in range(1, count - 1, 2) for p in ((i, i + 1), (i + 1, i))]
    return lax.ppermute(x, ("brick", "rep"), pairs)


def local(features, conv_weight, neighbours, cotangent):
    share, sites = features.shape
    total = conv_weight.shape[1]
    left = total - share
    chans, bricks, reps = (lax.axis_size(axis) for axis in ("chan", "brick", "rep"))
    place = [lax.axis_index(axis)[None] for axis in LINE]
    margin = sites + 2 * HALO
    flops = 2 * TAPS * share * sites

    def around(x):
        return [
            lax.ppermute(x, "chan", [((i + over) % chans, i) for i in range(chans)])
            for over in range(1, chans)
        ]

    def stack(parts):
        return parts[0] if len(parts) == 1 else jnp.concatenate(parts, axis=0)

    assert reps == 2
    swap = [(0, 1), (1, 0)]
    rest = stack(around(features))
    to_core, to_line = kernel(
        pack_body,
        "pack",
        [shape((share + max(share, 32), FAR))] * 2,
        [features, cotangent, neighbours],
        scalars=place,
        scratch=[pltpu.VMEM((2, TAPS, HALO), jnp.int32), pltpu.SemaphoreType.DMA((6,))],
        held=True,
    )
    line = line_swap(to_line)
    core = lax.ppermute(to_core, "rep", swap)
    lanes = -(-TAPS * share // 128) * 128
    own_weights, rest_weights, by_in, shifts, valid = kernel(
        prepare_body,
        "prepare",
        [
            shape((share, TAPS * share)),
            shape((share, TAPS * left)),
            shape((total, lanes)),
            shape((9, (sites + 2 * FAR) // LANES, share, LANES)),
            shape((TAPS, margin // LANES, ROWS, LANES)),
        ],
        [jnp.transpose(conv_weight, (0, 2, 1)), features, neighbours],
        scalars=place,
        scratch=[
            pltpu.VMEM((lanes, total), BF16),
            pltpu.VMEM((TAPS, sites), F32),
            pltpu.VMEM((TAPS, share, total), BF16),
            pltpu.VMEM((share, sites), BF16),
            pltpu.VMEM((TAPS, sites), jnp.int32),
            pltpu.SemaphoreType.DMA((3,)),
        ],
        held=True,
    )
    before, behind, both = kernel(
        after(ends_body, 3),
        "ends",
        [shape(core.shape), shape(core.shape), shape((share, 2 * NEAR))],
        [own_weights, core, line],
        scalars=place,
    )
    ends = stack(around(both))
    begun, own_shifts, valid = kernel(
        own_body,
        "forward_own",
        [shape((share, margin), F32), shape(shifts.shape), shape(valid.shape)],
        [before, behind, own_weights, shifts, valid],
        scratch=[pltpu.VMEM((32, HALO), F32)],
        aliases={3: 1, 4: 2},
    )
    rest_shifts, across, own_shifts = kernel(
        arrive_body,
        "arrive",
        [shape((9, (sites + 2 * FAR) // LANES, left, LANES)), shape((sites, total)), shape(own_shifts.shape)],
        [rest, own_shifts],
        aliases={1: 2},
    )
    output, grads, valid, _ = kernel(
        rest_body,
        "forward_rest",
        [
            shape((share, sites)),
            shape((9, (margin + WIDTH) // LANES, share, LANES)),
            shape(valid.shape),
            shape(rest_shifts.shape),
        ],
        [ends, rest_shifts, rest_weights, valid, begun, before, behind, own_shifts, cotangent],
        scratch=[
            pltpu.VMEM(((LEAD + LANES + margin) // LANES, share, LANES), BF16),
            pltpu.VMEM((share, WIDTH + margin), BF16),
            pltpu.VMEM((2, share, WIDTH), F32),
        ],
        aliases={1: 3, 3: 2},
        flops=flops * left,
    )

    piece = -(-TAPS * share // (reps * bricks * ROWS)) * ROWS
    half = piece * bricks
    kept, sent, valid, grads = kernel(
        functools.partial(weight_body, half),
        "grad_weight",
        [shape((half, total), F32), shape((half, total)), shape(valid.shape), shape(grads.shape)],
        [across, valid, grads],
        scalars=place,
        scratch=[pltpu.VMEM((reps * half, total), F32)],
        aliases={1: 2, 2: 3},
        flops=flops * total,
    )
    arrived = lax.ppermute(sent, "rep", swap)

    def feature_part(part, body, args, kept):
        outs = [shape((share, sites), F32), shape((left, sites))]
        return kernel(
            body,
            "grad_features_%d" % part,
            [shape(x.shape) for x in kept] + outs,
            args,
            aliases={len(args) - len(kept) + i: i for i in range(len(kept))}
            if part == 0
            else {len(args) - 2 + i: i for i in range(2)},
            flops=flops * total // 2,
        )

    valid, grads, *parts = feature_part(
        0, functools.partial(feature_body, 0), [by_in, valid, grads], [valid, grads]
    )
    size = half // 2
    mine, sent = kernel(
        after(split_body, 3),
        "split",
        [shape((size, total), F32), shape((size, total))],
        [parts[0], kept, arrived],
        scalars=place,
        flops=LATER,
    )
    pairs = [(i, i ^ 1) for i in range(bricks)]
    arrived = lax.ppermute(sent, "brick", pairs)
    own, other = feature_part(
        1, after(functools.partial(feature_body, 1), 0), [mine, by_in, valid, grads, *parts], []
    )
    terms = [
        lax.ppermute(
            other if left == share else other[(over - 1) * share : over * share],
            "chan",
            [(i, (i + over) % chans) for i in range(chans)],
        )
        for over in range(1, chans)
    ]
    mine = kernel(
        after(merge_body, 0),
        "merge_1",
        shape((size, total)),
        [own, mine, arrived],
        flops=LATER,
    )
    step = 2
    while step < bricks:
        other = lax.ppermute(mine, "brick", [(i, i ^ step) for i in range(bricks)])
        step *= 2
        mine = kernel(
            merge_body, "merge_%d" % step, shape((size, total)), [mine, other], flops=LATER
        )
    other = lax.ppermute(mine, "brick", pairs)
    side = kernel(
        gather_body, "gather", shape((half, total)), [mine, other], scalars=place, flops=LATER
    )
    other = lax.ppermute(side, "rep", swap)
    grad_features, token = kernel(
        add_body,
        "add",
        [shape((share, sites)), shape((8, 128), F32)],
        [cotangent, own, *terms],
    )
    grad_weight = kernel(
        after(functools.partial(join_body, half, share), 3),
        "join",
        shape((TAPS * share, total), F32),
        [token, side, other],
        scalars=place,
        scratch=[pltpu.VMEM((reps * half, total), BF16)],
        flops=LATER,
    )
    grad_weight = jnp.transpose(grad_weight.reshape(TAPS, share, total), (0, 2, 1))
    return output, grad_features, grad_weight


def solution(mesh):
    return jax.shard_map(
        local,
        mesh=mesh,
        in_specs=(
            P("chan", ("scene", "brick", "rep")),
            P(None, None, "chan"),
            P(None, ("scene", "brick", "rep")),
            P("chan", ("scene", "brick", "rep")),
        ),
        out_specs=(
            P("chan", ("scene", "brick", "rep")),
            P("chan", ("scene", "brick", "rep")),
            P("scene", None, "chan"),
        ),
        check_vma=False,
    )
```

```python
import functools

import jax
import jax.numpy as jnp
from jax import lax
from jax.experimental import pallas as pl
from jax.experimental.pallas import tpu as pltpu
from jax.sharding import PartitionSpec as P

EDGE = 16
FACE = EDGE * EDGE
TAPS = 27
HALO = 384
FAR = 2 * HALO
NEAR = 640
LEAD = 896
MANY = 14
DEEP = 18
ROWS = 16
LANES = 128
GROUP = 8
TILES = 6
WIDTH = TILES * LANES
LATER = 25 * 10**7
LINE = ("brick", "chan", "rep")
MIB = 1024 * 1024
F32, BF16 = jnp.float32, jnp.bfloat16

STEPS = [(k // 3 - 1) * EDGE + k % 3 - 1 for k in range(9)]

HERE = pl.BlockSpec(memory_space=pltpu.VMEM)
FAR_OFF = pl.BlockSpec(memory_space=pltpu.HBM)
SCALAR = pl.BlockSpec(memory_space=pltpu.SMEM)


def kernel(body, name, outs, args, scalars=(), scratch=(), aliases={}, limit=8, flops=0, held=False):
    if held:
        args = [pltpu.with_memory_space_constraint(x, pltpu.HBM) for x in args]
    single = not isinstance(outs, (tuple, list))
    return pl.pallas_call(
        body,
        out_shape=outs,
        in_specs=[SCALAR] * len(scalars) + [FAR_OFF if held else HERE] * len(args),
        out_specs=HERE if single else [HERE] * len(outs),
        scratch_shapes=list(scratch),
        input_output_aliases={len(scalars) + i: o for i, o in aliases.items()},
        compiler_params=pltpu.CompilerParams(vmem_limit_bytes=limit * MIB),
        cost_estimate=pl.CostEstimate(flops=flops, bytes_accessed=MIB, transcendentals=0),
        name=name,
    )(*scalars, *args)


def after(body, at):
    def ordered(*refs):
        body(*refs[:at], *refs[at + 1 :])

    return ordered


def shape(dims, kind=BF16):
    return jax.ShapeDtypeStruct(dims, kind)


def wide(ref, first, count, *rows):
    return jnp.concatenate([ref[(first + i, *rows)] for i in range(count)], axis=1)


def lay(ref, first, value, *rows):
    for i in range(value.shape[1] // LANES):
        ref[(first + i, *rows)] = value[:, i * LANES : (i + 1) * LANES]


def spread(window, target, rows, first):
    width = window.shape[1]
    for j, step in enumerate(STEPS):
        moved = pltpu.roll(window, -step % width, 1) if step else window
        lay(target.at[j], first, moved[:, LANES : width - LANES], rows)


def shift(shifts, low, high):
    for at in range(0, shifts.shape[2], ROWS):
        rows = pl.ds(at, ROWS)
        spread(wide(shifts.at[4], low - 1, high - low + 2, rows), shifts, rows, low)


def masked(shifts, valid, tap, at_shift, at_valid, tiles=TILES):
    keep = wide(valid.at[tap], at_valid, tiles)
    begin = at_shift + (tap // 9 - 1) * FACE // LANES
    return [
        wide(shifts.at[tap % 9], begin, tiles, pl.ds(at, ROWS)) * keep
        for at in range(0, shifts.shape[2], ROWS)
    ]


def groups(count=GROUP):
    return [range(first, min(first + count, TAPS)) for first in range(0, TAPS, count)]


def product(
    weights, shifts, valid, at_shift, at_valid, taps_of, between=(), count=GROUP
):
    channels = shifts.shape[2]
    total = None
    for at, group in enumerate(groups(count)):
        for piece in between[at :: len(groups(count))]:
            piece()
        rows = []
        for tap in group:
            rows += masked(shifts, valid, taps_of(tap), at_shift, at_valid)
        part = jnp.dot(
            weights[:, group[0] * channels : (group[-1] + 1) * channels],
            jnp.concatenate(rows, axis=0),
            preferred_element_type=F32,
        )
        total = part if total is None else total + part
    return total


def pack_body(brick, chan, rep, features, cotangent, neighbours, to_core, to_line, near, done):
    share, sites = features.shape
    copies = []
    for i, (out, last) in enumerate(((to_core, 1 - rep[0]), (to_line, rep[0]))):
        far = pl.ds(pl.multiple_of(last * (sites - FAR), 128), FAR)
        close = pl.ds(pl.multiple_of(last * (sites - HALO), 128), HALO)
        copies += [
            pltpu.make_async_copy(source, target, done.at[3 * i + j])
            for j, (source, target) in enumerate(
                [
                    (neighbours.at[:, close], near.at[i]),
                    (features.at[:, far], out.at[pl.ds(0, share), :]),
                    (cotangent.at[:, close], out.at[pl.ds(share, share), pl.ds(0, HALO)]),
                ]
            )
        ]
    for copy in copies:
        copy.start()
    for i, out in enumerate((to_core, to_line)):
        copies[3 * i].wait()
        kept = (near[i] >= 0).astype(F32)
        kept = jnp.concatenate([kept, jnp.zeros((32 - TAPS, HALO), F32)], axis=0)
        out[share : share + 32, HALO:] = kept.astype(BF16)
        copies[3 * i + 1].wait()
        copies[3 * i + 2].wait()


def ends_body(brick, chan, rep, core, line, before, behind, both):
    share = both.shape[0]

    def fill(first, second):
        before[...] = first[...]
        behind[...] = second[...]
        both[:, :NEAR] = first[:share, FAR - NEAR :]
        both[:, NEAR:] = second[:share, :NEAR]

    pl.when(rep[0] == 0)(functools.partial(fill, line, core))
    pl.when(rep[0] != 0)(functools.partial(fill, core, line))


def expand(kept, valid, first):
    for tap in range(TAPS):
        row = jnp.broadcast_to(kept[tap : tap + 1, :], (ROWS, kept.shape[1]))
        lay(valid.at[tap], first, row.astype(BF16))


def prepare_body(
    brick, chan, rep, by_out, features, neighbours, own, rest, by_in, shifts, valid, flat, kept, taken, staged, near, done
):
    total = by_out.shape[2]
    share, sites = features.shape
    turn = lax.rem(total - chan[0] * share, total)
    copies = [
        pltpu.make_async_copy(source, target, done.at[i])
        for i, (source, target) in enumerate(
            [
                (by_out, taken),
                (features, staged),
                (neighbours, near),
            ]
        )
    ]
    for copy in copies:
        copy.start()
    copies[0].wait()
    flat[...] = jnp.zeros_like(flat)
    for group in groups():
        taps = []
        for tap in group:
            ring = pltpu.roll(taken[tap].astype(F32), turn, 1)
            flat[tap * share : (tap + 1) * share, :] = ring.astype(BF16)
            taps.append(ring)
        first, last = group[0], group[-1] + 1
        own[:, first * share : last * share] = jnp.concatenate(
            [x[:, :share] for x in taps], axis=1
        ).astype(BF16)
        left = total - share
        rest[:, first * left : last * left] = jnp.concatenate(
            [x[:, share:] for x in taps], axis=1
        ).astype(BF16)
    by_in[...] = flat[...].T
    copies[1].wait()
    lay(shifts.at[4], FAR // LANES, staged[...])
    shift(shifts, FAR // LANES + 1, (FAR + sites) // LANES - 1)
    copies[2].wait()
    kept[...] = (near[...] >= 0).astype(F32)
    expand(kept, valid, HALO // LANES)


def own_body(left, right, weights, shifts_in, valid_in, begun, shifts, valid, kept):
    del shifts_in, valid_in
    share = begun.shape[0]
    edge = FAR // LANES
    far = shifts.shape[1] - edge
    for side, at, start in ((left, 0, 1), (right, 1, far - 1)):
        lay(shifts.at[4], at * far, side[:share, :])
        shift(shifts, start, start + edge)
        kept[...] = side[share : share + 32, HALO:].astype(F32)
        expand(kept, valid, at * (valid.shape[1] - HALO // LANES))

    def block(j, carry):
        begun[:, pl.ds(pl.multiple_of(j * WIDTH, LANES), WIDTH)] = product(
            weights, shifts, valid, j * TILES + HALO // LANES, j * TILES, lambda tap: tap
        )
        return carry

    lax.fori_loop(0, begun.shape[1] // WIDTH, block, 0)


def arrive_body(rest, own_in, shifts, across, own):
    del own_in
    sites = rest.shape[1]
    edge = FAR // LANES
    lay(shifts.at[4], edge, rest[...])
    shift(shifts, edge + 1, edge + sites // LANES - 1)

    def block(j, carry):
        at = j * TILES + edge
        across[pl.ds(pl.multiple_of(j * WIDTH, LANES), WIDTH), :] = jnp.concatenate(
            [wide(own.at[4], at, TILES), wide(shifts.at[4], at, TILES)], axis=0
        ).T
        return carry

    lax.fori_loop(0, sites // WIDTH, block, 0)


def rest_body(
    ends,
    shifts_in,
    weights,
    valid_in,
    begun,
    left,
    right,
    own,
    cotangent,
    output,
    grads,
    valid,
    shifts,
    grad,
    kept,
    hidden,
):
    del shifts_in, valid_in
    share, sites = cotangent.shape
    edge, near, halo, lead = (n // LANES for n in (FAR, NEAR, HALO, LEAD + LANES))
    far = shifts.shape[1] - edge
    lay(shifts.at[4], 0, jnp.zeros((shifts.shape[2], FAR - NEAR), BF16))
    lay(shifts.at[4], edge - near, ends[:, :NEAR])
    lay(shifts.at[4], far, ends[:, NEAR:])
    lay(shifts.at[4], far + near, jnp.zeros((shifts.shape[2], FAR - NEAR), BF16))
    shift(shifts, 1, 1 + edge)
    shift(shifts, far - 1, far - 1 + edge)
    lay(grad, lead, left[share : 2 * share, :HALO])
    lay(grad, lead + halo, cotangent[...])
    lay(grad, lead + halo + sites // LANES, right[share : 2 * share, :HALO])

    def finish(before, start, at):
        rows = pl.ds(at, ROWS)
        value = hidden[before, rows, :]
        sigma = 0.5 * jnp.tanh(0.5 * value) + 0.5
        features = wide(own.at[4], jnp.maximum(start - TILES, 0) + halo, TILES, rows)
        kept[rows, pl.ds(pl.multiple_of(start * LANES, LANES), WIDTH)] = (
            features.astype(F32) + value * sigma
        ).astype(BF16)
        there = start - TILES + lead
        ready = (
            wide(grad, there, TILES, rows).astype(F32) * sigma * (1.0 + value * (1.0 - sigma))
        ).astype(BF16)
        lay(grad, there, ready, rows)
        spread(wide(grad, start, TILES + 2, rows), grads, rows, start)

    def finishes(before, start):
        return [functools.partial(finish, before, start, at) for at in range(0, share, ROWS)]

    def block(j, carry):
        start = j * TILES
        here = pl.ds(pl.multiple_of(j * WIDTH, LANES), WIDTH)
        hidden[j % 2] = begun[:, here] + product(
            weights,
            shifts,
            valid,
            start + halo,
            start,
            lambda tap: tap,
            finishes((j + 1) % 2, start),
        )
        return carry

    count = begun.shape[1] // WIDTH
    lax.fori_loop(0, count, block, 0)
    for piece in finishes((count + 1) % 2, count * TILES):
        piece()
    output[...] = kept[:, WIDTH + HALO : WIDTH + HALO + sites]


def weight_body(half, brick, chan, rep, across, valid_in, grads_in, kept, sent, valid, grads, total):
    del valid_in, grads_in
    share, sites = grads.shape[2], across.shape[0]
    halo, lead = HALO // LANES, LEAD // LANES
    total[...] = jnp.zeros_like(total)

    def block(j, carry):
        start = j * DEEP + halo
        here = pl.ds(pl.multiple_of(j * DEEP * LANES, LANES), DEEP * LANES)
        features = across[here, :]
        for group in groups(MANY):
            rows = []
            for tap in group:
                rows += masked(grads, valid, TAPS - 1 - tap, start + lead, start, DEEP)
            total[group[0] * share : (group[-1] + 1) * share, :] += jnp.dot(
                jnp.concatenate(rows, axis=0), features, preferred_element_type=F32
            )
        return carry

    lax.fori_loop(0, sites // (DEEP * LANES), block, 0)
    mine = rep[0]
    kept[...] = total[pl.ds(pl.multiple_of(mine * half, ROWS), half), :]
    sent[...] = total[pl.ds(pl.multiple_of((1 - mine) * half, ROWS), half), :].astype(BF16)


def feature_body(part, weights, valid, grads, *refs):
    own, rest = refs[-2:]
    share, sites = own.shape
    blocks = sites // 2 // WIDTH

    def block(j, carry):
        at = part * blocks + j
        here = pl.ds(pl.multiple_of(at * WIDTH, LANES), WIDTH)
        start = at * TILES + HALO // LANES
        total = product(
            weights,
            grads,
            valid,
            start + LEAD // LANES,
            start,
            lambda tap: TAPS - 1 - tap,
            count=TAPS if part else GROUP,
        )
        own[:, here] = total[:share]
        rest[:, here] = total[share:].astype(BF16)
        return carry

    lax.fori_loop(0, blocks, block, 0)


def split_body(brick, chan, rep, kept, arrived, mine, sent):
    size = mine.shape[0]
    at = brick[0] % 2
    mine_rows = pl.ds(pl.multiple_of(at * size, ROWS), size)
    sent_rows = pl.ds(pl.multiple_of((1 - at) * size, ROWS), size)
    mine[...] = kept[mine_rows, :] + arrived[mine_rows, :].astype(F32)
    sent[...] = (kept[sent_rows, :] + arrived[sent_rows, :].astype(F32)).astype(BF16)


def merge_body(mine, other, out):
    out[...] = (mine[...].astype(F32) + other[...].astype(F32)).astype(BF16)


def gather_body(brick, chan, rep, mine, other, side):
    size = mine.shape[0]
    at = brick[0] % 2
    side[pl.ds(pl.multiple_of(at * size, ROWS), size), :] = mine[...]
    side[pl.ds(pl.multiple_of((1 - at) * size, ROWS), size), :] = other[...]


def join_body(half, share, brick, chan, rep, side, other, out, both):
    mine = rep[0]
    both[pl.ds(pl.multiple_of(mine * half, ROWS), half), :] = side[...]
    both[pl.ds(pl.multiple_of((1 - mine) * half, ROWS), half), :] = other[...]
    out[...] = pltpu.roll(both[: out.shape[0], :].astype(F32), chan[0] * share, 1)


def add_body(cotangent, own, *rest):
    *terms, out, token = rest
    token[...] = jnp.zeros_like(token)
    total = cotangent[...].astype(F32) + own[...]
    for term in terms:
        total += term[...].astype(F32)
    out[...] = total.astype(BF16)


def line_swap(x):
    count = lax.axis_size(("brick", "rep"))
    pairs = [p for i in range(1, count - 1, 2) for p in ((i, i + 1), (i + 1, i))]
    return lax.ppermute(x, ("brick", "rep"), pairs)


def local(features, conv_weight, neighbours, cotangent):
    share, sites = features.shape
    total = conv_weight.shape[1]
    left = total - share
    chans, bricks, reps = (lax.axis_size(axis) for axis in ("chan", "brick", "rep"))
    place = [lax.axis_index(axis)[None] for axis in LINE]
    margin = sites + 2 * HALO
    flops = 2 * TAPS * share * sites

    def around(x):
        return [
            lax.ppermute(x, "chan", [((i + over) % chans, i) for i in range(chans)])
            for over in range(1, chans)
        ]

    def stack(parts):
        return parts[0] if len(parts) == 1 else jnp.concatenate(parts, axis=0)

    assert reps == 2
    swap = [(0, 1), (1, 0)]
    rest = stack(around(features))
    to_core, to_line = kernel(
        pack_body,
        "pack",
        [shape((share + max(share, 32), FAR))] * 2,
        [features, cotangent, neighbours],
        scalars=place,
        scratch=[pltpu.VMEM((2, TAPS, HALO), jnp.int32), pltpu.SemaphoreType.DMA((6,))],
        held=True,
    )
    line = line_swap(to_line)
    core = lax.ppermute(to_core, "rep", swap)
    lanes = -(-TAPS * share // 128) * 128
    own_weights, rest_weights, by_in, shifts, valid = kernel(
        prepare_body,
        "prepare",
        [
            shape((share, TAPS * share)),
            shape((share, TAPS * left)),
            shape((total, lanes)),
            shape((9, (sites + 2 * FAR) // LANES, share, LANES)),
            shape((TAPS, margin // LANES, ROWS, LANES)),
        ],
        [jnp.transpose(conv_weight, (0, 2, 1)), features, neighbours],
        scalars=place,
        scratch=[
            pltpu.VMEM((lanes, total), BF16),
            pltpu.VMEM((TAPS, sites), F32),
            pltpu.VMEM((TAPS, share, total), BF16),
            pltpu.VMEM((share, sites), BF16),
            pltpu.VMEM((TAPS, sites), jnp.int32),
            pltpu.SemaphoreType.DMA((3,)),
        ],
        held=True,
    )
    before, behind, both = kernel(
        after(ends_body, 3),
        "ends",
        [shape(core.shape), shape(core.shape), shape((share, 2 * NEAR))],
        [own_weights, core, line],
        scalars=place,
    )
    ends = stack(around(both))
    begun, own_shifts, valid = kernel(
        own_body,
        "forward_own",
        [shape((share, margin), F32), shape(shifts.shape), shape(valid.shape)],
        [before, behind, own_weights, shifts, valid],
        scratch=[pltpu.VMEM((32, HALO), F32)],
        aliases={3: 1, 4: 2},
    )
    rest_shifts, across, own_shifts = kernel(
        arrive_body,
        "arrive",
        [shape((9, (sites + 2 * FAR) // LANES, left, LANES)), shape((sites, total)), shape(own_shifts.shape)],
        [rest, own_shifts],
        aliases={1: 2},
    )
    output, grads, valid, _ = kernel(
        rest_body,
        "forward_rest",
        [
            shape((share, sites)),
            shape((9, (margin + WIDTH) // LANES, share, LANES)),
            shape(valid.shape),
            shape(rest_shifts.shape),
        ],
        [ends, rest_shifts, rest_weights, valid, begun, before, behind, own_shifts, cotangent],
        scratch=[
            pltpu.VMEM(((LEAD + LANES + margin) // LANES, share, LANES), BF16),
            pltpu.VMEM((share, WIDTH + margin), BF16),
            pltpu.VMEM((2, share, WIDTH), F32),
        ],
        aliases={1: 3, 3: 2},
        flops=flops * left,
    )

    size = -(-TAPS * share // (reps * 2 * ROWS)) * ROWS
    half = 2 * size
    kept, sent, valid, grads = kernel(
        functools.partial(weight_body, half),
        "grad_weight",
        [shape((half, total), F32), shape((half, total)), shape(valid.shape), shape(grads.shape)],
        [across, valid, grads],
        scalars=place,
        scratch=[pltpu.VMEM((reps * half, total), F32)],
        aliases={1: 2, 2: 3},
        flops=flops * total,
    )
    arrived = lax.ppermute(sent, "rep", swap)

    def feature_part(part, body, args, kept):
        outs = [shape((share, sites), F32), shape((left, sites))]
        return kernel(
            body,
            "grad_features_%d" % part,
            [shape(x.shape) for x in kept] + outs,
            args,
            aliases={len(args) - len(kept) + i: i for i in range(len(kept))}
            if part == 0
            else {len(args) - 2 + i: i for i in range(2)},
            flops=flops * total // 2,
        )

    valid, grads, *parts = feature_part(
        0, functools.partial(feature_body, 0), [by_in, valid, grads], [valid, grads]
    )
    mine, sent = kernel(
        after(split_body, 3),
        "split",
        [shape((size, total), F32), shape((size, total))],
        [parts[0], kept, arrived],
        scalars=place,
        flops=LATER,
    )
    pairs = [(i, i ^ 1) for i in range(bricks)]
    arrived = lax.ppermute(sent, "brick", pairs)
    own, other = feature_part(
        1, after(functools.partial(feature_body, 1), 0), [mine, by_in, valid, grads, *parts], []
    )
    terms = [
        lax.ppermute(
            other if left == share else other[(over - 1) * share : over * share],
            "chan",
            [(i, (i + over) % chans) for i in range(chans)],
        )
        for over in range(1, chans)
    ]
    mine = kernel(
        after(merge_body, 0),
        "merge_1",
        shape((size, total)),
        [own, mine, arrived],
        flops=LATER,
    )
    step = 2
    while step < bricks:
        other = lax.ppermute(mine, "brick", [(i, i ^ step) for i in range(bricks)])
        step *= 2
        mine = kernel(
            merge_body, "merge_%d" % step, shape((size, total)), [mine, other], flops=LATER
        )
    other = lax.ppermute(mine, "brick", pairs)
    side = kernel(
        gather_body, "gather", shape((half, total)), [mine, other], scalars=place, flops=LATER
    )
    other = lax.ppermute(side, "rep", swap)
    grad_features, token = kernel(
        add_body,
        "add",
        [shape((share, sites)), shape((8, 128), F32)],
        [cotangent, own, *terms],
    )
    grad_weight = kernel(
        after(functools.partial(join_body, half, share), 3),
        "join",
        shape((TAPS * share, total), F32),
        [token, side, other],
        scalars=place,
        scratch=[pltpu.VMEM((reps * half, total), BF16)],
        flops=LATER,
    )
    grad_weight = jnp.transpose(grad_weight.reshape(TAPS, share, total), (0, 2, 1))
    return output, grad_features, grad_weight


def solution(mesh):
    return jax.shard_map(
        local,
        mesh=mesh,
        in_specs=(
            P("chan", ("scene", "brick", "rep")),
            P(None, None, "chan"),
            P(None, ("scene", "brick", "rep")),
            P("chan", ("scene", "brick", "rep")),
        ),
        out_specs=(
            P("chan", ("scene", "brick", "rep")),
            P("chan", ("scene", "brick", "rep")),
            P("scene", None, "chan"),
        ),
        check_vma=False,
    )
```

```python
import functools

import jax
import jax.numpy as jnp
from jax import lax
from jax.experimental import pallas as pl
from jax.experimental.pallas import tpu as pltpu
from jax.sharding import PartitionSpec as P

EDGE = 16
FACE = EDGE * EDGE
TAPS = 27
HALO = 384
FAR = 2 * HALO
NEAR = 640
LEAD = 896
MANY = 27
DEEP = 18
ROWS = 16
LANES = 128
GROUP = 8
TILES = 6
WIDTH = TILES * LANES
LATER = 25 * 10**7
LINE = ("brick", "chan", "rep")
MIB = 1024 * 1024
F32, BF16 = jnp.float32, jnp.bfloat16

STEPS = [(k // 3 - 1) * EDGE + k % 3 - 1 for k in range(9)]

HERE = pl.BlockSpec(memory_space=pltpu.VMEM)
FAR_OFF = pl.BlockSpec(memory_space=pltpu.HBM)
SCALAR = pl.BlockSpec(memory_space=pltpu.SMEM)


def kernel(body, name, outs, args, scalars=(), scratch=(), aliases={}, limit=8, flops=0, held=False):
    if held:
        args = [pltpu.with_memory_space_constraint(x, pltpu.HBM) for x in args]
    single = not isinstance(outs, (tuple, list))
    return pl.pallas_call(
        body,
        out_shape=outs,
        in_specs=[SCALAR] * len(scalars) + [FAR_OFF if held else HERE] * len(args),
        out_specs=HERE if single else [HERE] * len(outs),
        scratch_shapes=list(scratch),
        input_output_aliases={len(scalars) + i: o for i, o in aliases.items()},
        compiler_params=pltpu.CompilerParams(vmem_limit_bytes=limit * MIB),
        cost_estimate=pl.CostEstimate(flops=flops, bytes_accessed=MIB, transcendentals=0),
        name=name,
    )(*scalars, *args)


def after(body, at):
    def ordered(*refs):
        body(*refs[:at], *refs[at + 1 :])

    return ordered


def shape(dims, kind=BF16):
    return jax.ShapeDtypeStruct(dims, kind)


def wide(ref, first, count, *rows):
    return jnp.concatenate([ref[(first + i, *rows)] for i in range(count)], axis=1)


def lay(ref, first, value, *rows):
    for i in range(value.shape[1] // LANES):
        ref[(first + i, *rows)] = value[:, i * LANES : (i + 1) * LANES]


def spread(window, target, rows, first):
    width = window.shape[1]
    for j, step in enumerate(STEPS):
        moved = pltpu.roll(window, -step % width, 1) if step else window
        lay(target.at[j], first, moved[:, LANES : width - LANES], rows)


def shift(shifts, low, high):
    for at in range(0, shifts.shape[2], ROWS):
        rows = pl.ds(at, ROWS)
        spread(wide(shifts.at[4], low - 1, high - low + 2, rows), shifts, rows, low)


def masked(shifts, valid, tap, at_shift, at_valid, tiles=TILES):
    keep = wide(valid.at[tap], at_valid, tiles)
    begin = at_shift + (tap // 9 - 1) * FACE // LANES
    return [
        wide(shifts.at[tap % 9], begin, tiles, pl.ds(at, ROWS)) * keep
        for at in range(0, shifts.shape[2], ROWS)
    ]


def groups(count=GROUP):
    return [range(first, min(first + count, TAPS)) for first in range(0, TAPS, count)]


def product(
    weights, shifts, valid, at_shift, at_valid, taps_of, between=(), count=GROUP
):
    channels = shifts.shape[2]
    total = None
    for at, group in enumerate(groups(count)):
        for piece in between[at :: len(groups(count))]:
            piece()
        rows = []
        for tap in group:
            rows += masked(shifts, valid, taps_of(tap), at_shift, at_valid)
        part = jnp.dot(
            weights[:, group[0] * channels : (group[-1] + 1) * channels],
            jnp.concatenate(rows, axis=0),
            preferred_element_type=F32,
        )
        total = part if total is None else total + part
    return total


def pack_body(brick, chan, rep, features, cotangent, neighbours, to_core, to_line, near, done):
    share, sites = features.shape
    copies = []
    for i, (out, last) in enumerate(((to_core, 1 - rep[0]), (to_line, rep[0]))):
        far = pl.ds(pl.multiple_of(last * (sites - FAR), 128), FAR)
        close = pl.ds(pl.multiple_of(last * (sites - HALO), 128), HALO)
        copies += [
            pltpu.make_async_copy(source, target, done.at[3 * i + j])
            for j, (source, target) in enumerate(
                [
                    (neighbours.at[:, close], near.at[i]),
                    (features.at[:, far], out.at[pl.ds(0, share), :]),
                    (cotangent.at[:, close], out.at[pl.ds(share, share), pl.ds(0, HALO)]),
                ]
            )
        ]
    for copy in copies:
        copy.start()
    for i, out in enumerate((to_core, to_line)):
        copies[3 * i].wait()
        kept = (near[i] >= 0).astype(F32)
        kept = jnp.concatenate([kept, jnp.zeros((32 - TAPS, HALO), F32)], axis=0)
        out[share : share + 32, HALO:] = kept.astype(BF16)
        copies[3 * i + 1].wait()
        copies[3 * i + 2].wait()


def ends_body(brick, chan, rep, core, line, before, behind, both):
    share = both.shape[0]

    def fill(first, second):
        before[...] = first[...]
        behind[...] = second[...]
        both[:, :NEAR] = first[:share, FAR - NEAR :]
        both[:, NEAR:] = second[:share, :NEAR]

    pl.when(rep[0] == 0)(functools.partial(fill, line, core))
    pl.when(rep[0] != 0)(functools.partial(fill, core, line))


def expand(kept, valid, first):
    for tap in range(TAPS):
        row = jnp.broadcast_to(kept[tap : tap + 1, :], (ROWS, kept.shape[1]))
        lay(valid.at[tap], first, row.astype(BF16))


def prepare_body(
    brick, chan, rep, by_out, features, neighbours, own, rest, by_in, shifts, valid, flat, kept, taken, staged, near, done
):
    total = by_out.shape[2]
    share, sites = features.shape
    turn = lax.rem(total - chan[0] * share, total)
    copies = [
        pltpu.make_async_copy(source, target, done.at[i])
        for i, (source, target) in enumerate(
            [
                (by_out, taken),
                (features, staged),
                (neighbours, near),
            ]
        )
    ]
    for copy in copies:
        copy.start()
    copies[0].wait()
    flat[...] = jnp.zeros_like(flat)
    for group in groups():
        taps = []
        for tap in group:
            ring = pltpu.roll(taken[tap].astype(F32), turn, 1)
            flat[tap * share : (tap + 1) * share, :] = ring.astype(BF16)
            taps.append(ring)
        first, last = group[0], group[-1] + 1
        own[:, first * share : last * share] = jnp.concatenate(
            [x[:, :share] for x in taps], axis=1
        ).astype(BF16)
        left = total - share
        rest[:, first * left : last * left] = jnp.concatenate(
            [x[:, share:] for x in taps], axis=1
        ).astype(BF16)
    by_in[...] = flat[...].T
    copies[1].wait()
    lay(shifts.at[4], FAR // LANES, staged[...])
    shift(shifts, FAR // LANES + 1, (FAR + sites) // LANES - 1)
    copies[2].wait()
    kept[...] = (near[...] >= 0).astype(F32)
    expand(kept, valid, HALO // LANES)


def turn_over(shifts, across, column):
    channels = shifts.shape[2]

    def block(j, carry):
        rows = pl.ds(pl.multiple_of(j * WIDTH, LANES), WIDTH)
        across[rows, column : column + channels] = wide(
            shifts.at[4], j * TILES + FAR // LANES, TILES
        ).T
        return carry

    lax.fori_loop(0, across.shape[0] // WIDTH, block, 0)


def own_body(left, right, weights, shifts_in, valid_in, begun, shifts, valid, across, kept):
    del shifts_in, valid_in
    share = begun.shape[0]
    edge = FAR // LANES
    far = shifts.shape[1] - edge
    for side, at, start in ((left, 0, 1), (right, 1, far - 1)):
        lay(shifts.at[4], at * far, side[:share, :])
        shift(shifts, start, start + edge)
        kept[...] = side[share : share + 32, HALO:].astype(F32)
        expand(kept, valid, at * (valid.shape[1] - HALO // LANES))

    def block(j, carry):
        begun[:, pl.ds(pl.multiple_of(j * WIDTH, LANES), WIDTH)] = product(
            weights, shifts, valid, j * TILES + HALO // LANES, j * TILES, lambda tap: tap
        )
        return carry

    lax.fori_loop(0, begun.shape[1] // WIDTH, block, 0)
    turn_over(shifts, across, across.shape[1] - share)


def arrive_body(rest, across_in, shifts, across):
    del across_in
    sites = rest.shape[1]
    edge = FAR // LANES
    lay(shifts.at[4], edge, rest[...])
    shift(shifts, edge + 1, edge + sites // LANES - 1)
    turn_over(shifts, across, 0)


def rest_body(
    ends,
    shifts_in,
    weights,
    valid_in,
    begun,
    left,
    right,
    own,
    cotangent,
    kept,
    grads,
    valid,
    shifts,
    grad,
    hidden,
):
    del shifts_in, valid_in
    share, sites = cotangent.shape
    edge, near, halo, lead = (n // LANES for n in (FAR, NEAR, HALO, LEAD + LANES))
    far = shifts.shape[1] - edge
    lay(shifts.at[4], 0, jnp.zeros((shifts.shape[2], FAR - NEAR), BF16))
    lay(shifts.at[4], edge - near, ends[:, :NEAR])
    lay(shifts.at[4], far, ends[:, NEAR:])
    lay(shifts.at[4], far + near, jnp.zeros((shifts.shape[2], FAR - NEAR), BF16))
    shift(shifts, 1, 1 + edge)
    shift(shifts, far - 1, far - 1 + edge)
    lay(grad, lead, left[share : 2 * share, :HALO])
    lay(grad, lead + halo, cotangent[...])
    lay(grad, lead + halo + sites // LANES, right[share : 2 * share, :HALO])

    def finish(before, start, at):
        rows = pl.ds(at, ROWS)
        value = hidden[before, rows, :]
        sigma = 0.5 * jnp.tanh(0.5 * value) + 0.5
        features = wide(own.at[4], jnp.maximum(start - TILES, 0) + halo, TILES, rows)
        kept[rows, pl.ds(pl.multiple_of(start * LANES, LANES), WIDTH)] = (
            features.astype(F32) + value * sigma
        ).astype(BF16)
        there = start - TILES + lead
        ready = (
            wide(grad, there, TILES, rows).astype(F32) * sigma * (1.0 + value * (1.0 - sigma))
        ).astype(BF16)
        lay(grad, there, ready, rows)
        spread(wide(grad, start, TILES + 2, rows), grads, rows, start)

    def finishes(before, start):
        return [functools.partial(finish, before, start, at) for at in range(0, share, ROWS)]

    def block(j, carry):
        start = j * TILES
        here = pl.ds(pl.multiple_of(j * WIDTH, LANES), WIDTH)
        hidden[j % 2] = begun[:, here] + product(
            weights,
            shifts,
            valid,
            start + halo,
            start,
            lambda tap: tap,
            finishes((j + 1) % 2, start),
        )
        return carry

    count = begun.shape[1] // WIDTH
    lax.fori_loop(0, count, block, 0)
    for piece in finishes((count + 1) % 2, count * TILES):
        piece()


def weight_body(half, brick, chan, rep, across, valid_in, grads_in, kept, sent, valid, grads, total):
    del valid_in, grads_in
    share, sites = grads.shape[2], across.shape[0]
    halo, lead = HALO // LANES, LEAD // LANES
    total[...] = jnp.zeros_like(total)

    def block(j, carry):
        start = j * DEEP + halo
        here = pl.ds(pl.multiple_of(j * DEEP * LANES, LANES), DEEP * LANES)
        features = across[here, :]
        for group in groups(MANY):
            rows = []
            for tap in group:
                rows += masked(grads, valid, TAPS - 1 - tap, start + lead, start, DEEP)
            total[group[0] * share : (group[-1] + 1) * share, :] += jnp.dot(
                jnp.concatenate(rows, axis=0), features, preferred_element_type=F32
            )
        return carry

    lax.fori_loop(0, sites // (DEEP * LANES), block, 0)
    mine = rep[0]
    kept[...] = total[pl.ds(pl.multiple_of(mine * half, ROWS), half), :]
    sent[...] = total[pl.ds(pl.multiple_of((1 - mine) * half, ROWS), half), :].astype(BF16)


def feature_body(part, weights, valid, grads, *refs):
    own, rest = refs[-2:]
    share, sites = own.shape
    blocks = sites // 2 // WIDTH

    def block(j, carry):
        at = part * blocks + j
        here = pl.ds(pl.multiple_of(at * WIDTH, LANES), WIDTH)
        start = at * TILES + HALO // LANES
        total = product(
            weights,
            grads,
            valid,
            start + LEAD // LANES,
            start,
            lambda tap: TAPS - 1 - tap,
            count=TAPS if part else GROUP,
        )
        own[:, here] = total[:share]
        rest[:, here] = total[share:].astype(BF16)
        return carry

    lax.fori_loop(0, blocks, block, 0)


def split_body(brick, chan, rep, kept, arrived, mine, sent):
    size = mine.shape[0]
    at = brick[0] % 2
    mine_rows = pl.ds(pl.multiple_of(at * size, ROWS), size)
    sent_rows = pl.ds(pl.multiple_of((1 - at) * size, ROWS), size)
    mine[...] = kept[mine_rows, :] + arrived[mine_rows, :].astype(F32)
    sent[...] = (kept[sent_rows, :] + arrived[sent_rows, :].astype(F32)).astype(BF16)


def merge_body(mine, other, out):
    out[...] = (mine[...].astype(F32) + other[...].astype(F32)).astype(BF16)


def gather_body(brick, chan, rep, mine, other, side):
    size = mine.shape[0]
    at = brick[0] % 2
    side[pl.ds(pl.multiple_of(at * size, ROWS), size), :] = mine[...]
    side[pl.ds(pl.multiple_of((1 - at) * size, ROWS), size), :] = other[...]


def join_body(half, share, brick, chan, rep, side, other, out, both):
    mine = rep[0]
    turn = lax.rem((chan[0] + 1) * share, out.shape[1])
    both[pl.ds(pl.multiple_of(mine * half, ROWS), half), :] = side[...]
    both[pl.ds(pl.multiple_of((1 - mine) * half, ROWS), half), :] = other[...]
    out[...] = pltpu.roll(both[: out.shape[0], :].astype(F32), turn, 1)


def emit_body(held, out, token):
    token[...] = jnp.zeros_like(token)
    out[...] = held[:, WIDTH + HALO : WIDTH + HALO + out.shape[1]]


def add_body(cotangent, own, *rest):
    *terms, out, token = rest
    token[...] = jnp.zeros_like(token)
    total = cotangent[...].astype(F32) + own[...]
    for term in terms:
        total += term[...].astype(F32)
    out[...] = total.astype(BF16)


def line_swap(x):
    count = lax.axis_size(("brick", "rep"))
    pairs = [p for i in range(1, count - 1, 2) for p in ((i, i + 1), (i + 1, i))]
    return lax.ppermute(x, ("brick", "rep"), pairs)


def local(features, conv_weight, neighbours, cotangent):
    share, sites = features.shape
    total = conv_weight.shape[1]
    left = total - share
    chans, bricks, reps = (lax.axis_size(axis) for axis in ("chan", "brick", "rep"))
    place = [lax.axis_index(axis)[None] for axis in LINE]
    margin = sites + 2 * HALO
    flops = 2 * TAPS * share * sites

    def around(x):
        return [
            lax.ppermute(x, "chan", [((i + over) % chans, i) for i in range(chans)])
            for over in range(1, chans)
        ]

    def stack(parts):
        return parts[0] if len(parts) == 1 else jnp.concatenate(parts, axis=0)

    assert reps == 2
    swap = [(0, 1), (1, 0)]
    rest = stack(around(features))
    to_core, to_line = kernel(
        pack_body,
        "pack",
        [shape((share + max(share, 32), FAR))] * 2,
        [features, cotangent, neighbours],
        scalars=place,
        scratch=[pltpu.VMEM((2, TAPS, HALO), jnp.int32), pltpu.SemaphoreType.DMA((6,))],
        held=True,
    )
    line = line_swap(to_line)
    core = lax.ppermute(to_core, "rep", swap)
    lanes = -(-TAPS * share // 128) * 128
    own_weights, rest_weights, by_in, shifts, valid = kernel(
        prepare_body,
        "prepare",
        [
            shape((share, TAPS * share)),
            shape((share, TAPS * left)),
            shape((total, lanes)),
            shape((9, (sites + 2 * FAR) // LANES, share, LANES)),
            shape((TAPS, margin // LANES, ROWS, LANES)),
        ],
        [jnp.transpose(conv_weight, (0, 2, 1)), features, neighbours],
        scalars=place,
        scratch=[
            pltpu.VMEM((lanes, total), BF16),
            pltpu.VMEM((TAPS, sites), F32),
            pltpu.VMEM((TAPS, share, total), BF16),
            pltpu.VMEM((share, sites), BF16),
            pltpu.VMEM((TAPS, sites), jnp.int32),
            pltpu.SemaphoreType.DMA((3,)),
        ],
        held=True,
    )
    before, behind, both = kernel(
        after(ends_body, 3),
        "ends",
        [shape(core.shape), shape(core.shape), shape((share, 2 * NEAR))],
        [own_weights, core, line],
        scalars=place,
    )
    ends = stack(around(both))
    begun, own_shifts, valid, across = kernel(
        own_body,
        "forward_own",
        [
            shape((share, margin), F32),
            shape(shifts.shape),
            shape(valid.shape),
            shape((sites, total)),
        ],
        [before, behind, own_weights, shifts, valid],
        scratch=[pltpu.VMEM((32, HALO), F32)],
        aliases={3: 1, 4: 2},
    )
    rest_shifts, across = kernel(
        arrive_body,
        "arrive",
        [shape((9, (sites + 2 * FAR) // LANES, left, LANES)), shape(across.shape)],
        [rest, across],
        aliases={1: 1},
    )
    held, grads, valid, _ = kernel(
        rest_body,
        "forward_rest",
        [
            shape((share, WIDTH + margin)),
            shape((9, (margin + WIDTH) // LANES, share, LANES)),
            shape(valid.shape),
            shape(rest_shifts.shape),
        ],
        [ends, rest_shifts, rest_weights, valid, begun, before, behind, own_shifts, cotangent],
        scratch=[
            pltpu.VMEM(((LEAD + LANES + margin) // LANES, share, LANES), BF16),
            pltpu.VMEM((2, share, WIDTH), F32),
        ],
        aliases={1: 3, 3: 2},
        flops=flops * left,
    )

    size = -(-TAPS * share // (reps * 2 * ROWS)) * ROWS
    half = 2 * size
    kept, sent, valid, grads = kernel(
        functools.partial(weight_body, half),
        "grad_weight",
        [shape((half, total), F32), shape((half, total)), shape(valid.shape), shape(grads.shape)],
        [across, valid, grads],
        scalars=place,
        scratch=[pltpu.VMEM((reps * half, total), F32)],
        aliases={1: 2, 2: 3},
        flops=flops * total,
    )
    arrived = lax.ppermute(sent, "rep", swap)

    def feature_part(part, body, args, kept):
        outs = [shape((share, sites), F32), shape((left, sites))]
        return kernel(
            body,
            "grad_features_%d" % part,
            [shape(x.shape) for x in kept] + outs,
            args,
            aliases={len(args) - len(kept) + i: i for i in range(len(kept))}
            if part == 0
            else {len(args) - 2 + i: i for i in range(2)},
            flops=flops * total // 2,
        )

    valid, grads, *parts = feature_part(
        0, functools.partial(feature_body, 0), [by_in, valid, grads], [valid, grads]
    )
    mine, sent = kernel(
        after(split_body, 3),
        "split",
        [shape((size, total), F32), shape((size, total))],
        [parts[0], kept, arrived],
        scalars=place,
        flops=LATER,
    )
    pairs = [(i, i ^ 1) for i in range(bricks)]
    arrived = lax.ppermute(sent, "brick", pairs)
    own, other = feature_part(
        1, after(functools.partial(feature_body, 1), 0), [mine, by_in, valid, grads, *parts], []
    )
    terms = [
        lax.ppermute(
            other if left == share else other[(over - 1) * share : over * share],
            "chan",
            [(i, (i + over) % chans) for i in range(chans)],
        )
        for over in range(1, chans)
    ]
    mine = kernel(
        after(merge_body, 0),
        "merge_1",
        shape((size, total)),
        [own, mine, arrived],
        flops=LATER,
    )
    output, token = kernel(
        after(emit_body, 0),
        "emit",
        [shape((share, sites)), shape((8, LANES), F32)],
        [mine, held],
    )
    step = 2
    while step < bricks:
        other = lax.ppermute(mine, "brick", [(i, i ^ step) for i in range(bricks)])
        step *= 2
        mine = kernel(
            after(merge_body, 0),
            "merge_%d" % step,
            shape((size, total)),
            [token, mine, other],
            flops=LATER,
        )
    other = lax.ppermute(mine, "brick", pairs)
    side = kernel(
        gather_body, "gather", shape((half, total)), [mine, other], scalars=place, flops=LATER
    )
    other = lax.ppermute(side, "rep", swap)
    grad_features, token = kernel(
        add_body,
        "add",
        [shape((share, sites)), shape((8, 128), F32)],
        [cotangent, own, *terms],
    )
    grad_weight = kernel(
        after(functools.partial(join_body, half, share), 3),
        "join",
        shape((TAPS * share, total), F32),
        [token, side, other],
        scalars=place,
        scratch=[pltpu.VMEM((reps * half, total), BF16)],
        flops=LATER,
    )
    grad_weight = jnp.transpose(grad_weight.reshape(TAPS, share, total), (0, 2, 1))
    return output, grad_features, grad_weight


def solution(mesh):
    return jax.shard_map(
        local,
        mesh=mesh,
        in_specs=(
            P("chan", ("scene", "brick", "rep")),
            P(None, None, "chan"),
            P(None, ("scene", "brick", "rep")),
            P("chan", ("scene", "brick", "rep")),
        ),
        out_specs=(
            P("chan", ("scene", "brick", "rep")),
            P("chan", ("scene", "brick", "rep")),
            P("scene", None, "chan"),
        ),
        check_vma=False,
    )
```

```python
import functools

import jax
import jax.numpy as jnp
from jax import lax
from jax.experimental import pallas as pl
from jax.experimental.pallas import tpu as pltpu
from jax.sharding import PartitionSpec as P

EDGE = 16
FACE = EDGE * EDGE
TAPS = 27
HALO = 384
FAR = 2 * HALO
NEAR = 640
LEAD = 896
MANY = 27
DEEP = 18
ROWS = 16
LANES = 128
GROUP = 8
TILES = 6
WIDTH = TILES * LANES
LATER = 12 * 10**8
LINE = ("brick", "chan", "rep")
MIB = 1024 * 1024
F32, BF16 = jnp.float32, jnp.bfloat16

STEPS = [(k // 3 - 1) * EDGE + k % 3 - 1 for k in range(9)]

HERE = pl.BlockSpec(memory_space=pltpu.VMEM)
FAR_OFF = pl.BlockSpec(memory_space=pltpu.HBM)
SCALAR = pl.BlockSpec(memory_space=pltpu.SMEM)


def kernel(body, name, outs, args, scalars=(), scratch=(), aliases={}, limit=8, flops=0, held=False):
    if held:
        args = [pltpu.with_memory_space_constraint(x, pltpu.HBM) for x in args]
    single = not isinstance(outs, (tuple, list))
    return pl.pallas_call(
        body,
        out_shape=outs,
        in_specs=[SCALAR] * len(scalars) + [FAR_OFF if held else HERE] * len(args),
        out_specs=HERE if single else [HERE] * len(outs),
        scratch_shapes=list(scratch),
        input_output_aliases={len(scalars) + i: o for i, o in aliases.items()},
        compiler_params=pltpu.CompilerParams(vmem_limit_bytes=limit * MIB),
        cost_estimate=pl.CostEstimate(flops=flops, bytes_accessed=MIB, transcendentals=0),
        name=name,
    )(*scalars, *args)


def after(body, at):
    def ordered(*refs):
        body(*refs[:at], *refs[at + 1 :])

    return ordered


def shape(dims, kind=BF16):
    return jax.ShapeDtypeStruct(dims, kind)


def wide(ref, first, count, *rows):
    return jnp.concatenate([ref[(first + i, *rows)] for i in range(count)], axis=1)


def lay(ref, first, value, *rows):
    for i in range(value.shape[1] // LANES):
        ref[(first + i, *rows)] = value[:, i * LANES : (i + 1) * LANES]


def spread(window, target, rows, first):
    width = window.shape[1]
    for j, step in enumerate(STEPS):
        moved = pltpu.roll(window, -step % width, 1) if step else window
        lay(target.at[j], first, moved[:, LANES : width - LANES], rows)


def shift(shifts, low, high):
    for at in range(0, shifts.shape[2], ROWS):
        rows = pl.ds(at, ROWS)
        spread(wide(shifts.at[4], low - 1, high - low + 2, rows), shifts, rows, low)


def masked(shifts, valid, tap, at_shift, at_valid, tiles=TILES):
    keep = wide(valid.at[tap], at_valid, tiles)
    begin = at_shift + (tap // 9 - 1) * FACE // LANES
    return [
        wide(shifts.at[tap % 9], begin, tiles, pl.ds(at, ROWS)) * keep
        for at in range(0, shifts.shape[2], ROWS)
    ]


def groups(count=GROUP):
    return [range(first, min(first + count, TAPS)) for first in range(0, TAPS, count)]


def product(
    weights, shifts, valid, at_shift, at_valid, taps_of, between=(), count=GROUP
):
    channels = shifts.shape[2]
    total = None
    for at, group in enumerate(groups(count)):
        for piece in between[at :: len(groups(count))]:
            piece()
        rows = []
        for tap in group:
            rows += masked(shifts, valid, taps_of(tap), at_shift, at_valid)
        part = jnp.dot(
            weights[:, group[0] * channels : (group[-1] + 1) * channels],
            jnp.concatenate(rows, axis=0),
            preferred_element_type=F32,
        )
        total = part if total is None else total + part
    return total


def pack_body(brick, chan, rep, features, cotangent, neighbours, to_core, to_line, near, done):
    share, sites = features.shape
    copies = []
    for i, (out, last) in enumerate(((to_core, 1 - rep[0]), (to_line, rep[0]))):
        far = pl.ds(pl.multiple_of(last * (sites - FAR), 128), FAR)
        close = pl.ds(pl.multiple_of(last * (sites - HALO), 128), HALO)
        copies += [
            pltpu.make_async_copy(source, target, done.at[3 * i + j])
            for j, (source, target) in enumerate(
                [
                    (neighbours.at[:, close], near.at[i]),
                    (features.at[:, far], out.at[pl.ds(0, share), :]),
                    (cotangent.at[:, close], out.at[pl.ds(share, share), pl.ds(0, HALO)]),
                ]
            )
        ]
    for copy in copies:
        copy.start()
    for i, out in enumerate((to_core, to_line)):
        copies[3 * i].wait()
        kept = (near[i] >= 0).astype(F32)
        kept = jnp.concatenate([kept, jnp.zeros((32 - TAPS, HALO), F32)], axis=0)
        out[share : share + 32, HALO:] = kept.astype(BF16)
        copies[3 * i + 1].wait()
        copies[3 * i + 2].wait()


def ends_body(brick, chan, rep, core, line, before, behind, both):
    share = both.shape[0]

    def fill(first, second):
        before[...] = first[...]
        behind[...] = second[...]
        both[:, :NEAR] = first[:share, FAR - NEAR :]
        both[:, NEAR:] = second[:share, :NEAR]

    pl.when(rep[0] == 0)(functools.partial(fill, line, core))
    pl.when(rep[0] != 0)(functools.partial(fill, core, line))


def expand(kept, valid, first):
    for tap in range(TAPS):
        row = jnp.broadcast_to(kept[tap : tap + 1, :], (ROWS, kept.shape[1]))
        lay(valid.at[tap], first, row.astype(BF16))


def prepare_body(
    brick, chan, rep, by_out, features, neighbours, own, rest, by_in, shifts, valid, flat, kept, taken, staged, near, done
):
    total = by_out.shape[2]
    share, sites = features.shape
    turn = lax.rem(total - chan[0] * share, total)
    copies = [
        pltpu.make_async_copy(source, target, done.at[i])
        for i, (source, target) in enumerate(
            [
                (by_out, taken),
                (features, staged),
                (neighbours, near),
            ]
        )
    ]
    for copy in copies:
        copy.start()
    copies[0].wait()
    flat[...] = jnp.zeros_like(flat)
    for group in groups():
        taps = []
        for tap in group:
            ring = pltpu.roll(taken[tap].astype(F32), turn, 1)
            flat[tap * share : (tap + 1) * share, :] = ring.astype(BF16)
            taps.append(ring)
        first, last = group[0], group[-1] + 1
        own[:, first * share : last * share] = jnp.concatenate(
            [x[:, :share] for x in taps], axis=1
        ).astype(BF16)
        left = total - share
        rest[:, first * left : last * left] = jnp.concatenate(
            [x[:, share:] for x in taps], axis=1
        ).astype(BF16)
    by_in[...] = flat[...].T
    copies[1].wait()
    lay(shifts.at[4], FAR // LANES, staged[...])
    shift(shifts, FAR // LANES + 1, (FAR + sites) // LANES - 1)
    copies[2].wait()
    kept[...] = (near[...] >= 0).astype(F32)
    expand(kept, valid, HALO // LANES)


def own_body(left, right, weights, shifts_in, valid_in, begun, shifts, valid, kept):
    del shifts_in, valid_in
    share = begun.shape[0]
    edge = FAR // LANES
    far = shifts.shape[1] - edge
    for side, at, start in ((left, 0, 1), (right, 1, far - 1)):
        lay(shifts.at[4], at * far, side[:share, :])
        shift(shifts, start, start + edge)
        kept[...] = side[share : share + 32, HALO:].astype(F32)
        expand(kept, valid, at * (valid.shape[1] - HALO // LANES))

    def block(j, carry):
        begun[:, pl.ds(pl.multiple_of(j * WIDTH, LANES), WIDTH)] = product(
            weights, shifts, valid, j * TILES + HALO // LANES, j * TILES, lambda tap: tap
        )
        return carry

    lax.fori_loop(0, begun.shape[1] // WIDTH, block, 0)


def arrive_body(rest, own_in, shifts, across, own):
    del own_in
    sites = rest.shape[1]
    edge = FAR // LANES
    lay(shifts.at[4], edge, rest[...])
    shift(shifts, edge + 1, edge + sites // LANES - 1)

    def block(j, carry):
        at = j * TILES + edge
        across[pl.ds(pl.multiple_of(j * WIDTH, LANES), WIDTH), :] = jnp.concatenate(
            [wide(own.at[4], at, TILES), wide(shifts.at[4], at, TILES)], axis=0
        ).T
        return carry

    lax.fori_loop(0, sites // WIDTH, block, 0)


def rest_body(
    ends,
    shifts_in,
    weights,
    valid_in,
    begun,
    left,
    right,
    own,
    cotangent,
    kept,
    grads,
    valid,
    shifts,
    grad,
    hidden,
):
    del shifts_in, valid_in
    share, sites = cotangent.shape
    edge, near, halo, lead = (n // LANES for n in (FAR, NEAR, HALO, LEAD + LANES))
    far = shifts.shape[1] - edge
    lay(shifts.at[4], 0, jnp.zeros((shifts.shape[2], FAR - NEAR), BF16))
    lay(shifts.at[4], edge - near, ends[:, :NEAR])
    lay(shifts.at[4], far, ends[:, NEAR:])
    lay(shifts.at[4], far + near, jnp.zeros((shifts.shape[2], FAR - NEAR), BF16))
    shift(shifts, 1, 1 + edge)
    shift(shifts, far - 1, far - 1 + edge)
    lay(grad, lead, left[share : 2 * share, :HALO])
    lay(grad, lead + halo, cotangent[...])
    lay(grad, lead + halo + sites // LANES, right[share : 2 * share, :HALO])

    def finish(before, start, at):
        rows = pl.ds(at, ROWS)
        value = hidden[before, rows, :]
        sigma = 0.5 * jnp.tanh(0.5 * value) + 0.5
        features = wide(own.at[4], jnp.maximum(start - TILES, 0) + halo, TILES, rows)
        kept[rows, pl.ds(pl.multiple_of(start * LANES, LANES), WIDTH)] = (
            features.astype(F32) + value * sigma
        ).astype(BF16)
        there = start - TILES + lead
        ready = (
            wide(grad, there, TILES, rows).astype(F32) * sigma * (1.0 + value * (1.0 - sigma))
        ).astype(BF16)
        lay(grad, there, ready, rows)
        spread(wide(grad, start, TILES + 2, rows), grads, rows, start)

    def finishes(before, start):
        return [functools.partial(finish, before, start, at) for at in range(0, share, ROWS)]

    def block(j, carry):
        start = j * TILES
        here = pl.ds(pl.multiple_of(j * WIDTH, LANES), WIDTH)
        hidden[j % 2] = begun[:, here] + product(
            weights,
            shifts,
            valid,
            start + halo,
            start,
            lambda tap: tap,
            finishes((j + 1) % 2, start),
        )
        return carry

    count = begun.shape[1] // WIDTH
    lax.fori_loop(0, count, block, 0)
    for piece in finishes((count + 1) % 2, count * TILES):
        piece()


def weight_body(half, brick, chan, rep, across, valid_in, grads_in, kept, sent, valid, grads, total):
    del valid_in, grads_in
    share, sites = grads.shape[2], across.shape[0]
    halo, lead = HALO // LANES, LEAD // LANES
    total[...] = jnp.zeros_like(total)

    def block(j, carry):
        start = j * DEEP + halo
        here = pl.ds(pl.multiple_of(j * DEEP * LANES, LANES), DEEP * LANES)
        features = across[here, :]
        for group in groups(MANY):
            rows = []
            for tap in group:
                rows += masked(grads, valid, TAPS - 1 - tap, start + lead, start, DEEP)
            total[group[0] * share : (group[-1] + 1) * share, :] += jnp.dot(
                jnp.concatenate(rows, axis=0), features, preferred_element_type=F32
            )
        return carry

    lax.fori_loop(0, sites // (DEEP * LANES), block, 0)
    mine = rep[0]
    kept[...] = total[pl.ds(pl.multiple_of(mine * half, ROWS), half), :]
    sent[...] = total[pl.ds(pl.multiple_of((1 - mine) * half, ROWS), half), :].astype(BF16)


def feature_body(part, weights, valid, grads, own, rest):
    share, sites = own.shape
    blocks = sites // WIDTH

    def block(j, carry):
        here = pl.ds(pl.multiple_of(j * WIDTH, LANES), WIDTH)
        start = (part * blocks + j) * TILES + HALO // LANES
        total = product(
            weights, grads, valid, start + LEAD // LANES, start, lambda tap: TAPS - 1 - tap
        )
        own[:, here] = total[:share]
        rest[:, here] = total[share:].astype(BF16)
        return carry

    lax.fori_loop(0, blocks, block, 0)


def split_body(brick, chan, rep, kept, arrived, mine, sent):
    size = mine.shape[0]
    at = brick[0] % 2
    mine_rows = pl.ds(pl.multiple_of(at * size, ROWS), size)
    sent_rows = pl.ds(pl.multiple_of((1 - at) * size, ROWS), size)
    mine[...] = kept[mine_rows, :] + arrived[mine_rows, :].astype(F32)
    sent[...] = (kept[sent_rows, :] + arrived[sent_rows, :].astype(F32)).astype(BF16)


def merge_body(mine, other, out):
    out[...] = (mine[...].astype(F32) + other[...].astype(F32)).astype(BF16)


def gather_body(brick, chan, rep, mine, other, side):
    size = mine.shape[0]
    at = brick[0] % 2
    side[pl.ds(pl.multiple_of(at * size, ROWS), size), :] = mine[...]
    side[pl.ds(pl.multiple_of((1 - at) * size, ROWS), size), :] = other[...]


def join_body(half, share, brick, chan, rep, side, other, out, both):
    mine = rep[0]
    turn = chan[0] * share
    both[pl.ds(pl.multiple_of(mine * half, ROWS), half), :] = side[...]
    both[pl.ds(pl.multiple_of((1 - mine) * half, ROWS), half), :] = other[...]
    out[...] = pltpu.roll(both[: out.shape[0], :].astype(F32), turn, 1)


def emit_body(held, out, token):
    token[...] = jnp.zeros_like(token)
    out[...] = held[:, WIDTH + HALO : WIDTH + HALO + out.shape[1]]


def add_body(part, done, cotangent, own, *rest):
    *terms, out, token = rest
    token[...] = jnp.zeros_like(token)
    sites = own.shape[1]
    total = cotangent[:, part * sites : (part + 1) * sites].astype(F32) + own[...]
    for term in terms:
        total += term[...].astype(F32)
    if part == 0:
        out[...] = total.astype(BF16)
    else:
        out[:, :sites] = done[...]
        out[:, sites:] = total.astype(BF16)


def line_swap(x):
    count = lax.axis_size(("brick", "rep"))
    pairs = [p for i in range(1, count - 1, 2) for p in ((i, i + 1), (i + 1, i))]
    return lax.ppermute(x, ("brick", "rep"), pairs)


def local(features, conv_weight, neighbours, cotangent):
    share, sites = features.shape
    total = conv_weight.shape[1]
    left = total - share
    chans, bricks, reps = (lax.axis_size(axis) for axis in ("chan", "brick", "rep"))
    place = [lax.axis_index(axis)[None] for axis in LINE]
    margin = sites + 2 * HALO
    flops = 2 * TAPS * share * sites

    def around(x):
        return [
            lax.ppermute(x, "chan", [((i + over) % chans, i) for i in range(chans)])
            for over in range(1, chans)
        ]

    def stack(parts):
        return parts[0] if len(parts) == 1 else jnp.concatenate(parts, axis=0)

    assert reps == 2
    swap = [(0, 1), (1, 0)]
    rest = stack(around(features))
    to_core, to_line = kernel(
        pack_body,
        "pack",
        [shape((share + max(share, 32), FAR))] * 2,
        [features, cotangent, neighbours],
        scalars=place,
        scratch=[pltpu.VMEM((2, TAPS, HALO), jnp.int32), pltpu.SemaphoreType.DMA((6,))],
        held=True,
    )
    line = line_swap(to_line)
    core = lax.ppermute(to_core, "rep", swap)
    lanes = -(-TAPS * share // 128) * 128
    own_weights, rest_weights, by_in, shifts, valid = kernel(
        prepare_body,
        "prepare",
        [
            shape((share, TAPS * share)),
            shape((share, TAPS * left)),
            shape((total, lanes)),
            shape((9, (sites + 2 * FAR) // LANES, share, LANES)),
            shape((TAPS, margin // LANES, ROWS, LANES)),
        ],
        [jnp.transpose(conv_weight, (0, 2, 1)), features, neighbours],
        scalars=place,
        scratch=[
            pltpu.VMEM((lanes, total), BF16),
            pltpu.VMEM((TAPS, sites), F32),
            pltpu.VMEM((TAPS, share, total), BF16),
            pltpu.VMEM((share, sites), BF16),
            pltpu.VMEM((TAPS, sites), jnp.int32),
            pltpu.SemaphoreType.DMA((3,)),
        ],
        held=True,
    )
    before, behind, both = kernel(
        after(ends_body, 3),
        "ends",
        [shape(core.shape), shape(core.shape), shape((share, 2 * NEAR))],
        [own_weights, core, line],
        scalars=place,
    )
    ends = stack(around(both))
    begun, own_shifts, valid = kernel(
        own_body,
        "forward_own",
        [shape((share, margin), F32), shape(shifts.shape), shape(valid.shape)],
        [before, behind, own_weights, shifts, valid],
        scratch=[pltpu.VMEM((32, HALO), F32)],
        aliases={3: 1, 4: 2},
    )
    rest_shifts, across, own_shifts = kernel(
        arrive_body,
        "arrive",
        [shape((9, (sites + 2 * FAR) // LANES, left, LANES)), shape((sites, total)), shape(own_shifts.shape)],
        [rest, own_shifts],
        aliases={1: 2},
    )
    held, grads, valid, _ = kernel(
        rest_body,
        "forward_rest",
        [
            shape((share, WIDTH + margin)),
            shape((9, (margin + WIDTH) // LANES, share, LANES)),
            shape(valid.shape),
            shape(rest_shifts.shape),
        ],
        [ends, rest_shifts, rest_weights, valid, begun, before, behind, own_shifts, cotangent],
        scratch=[
            pltpu.VMEM(((LEAD + LANES + margin) // LANES, share, LANES), BF16),
            pltpu.VMEM((2, share, WIDTH), F32),
        ],
        aliases={1: 3, 3: 2},
        flops=flops * left,
    )

    size = -(-TAPS * share // (reps * 2 * ROWS)) * ROWS
    half = 2 * size
    kept, sent, valid, grads = kernel(
        functools.partial(weight_body, half),
        "grad_weight",
        [shape((half, total), F32), shape((half, total)), shape(valid.shape), shape(grads.shape)],
        [across, valid, grads],
        scalars=place,
        scratch=[pltpu.VMEM((reps * half, total), F32)],
        aliases={1: 2, 2: 3},
        flops=flops * total,
    )
    arrived = lax.ppermute(sent, "rep", swap)

    def feature_part(part, first):
        own, other = kernel(
            after(functools.partial(feature_body, part), 0),
            "grad_features_%d" % part,
            [shape((share, sites // 2), F32), shape((left, sites // 2))],
            [first, by_in, valid, grads],
            flops=flops * total // 2,
        )
        return [own] + [
            lax.ppermute(
                other if left == share else other[(over - 1) * share : over * share],
                "chan",
                [(i, (i + over) % chans) for i in range(chans)],
            )
            for over in range(1, chans)
        ]

    mine, sent = kernel(
        split_body,
        "split",
        [shape((size, total), F32), shape((size, total))],
        [kept, arrived],
        scalars=place,
        flops=LATER,
    )
    pairs = [(i, i ^ 1) for i in range(bricks)]
    arrived = lax.ppermute(sent, "brick", pairs)
    first = feature_part(0, mine)
    mine = kernel(
        after(merge_body, 0),
        "merge_1",
        shape((size, total)),
        [first[0], mine, arrived],
        flops=LATER,
    )
    second = feature_part(1, mine)
    output, token = kernel(
        after(emit_body, 0),
        "emit",
        [shape((share, sites)), shape((8, LANES), F32)],
        [second[0], held],
    )
    step = 2
    while step < bricks:
        other = lax.ppermute(mine, "brick", [(i, i ^ step) for i in range(bricks)])
        step *= 2
        mine = kernel(
            after(merge_body, 0),
            "merge_%d" % step,
            shape((size, total)),
            [token, mine, other],
            flops=LATER,
        )
    other = lax.ppermute(mine, "brick", pairs)
    begun, token = kernel(
        functools.partial(add_body, 0),
        "add_0",
        [shape((share, sites // 2)), shape((8, LANES), F32)],
        [mine, cotangent, *first],
    )
    side = kernel(
        after(after(gather_body, 3), 3),
        "gather",
        shape((half, total)),
        [token, second[1], mine, other],
        scalars=place,
        flops=LATER,
    )
    other = lax.ppermute(side, "rep", swap)
    grad_features, token = kernel(
        functools.partial(add_body, 1),
        "add_1",
        [shape((share, sites)), shape((8, LANES), F32)],
        [begun, cotangent, *second],
    )
    grad_weight = kernel(
        after(functools.partial(join_body, half, share), 3),
        "join",
        shape((TAPS * share, total), F32),
        [token, side, other],
        scalars=place,
        scratch=[pltpu.VMEM((reps * half, total), BF16)],
        flops=LATER,
    )
    grad_weight = jnp.transpose(grad_weight.reshape(TAPS, share, total), (0, 2, 1))
    return output, grad_features, grad_weight


def solution(mesh):
    return jax.shard_map(
        local,
        mesh=mesh,
        in_specs=(
            P("chan", ("scene", "brick", "rep")),
            P(None, None, "chan"),
            P(None, ("scene", "brick", "rep")),
            P("chan", ("scene", "brick", "rep")),
        ),
        out_specs=(
            P("chan", ("scene", "brick", "rep")),
            P("chan", ("scene", "brick", "rep")),
            P("scene", None, "chan"),
        ),
        check_vma=False,
    )
```

```python
import functools

import jax
import jax.numpy as jnp
from jax import lax
from jax.experimental import pallas as pl
from jax.experimental.pallas import tpu as pltpu
from jax.sharding import PartitionSpec as P

EDGE = 16
FACE = EDGE * EDGE
TAPS = 27
HALO = 384
FAR = 2 * HALO
NEAR = 640
LEAD = 896
MANY = 27
DEEP = 18
ROWS = 16
LANES = 128
GROUP = 8
TILES = 6
WIDTH = TILES * LANES
LATER = 12 * 10**8
LINE = ("brick", "chan", "rep")
MIB = 1024 * 1024
F32, BF16 = jnp.float32, jnp.bfloat16

STEPS = [(k // 3 - 1) * EDGE + k % 3 - 1 for k in range(9)]

HERE = pl.BlockSpec(memory_space=pltpu.VMEM)
FAR_OFF = pl.BlockSpec(memory_space=pltpu.HBM)
SCALAR = pl.BlockSpec(memory_space=pltpu.SMEM)


def kernel(body, name, outs, args, scalars=(), scratch=(), aliases={}, limit=8, flops=0, held=False):
    if held:
        args = [pltpu.with_memory_space_constraint(x, pltpu.HBM) for x in args]
    single = not isinstance(outs, (tuple, list))
    return pl.pallas_call(
        body,
        out_shape=outs,
        in_specs=[SCALAR] * len(scalars) + [FAR_OFF if held else HERE] * len(args),
        out_specs=HERE if single else [HERE] * len(outs),
        scratch_shapes=list(scratch),
        input_output_aliases={len(scalars) + i: o for i, o in aliases.items()},
        compiler_params=pltpu.CompilerParams(vmem_limit_bytes=limit * MIB),
        cost_estimate=pl.CostEstimate(flops=flops, bytes_accessed=MIB, transcendentals=0),
        name=name,
    )(*scalars, *args)


def after(body, at):
    def ordered(*refs):
        body(*refs[:at], *refs[at + 1 :])

    return ordered


def shape(dims, kind=BF16):
    return jax.ShapeDtypeStruct(dims, kind)


def wide(ref, first, count, *rows):
    return jnp.concatenate([ref[(first + i, *rows)] for i in range(count)], axis=1)


def lay(ref, first, value, *rows):
    for i in range(value.shape[1] // LANES):
        ref[(first + i, *rows)] = value[:, i * LANES : (i + 1) * LANES]


def spread(window, target, rows, first):
    width = window.shape[1]
    for j, step in enumerate(STEPS):
        moved = pltpu.roll(window, -step % width, 1) if step else window
        lay(target.at[j], first, moved[:, LANES : width - LANES], rows)


def shift(shifts, low, high):
    for at in range(0, shifts.shape[2], ROWS):
        rows = pl.ds(at, ROWS)
        spread(wide(shifts.at[4], low - 1, high - low + 2, rows), shifts, rows, low)


def masked(shifts, valid, tap, at_shift, at_valid, tiles=TILES):
    keep = wide(valid.at[tap], at_valid, tiles)
    begin = at_shift + (tap // 9 - 1) * FACE // LANES
    return [
        wide(shifts.at[tap % 9], begin, tiles, pl.ds(at, ROWS)) * keep
        for at in range(0, shifts.shape[2], ROWS)
    ]


def groups(count=GROUP):
    return [range(first, min(first + count, TAPS)) for first in range(0, TAPS, count)]


def product(
    weights, shifts, valid, at_shift, at_valid, taps_of, between=(), count=GROUP
):
    channels = shifts.shape[2]
    total = None
    for at, group in enumerate(groups(count)):
        for piece in between[at :: len(groups(count))]:
            piece()
        rows = []
        for tap in group:
            rows += masked(shifts, valid, taps_of(tap), at_shift, at_valid)
        part = jnp.dot(
            weights[:, group[0] * channels : (group[-1] + 1) * channels],
            jnp.concatenate(rows, axis=0),
            preferred_element_type=F32,
        )
        total = part if total is None else total + part
    return total


def pack_body(brick, chan, rep, features, cotangent, neighbours, to_core, to_line, near, done):
    share, sites = features.shape
    copies = []
    for i, (out, last) in enumerate(((to_core, 1 - rep[0]), (to_line, rep[0]))):
        far = pl.ds(pl.multiple_of(last * (sites - FAR), 128), FAR)
        close = pl.ds(pl.multiple_of(last * (sites - HALO), 128), HALO)
        copies += [
            pltpu.make_async_copy(source, target, done.at[3 * i + j])
            for j, (source, target) in enumerate(
                [
                    (neighbours.at[:, close], near.at[i]),
                    (features.at[:, far], out.at[pl.ds(0, share), :]),
                    (cotangent.at[:, close], out.at[pl.ds(share, share), pl.ds(0, HALO)]),
                ]
            )
        ]
    for copy in copies:
        copy.start()
    for i, out in enumerate((to_core, to_line)):
        copies[3 * i].wait()
        kept = (near[i] >= 0).astype(F32)
        kept = jnp.concatenate([kept, jnp.zeros((32 - TAPS, HALO), F32)], axis=0)
        out[share : share + 32, HALO:] = kept.astype(BF16)
        copies[3 * i + 1].wait()
        copies[3 * i + 2].wait()


def ends_body(brick, chan, rep, core, line, before, behind, both):
    share = both.shape[0]

    def fill(first, second):
        before[...] = first[...]
        behind[...] = second[...]
        both[:, :NEAR] = first[:share, FAR - NEAR :]
        both[:, NEAR:] = second[:share, :NEAR]

    pl.when(rep[0] == 0)(functools.partial(fill, line, core))
    pl.when(rep[0] != 0)(functools.partial(fill, core, line))


def expand(kept, valid, first):
    for tap in range(TAPS):
        row = jnp.broadcast_to(kept[tap : tap + 1, :], (ROWS, kept.shape[1]))
        lay(valid.at[tap], first, row.astype(BF16))


def prepare_body(
    brick, chan, rep, by_out, features, neighbours, own, rest, by_in, shifts, valid, flat, kept, taken, staged, near, done
):
    total = by_out.shape[2]
    share, sites = features.shape
    turn = lax.rem(total - chan[0] * share, total)
    copies = [
        pltpu.make_async_copy(source, target, done.at[i])
        for i, (source, target) in enumerate(
            [
                (by_out, taken),
                (features, staged),
                (neighbours, near),
            ]
        )
    ]
    for copy in copies:
        copy.start()
    copies[0].wait()
    flat[...] = jnp.zeros_like(flat)
    for group in groups():
        taps = []
        for tap in group:
            ring = pltpu.roll(taken[tap].astype(F32), turn, 1)
            flat[tap * share : (tap + 1) * share, :] = ring.astype(BF16)
            taps.append(ring)
        first, last = group[0], group[-1] + 1
        own[:, first * share : last * share] = jnp.concatenate(
            [x[:, :share] for x in taps], axis=1
        ).astype(BF16)
        left = total - share
        rest[:, first * left : last * left] = jnp.concatenate(
            [x[:, share:] for x in taps], axis=1
        ).astype(BF16)
    by_in[...] = flat[...].T
    copies[1].wait()
    lay(shifts.at[4], FAR // LANES, staged[...])
    shift(shifts, FAR // LANES + 1, (FAR + sites) // LANES - 1)
    copies[2].wait()
    kept[...] = (near[...] >= 0).astype(F32)
    expand(kept, valid, HALO // LANES)


def own_body(left, right, weights, shifts_in, valid_in, begun, shifts, valid, kept):
    del shifts_in, valid_in
    share = begun.shape[0]
    edge = FAR // LANES
    far = shifts.shape[1] - edge
    for side, at, start in ((left, 0, 1), (right, 1, far - 1)):
        lay(shifts.at[4], at * far, side[:share, :])
        shift(shifts, start, start + edge)
        kept[...] = side[share : share + 32, HALO:].astype(F32)
        expand(kept, valid, at * (valid.shape[1] - HALO // LANES))

    def block(j, carry):
        begun[:, pl.ds(pl.multiple_of(j * WIDTH, LANES), WIDTH)] = product(
            weights, shifts, valid, j * TILES + HALO // LANES, j * TILES, lambda tap: tap
        )
        return carry

    lax.fori_loop(0, begun.shape[1] // WIDTH, block, 0)


def arrive_body(rest, own_in, shifts, across, own):
    del own_in
    sites = rest.shape[1]
    edge = FAR // LANES
    lay(shifts.at[4], edge, rest[...])
    shift(shifts, edge + 1, edge + sites // LANES - 1)

    def block(j, carry):
        at = j * TILES + edge
        across[pl.ds(pl.multiple_of(j * WIDTH, LANES), WIDTH), :] = jnp.concatenate(
            [wide(own.at[4], at, TILES), wide(shifts.at[4], at, TILES)], axis=0
        ).T
        return carry

    lax.fori_loop(0, sites // WIDTH, block, 0)


def rest_body(
    ends,
    shifts_in,
    weights,
    valid_in,
    begun,
    left,
    right,
    own,
    cotangent,
    kept,
    grads,
    valid,
    shifts,
    grad,
    hidden,
):
    del shifts_in, valid_in
    share, sites = cotangent.shape
    edge, near, halo, lead = (n // LANES for n in (FAR, NEAR, HALO, LEAD + LANES))
    far = shifts.shape[1] - edge
    lay(shifts.at[4], 0, jnp.zeros((shifts.shape[2], FAR - NEAR), BF16))
    lay(shifts.at[4], edge - near, ends[:, :NEAR])
    lay(shifts.at[4], far, ends[:, NEAR:])
    lay(shifts.at[4], far + near, jnp.zeros((shifts.shape[2], FAR - NEAR), BF16))
    shift(shifts, 1, 1 + edge)
    shift(shifts, far - 1, far - 1 + edge)
    lay(grad, lead, left[share : 2 * share, :HALO])
    lay(grad, lead + halo, cotangent[...])
    lay(grad, lead + halo + sites // LANES, right[share : 2 * share, :HALO])

    def finish(before, start, at):
        rows = pl.ds(at, ROWS)
        value = hidden[before, rows, :]
        sigma = 0.5 * jnp.tanh(0.5 * value) + 0.5
        features = wide(own.at[4], jnp.maximum(start - TILES, 0) + halo, TILES, rows)
        kept[rows, pl.ds(pl.multiple_of(start * LANES, LANES), WIDTH)] = (
            features.astype(F32) + value * sigma
        ).astype(BF16)
        there = start - TILES + lead
        ready = (
            wide(grad, there, TILES, rows).astype(F32) * sigma * (1.0 + value * (1.0 - sigma))
        ).astype(BF16)
        lay(grad, there, ready, rows)
        spread(wide(grad, start, TILES + 2, rows), grads, rows, start)

    def finishes(before, start):
        return [functools.partial(finish, before, start, at) for at in range(0, share, ROWS)]

    def block(j, carry):
        start = j * TILES
        here = pl.ds(pl.multiple_of(j * WIDTH, LANES), WIDTH)
        hidden[j % 2] = begun[:, here] + product(
            weights,
            shifts,
            valid,
            start + halo,
            start,
            lambda tap: tap,
            finishes((j + 1) % 2, start),
        )
        return carry

    count = begun.shape[1] // WIDTH
    lax.fori_loop(0, count, block, 0)
    for piece in finishes((count + 1) % 2, count * TILES):
        piece()


def weight_body(half, brick, chan, rep, across, valid_in, grads_in, kept, sent, valid, grads, total):
    del valid_in, grads_in
    share, sites = grads.shape[2], across.shape[0]
    halo, lead = HALO // LANES, LEAD // LANES
    total[...] = jnp.zeros_like(total)

    def block(j, carry):
        start = j * DEEP + halo
        here = pl.ds(pl.multiple_of(j * DEEP * LANES, LANES), DEEP * LANES)
        features = across[here, :]
        for group in groups(MANY):
            rows = []
            for tap in group:
                rows += masked(grads, valid, TAPS - 1 - tap, start + lead, start, DEEP)
            total[group[0] * share : (group[-1] + 1) * share, :] += jnp.dot(
                jnp.concatenate(rows, axis=0), features, preferred_element_type=F32
            )
        return carry

    lax.fori_loop(0, sites // (DEEP * LANES), block, 0)
    mine = rep[0]
    kept[...] = total[pl.ds(pl.multiple_of(mine * half, ROWS), half), :]
    sent[...] = total[pl.ds(pl.multiple_of((1 - mine) * half, ROWS), half), :].astype(BF16)


def feature_body(first, last, lead_in, weights, valid, grads, *refs):
    own, rest = refs[-2:]
    share = own.shape[0]

    def block(j, carry):
        here = pl.ds(pl.multiple_of((j - lead_in) * WIDTH, LANES), WIDTH)
        start = j * TILES + HALO // LANES
        total = product(
            weights, grads, valid, start + LEAD // LANES, start, lambda tap: TAPS - 1 - tap
        )
        own[:, here] = total[:share]
        rest[:, here] = total[share:].astype(BF16)
        return carry

    lax.fori_loop(first, last, block, 0)


def split_body(brick, chan, rep, kept, arrived, mine, sent):
    size = mine.shape[0]
    at = brick[0] % 2
    mine_rows = pl.ds(pl.multiple_of(at * size, ROWS), size)
    sent_rows = pl.ds(pl.multiple_of((1 - at) * size, ROWS), size)
    mine[...] = kept[mine_rows, :] + arrived[mine_rows, :].astype(F32)
    sent[...] = (kept[sent_rows, :] + arrived[sent_rows, :].astype(F32)).astype(BF16)


def merge_body(mine, other, out):
    out[...] = (mine[...].astype(F32) + other[...].astype(F32)).astype(BF16)


def gather_body(brick, chan, rep, mine, other, side):
    size = mine.shape[0]
    at = brick[0] % 2
    side[pl.ds(pl.multiple_of(at * size, ROWS), size), :] = mine[...]
    side[pl.ds(pl.multiple_of((1 - at) * size, ROWS), size), :] = other[...]


def join_body(half, share, brick, chan, rep, side, other, out, both):
    mine = rep[0]
    turn = chan[0] * share
    both[pl.ds(pl.multiple_of(mine * half, ROWS), half), :] = side[...]
    both[pl.ds(pl.multiple_of((1 - mine) * half, ROWS), half), :] = other[...]
    out[...] = pltpu.roll(both[: out.shape[0], :].astype(F32), turn, 1)


def emit_body(held, out, token):
    token[...] = jnp.zeros_like(token)
    out[...] = held[:, WIDTH + HALO : WIDTH + HALO + out.shape[1]]


def add_body(part, done, cotangent, own, *rest):
    *terms, out, token = rest
    token[...] = jnp.zeros_like(token)
    sites = own.shape[1]
    begin = part * (cotangent.shape[1] - sites)
    total = cotangent[:, begin : begin + sites].astype(F32) + own[...]
    for term in terms:
        total += term[...].astype(F32)
    if part == 0:
        out[...] = total.astype(BF16)
    else:
        out[:, :begin] = done[...]
        out[:, begin:] = total.astype(BF16)


def line_swap(x):
    count = lax.axis_size(("brick", "rep"))
    pairs = [p for i in range(1, count - 1, 2) for p in ((i, i + 1), (i + 1, i))]
    return lax.ppermute(x, ("brick", "rep"), pairs)


def local(features, conv_weight, neighbours, cotangent):
    share, sites = features.shape
    total = conv_weight.shape[1]
    left = total - share
    chans, bricks, reps = (lax.axis_size(axis) for axis in ("chan", "brick", "rep"))
    place = [lax.axis_index(axis)[None] for axis in LINE]
    margin = sites + 2 * HALO
    flops = 2 * TAPS * share * sites

    def around(x):
        return [
            lax.ppermute(x, "chan", [((i + over) % chans, i) for i in range(chans)])
            for over in range(1, chans)
        ]

    def stack(parts):
        return parts[0] if len(parts) == 1 else jnp.concatenate(parts, axis=0)

    assert reps == 2
    swap = [(0, 1), (1, 0)]
    rest = stack(around(features))
    to_core, to_line = kernel(
        pack_body,
        "pack",
        [shape((share + max(share, 32), FAR))] * 2,
        [features, cotangent, neighbours],
        scalars=place,
        scratch=[pltpu.VMEM((2, TAPS, HALO), jnp.int32), pltpu.SemaphoreType.DMA((6,))],
        held=True,
    )
    line = line_swap(to_line)
    core = lax.ppermute(to_core, "rep", swap)
    lanes = -(-TAPS * share // 128) * 128
    own_weights, rest_weights, by_in, shifts, valid = kernel(
        prepare_body,
        "prepare",
        [
            shape((share, TAPS * share)),
            shape((share, TAPS * left)),
            shape((total, lanes)),
            shape((9, (sites + 2 * FAR) // LANES, share, LANES)),
            shape((TAPS, margin // LANES, ROWS, LANES)),
        ],
        [jnp.transpose(conv_weight, (0, 2, 1)), features, neighbours],
        scalars=place,
        scratch=[
            pltpu.VMEM((lanes, total), BF16),
            pltpu.VMEM((TAPS, sites), F32),
            pltpu.VMEM((TAPS, share, total), BF16),
            pltpu.VMEM((share, sites), BF16),
            pltpu.VMEM((TAPS, sites), jnp.int32),
            pltpu.SemaphoreType.DMA((3,)),
        ],
        held=True,
    )
    before, behind, both = kernel(
        after(ends_body, 3),
        "ends",
        [shape(core.shape), shape(core.shape), shape((share, 2 * NEAR))],
        [own_weights, core, line],
        scalars=place,
    )
    ends = stack(around(both))
    begun, own_shifts, valid = kernel(
        own_body,
        "forward_own",
        [shape((share, margin), F32), shape(shifts.shape), shape(valid.shape)],
        [before, behind, own_weights, shifts, valid],
        scratch=[pltpu.VMEM((32, HALO), F32)],
        aliases={3: 1, 4: 2},
    )
    rest_shifts, across, own_shifts = kernel(
        arrive_body,
        "arrive",
        [shape((9, (sites + 2 * FAR) // LANES, left, LANES)), shape((sites, total)), shape(own_shifts.shape)],
        [rest, own_shifts],
        aliases={1: 2},
    )
    held, grads, valid, _ = kernel(
        rest_body,
        "forward_rest",
        [
            shape((share, WIDTH + margin)),
            shape((9, (margin + WIDTH) // LANES, share, LANES)),
            shape(valid.shape),
            shape(rest_shifts.shape),
        ],
        [ends, rest_shifts, rest_weights, valid, begun, before, behind, own_shifts, cotangent],
        scratch=[
            pltpu.VMEM(((LEAD + LANES + margin) // LANES, share, LANES), BF16),
            pltpu.VMEM((2, share, WIDTH), F32),
        ],
        aliases={1: 3, 3: 2},
        flops=flops * left,
    )

    size = -(-TAPS * share // (reps * 2 * ROWS)) * ROWS
    half = 2 * size
    kept, sent, valid, grads = kernel(
        functools.partial(weight_body, half),
        "grad_weight",
        [shape((half, total), F32), shape((half, total)), shape(valid.shape), shape(grads.shape)],
        [across, valid, grads],
        scalars=place,
        scratch=[pltpu.VMEM((reps * half, total), F32)],
        aliases={1: 2, 2: 3},
        flops=flops * total,
    )
    arrived = lax.ppermute(sent, "rep", swap)

    third = sites // WIDTH // 3

    def feature_part(part, ahead, so_far=()):
        lead_in = 2 * third if part == 2 else 0
        count = third if part == 2 else 2 * third
        return kernel(
            after(
                functools.partial(feature_body, part * third, (part + 1) * third, lead_in), 0
            ),
            "grad_features_%d" % part,
            [shape((share, count * WIDTH), F32), shape((left, count * WIDTH))],
            [ahead, by_in, valid, grads, *so_far],
            aliases={4 + i: i for i in range(len(so_far))},
            flops=flops * total // 3,
        )

    def terms_of(own, other):
        return [own] + [
            lax.ppermute(
                other if left == share else other[(over - 1) * share : over * share],
                "chan",
                [(i, (i + over) % chans) for i in range(chans)],
            )
            for over in range(1, chans)
        ]

    parts = feature_part(0, kept)
    mine, sent = kernel(
        after(split_body, 3),
        "split",
        [shape((size, total), F32), shape((size, total))],
        [parts[0], kept, arrived],
        scalars=place,
        flops=LATER,
    )
    pairs = [(i, i ^ 1) for i in range(bricks)]
    arrived = lax.ppermute(sent, "brick", pairs)
    first = terms_of(*feature_part(1, mine, parts))
    mine = kernel(
        after(merge_body, 0),
        "merge_1",
        shape((size, total)),
        [first[0], mine, arrived],
        flops=LATER,
    )
    second = terms_of(*feature_part(2, mine))
    output, token = kernel(
        after(emit_body, 0),
        "emit",
        [shape((share, sites)), shape((8, LANES), F32)],
        [second[0], held],
    )
    step = 2
    while step < bricks:
        other = lax.ppermute(mine, "brick", [(i, i ^ step) for i in range(bricks)])
        step *= 2
        mine = kernel(
            after(merge_body, 0),
            "merge_%d" % step,
            shape((size, total)),
            [token, mine, other],
            flops=LATER,
        )
    other = lax.ppermute(mine, "brick", pairs)
    begun, token = kernel(
        functools.partial(add_body, 0),
        "add_0",
        [shape((share, 2 * third * WIDTH)), shape((8, LANES), F32)],
        [mine, cotangent, *first],
    )
    side = kernel(
        after(after(gather_body, 3), 3),
        "gather",
        shape((half, total)),
        [token, second[1], mine, other],
        scalars=place,
        flops=LATER,
    )
    other = lax.ppermute(side, "rep", swap)
    grad_features, token = kernel(
        functools.partial(add_body, 1),
        "add_1",
        [shape((share, sites)), shape((8, LANES), F32)],
        [begun, cotangent, *second],
    )
    grad_weight = kernel(
        after(functools.partial(join_body, half, share), 3),
        "join",
        shape((TAPS * share, total), F32),
        [token, side, other],
        scalars=place,
        scratch=[pltpu.VMEM((reps * half, total), BF16)],
        flops=LATER,
    )
    grad_weight = jnp.transpose(grad_weight.reshape(TAPS, share, total), (0, 2, 1))
    return output, grad_features, grad_weight


def solution(mesh):
    return jax.shard_map(
        local,
        mesh=mesh,
        in_specs=(
            P("chan", ("scene", "brick", "rep")),
            P(None, None, "chan"),
            P(None, ("scene", "brick", "rep")),
            P("chan", ("scene", "brick", "rep")),
        ),
        out_specs=(
            P("chan", ("scene", "brick", "rep")),
            P("chan", ("scene", "brick", "rep")),
            P("scene", None, "chan"),
        ),
        check_vma=False,
    )
```

```python
import functools

import jax
import jax.numpy as jnp
from jax import lax
from jax.experimental import pallas as pl
from jax.experimental.pallas import tpu as pltpu
from jax.sharding import PartitionSpec as P

EDGE = 16
FACE = EDGE * EDGE
TAPS = 27
HALO = 384
FAR = 2 * HALO
NEAR = 640
LEAD = 896
MANY = 27
DEEP = 18
ROWS = 16
LANES = 128
GROUP = 8
TILES = 6
WIDTH = TILES * LANES
LATER = 12 * 10**8
LINE = ("brick", "chan", "rep")
MIB = 1024 * 1024
F32, BF16 = jnp.float32, jnp.bfloat16

STEPS = [(k // 3 - 1) * EDGE + k % 3 - 1 for k in range(9)]

HERE = pl.BlockSpec(memory_space=pltpu.VMEM)
FAR_OFF = pl.BlockSpec(memory_space=pltpu.HBM)
SCALAR = pl.BlockSpec(memory_space=pltpu.SMEM)


def kernel(body, name, outs, args, scalars=(), scratch=(), aliases={}, limit=8, flops=0, held=False):
    if held:
        args = [pltpu.with_memory_space_constraint(x, pltpu.HBM) for x in args]
    single = not isinstance(outs, (tuple, list))
    return pl.pallas_call(
        body,
        out_shape=outs,
        in_specs=[SCALAR] * len(scalars) + [FAR_OFF if held else HERE] * len(args),
        out_specs=HERE if single else [HERE] * len(outs),
        scratch_shapes=list(scratch),
        input_output_aliases={len(scalars) + i: o for i, o in aliases.items()},
        compiler_params=pltpu.CompilerParams(vmem_limit_bytes=limit * MIB),
        cost_estimate=pl.CostEstimate(flops=flops, bytes_accessed=MIB, transcendentals=0),
        name=name,
    )(*scalars, *args)


def after(body, at):
    def ordered(*refs):
        body(*refs[:at], *refs[at + 1 :])

    return ordered


def shape(dims, kind=BF16):
    return jax.ShapeDtypeStruct(dims, kind)


def wide(ref, first, count, *rows):
    return jnp.concatenate([ref[(first + i, *rows)] for i in range(count)], axis=1)


def lay(ref, first, value, *rows):
    for i in range(value.shape[1] // LANES):
        ref[(first + i, *rows)] = value[:, i * LANES : (i + 1) * LANES]


def spread(window, target, rows, first):
    width = window.shape[1]
    for j, step in enumerate(STEPS):
        moved = pltpu.roll(window, -step % width, 1) if step else window
        lay(target.at[j], first, moved[:, LANES : width - LANES], rows)


def shift(shifts, low, high):
    for at in range(0, shifts.shape[2], ROWS):
        rows = pl.ds(at, ROWS)
        spread(wide(shifts.at[4], low - 1, high - low + 2, rows), shifts, rows, low)


def masked(shifts, valid, tap, at_shift, at_valid, tiles=TILES):
    keep = wide(valid.at[tap], at_valid, tiles)
    begin = at_shift + (tap // 9 - 1) * FACE // LANES
    return [
        wide(shifts.at[tap % 9], begin, tiles, pl.ds(at, ROWS)) * keep
        for at in range(0, shifts.shape[2], ROWS)
    ]


def groups(count=GROUP):
    return [range(first, min(first + count, TAPS)) for first in range(0, TAPS, count)]


def product(
    weights, shifts, valid, at_shift, at_valid, taps_of, between=(), count=GROUP
):
    channels = shifts.shape[2]
    total = None
    for at, group in enumerate(groups(count)):
        for piece in between[at :: len(groups(count))]:
            piece()
        rows = []
        for tap in group:
            rows += masked(shifts, valid, taps_of(tap), at_shift, at_valid)
        part = jnp.dot(
            weights[:, group[0] * channels : (group[-1] + 1) * channels],
            jnp.concatenate(rows, axis=0),
            preferred_element_type=F32,
        )
        total = part if total is None else total + part
    return total


def pack_body(brick, chan, rep, features, cotangent, neighbours, to_core, to_line, near, done):
    share, sites = features.shape
    copies = []
    for i, (out, last) in enumerate(((to_core, 1 - rep[0]), (to_line, rep[0]))):
        far = pl.ds(pl.multiple_of(last * (sites - FAR), 128), FAR)
        close = pl.ds(pl.multiple_of(last * (sites - HALO), 128), HALO)
        copies += [
            pltpu.make_async_copy(source, target, done.at[3 * i + j])
            for j, (source, target) in enumerate(
                [
                    (neighbours.at[:, close], near.at[i]),
                    (features.at[:, far], out.at[pl.ds(0, share), :]),
                    (cotangent.at[:, close], out.at[pl.ds(share, share), pl.ds(0, HALO)]),
                ]
            )
        ]
    for copy in copies:
        copy.start()
    for i, out in enumerate((to_core, to_line)):
        copies[3 * i].wait()
        kept = (near[i] >= 0).astype(F32)
        kept = jnp.concatenate([kept, jnp.zeros((32 - TAPS, HALO), F32)], axis=0)
        out[share : share + 32, HALO:] = kept.astype(BF16)
        copies[3 * i + 1].wait()
        copies[3 * i + 2].wait()


def ends_body(brick, chan, rep, core, line, before, behind, both):
    share = both.shape[0]

    def fill(first, second):
        before[...] = first[...]
        behind[...] = second[...]
        both[:, :NEAR] = first[:share, FAR - NEAR :]
        both[:, NEAR:] = second[:share, :NEAR]

    pl.when(rep[0] == 0)(functools.partial(fill, line, core))
    pl.when(rep[0] != 0)(functools.partial(fill, core, line))


def expand(kept, valid, first):
    for tap in range(TAPS):
        row = jnp.broadcast_to(kept[tap : tap + 1, :], (ROWS, kept.shape[1]))
        lay(valid.at[tap], first, row.astype(BF16))


def prepare_body(
    brick, chan, rep, by_out, features, neighbours, own, rest, by_in, shifts, valid, flat, kept, taken, staged, near, done
):
    total = by_out.shape[2]
    share, sites = features.shape
    turn = lax.rem(total - chan[0] * share, total)
    copies = [
        pltpu.make_async_copy(source, target, done.at[i])
        for i, (source, target) in enumerate(
            [
                (by_out, taken),
                (features, staged),
                (neighbours, near),
            ]
        )
    ]
    for copy in copies:
        copy.start()
    copies[0].wait()
    flat[...] = jnp.zeros_like(flat)
    for group in groups():
        taps = []
        for tap in group:
            ring = pltpu.roll(taken[tap].astype(F32), turn, 1)
            flat[tap * share : (tap + 1) * share, :] = ring.astype(BF16)
            taps.append(ring)
        first, last = group[0], group[-1] + 1
        own[:, first * share : last * share] = jnp.concatenate(
            [x[:, :share] for x in taps], axis=1
        ).astype(BF16)
        left = total - share
        rest[:, first * left : last * left] = jnp.concatenate(
            [x[:, share:] for x in taps], axis=1
        ).astype(BF16)
    by_in[...] = flat[...].T
    copies[1].wait()
    lay(shifts.at[4], FAR // LANES, staged[...])
    shift(shifts, FAR // LANES + 1, (FAR + sites) // LANES - 1)
    copies[2].wait()
    kept[...] = (near[...] >= 0).astype(F32)
    expand(kept, valid, HALO // LANES)


def own_body(left, right, weights, shifts_in, valid_in, begun, shifts, valid, kept):
    del shifts_in, valid_in
    share = begun.shape[0]
    edge = FAR // LANES
    far = shifts.shape[1] - edge
    for side, at, start in ((left, 0, 1), (right, 1, far - 1)):
        lay(shifts.at[4], at * far, side[:share, :])
        shift(shifts, start, start + edge)
        kept[...] = side[share : share + 32, HALO:].astype(F32)
        expand(kept, valid, at * (valid.shape[1] - HALO // LANES))

    def block(j, carry):
        begun[:, pl.ds(pl.multiple_of(j * WIDTH, LANES), WIDTH)] = product(
            weights, shifts, valid, j * TILES + HALO // LANES, j * TILES, lambda tap: tap
        )
        return carry

    lax.fori_loop(0, begun.shape[1] // WIDTH, block, 0)


def arrive_body(rest, own_in, shifts, across, own):
    del own_in
    sites = rest.shape[1]
    edge = FAR // LANES
    lay(shifts.at[4], edge, rest[...])
    shift(shifts, edge + 1, edge + sites // LANES - 1)

    def block(j, carry):
        at = j * TILES + edge
        across[pl.ds(pl.multiple_of(j * WIDTH, LANES), WIDTH), :] = jnp.concatenate(
            [wide(own.at[4], at, TILES), wide(shifts.at[4], at, TILES)], axis=0
        ).T
        return carry

    lax.fori_loop(0, sites // WIDTH, block, 0)


def rest_body(
    ends,
    shifts_in,
    weights,
    valid_in,
    begun,
    left,
    right,
    own,
    cotangent,
    kept,
    grads,
    valid,
    shifts,
    grad,
    hidden,
):
    del shifts_in, valid_in
    share, sites = cotangent.shape
    edge, near, halo, lead = (n // LANES for n in (FAR, NEAR, HALO, LEAD + LANES))
    far = shifts.shape[1] - edge
    lay(shifts.at[4], 0, jnp.zeros((shifts.shape[2], FAR - NEAR), BF16))
    lay(shifts.at[4], edge - near, ends[:, :NEAR])
    lay(shifts.at[4], far, ends[:, NEAR:])
    lay(shifts.at[4], far + near, jnp.zeros((shifts.shape[2], FAR - NEAR), BF16))
    shift(shifts, 1, 1 + edge)
    shift(shifts, far - 1, far - 1 + edge)
    lay(grad, lead, left[share : 2 * share, :HALO])
    lay(grad, lead + halo, cotangent[...])
    lay(grad, lead + halo + sites // LANES, right[share : 2 * share, :HALO])

    def finish(before, start, at):
        rows = pl.ds(at, ROWS)
        value = hidden[before, rows, :]
        sigma = 0.5 * jnp.tanh(0.5 * value) + 0.5
        features = wide(own.at[4], jnp.maximum(start - TILES, 0) + halo, TILES, rows)
        kept[rows, pl.ds(pl.multiple_of(start * LANES, LANES), WIDTH)] = (
            features.astype(F32) + value * sigma
        ).astype(BF16)
        there = start - TILES + lead
        ready = (
            wide(grad, there, TILES, rows).astype(F32) * sigma * (1.0 + value * (1.0 - sigma))
        ).astype(BF16)
        lay(grad, there, ready, rows)
        spread(wide(grad, start, TILES + 2, rows), grads, rows, start)

    def finishes(before, start):
        return [functools.partial(finish, before, start, at) for at in range(0, share, ROWS)]

    def block(j, carry):
        start = j * TILES
        here = pl.ds(pl.multiple_of(j * WIDTH, LANES), WIDTH)
        hidden[j % 2] = begun[:, here] + product(
            weights,
            shifts,
            valid,
            start + halo,
            start,
            lambda tap: tap,
            finishes((j + 1) % 2, start),
        )
        return carry

    count = begun.shape[1] // WIDTH
    lax.fori_loop(0, count, block, 0)
    for piece in finishes((count + 1) % 2, count * TILES):
        piece()


def weight_body(half, brick, chan, rep, across, valid_in, grads_in, kept, sent, valid, grads, total):
    del valid_in, grads_in
    share, sites = grads.shape[2], across.shape[0]
    halo, lead = HALO // LANES, LEAD // LANES
    if total.shape[0] > TAPS * share:
        total[...] = jnp.zeros_like(total)

    for j in range(sites // (DEEP * LANES)):
        start = j * DEEP + halo
        here = pl.ds(j * DEEP * LANES, DEEP * LANES)
        features = across[here, :]
        for group in groups(MANY):
            rows = []
            for tap in group:
                rows += masked(grads, valid, TAPS - 1 - tap, start + lead, start, DEEP)
            part = jnp.dot(jnp.concatenate(rows, axis=0), features, preferred_element_type=F32)
            here = slice(group[0] * share, (group[-1] + 1) * share)
            total[here, :] = part if j == 0 else total[here, :] + part
    mine = rep[0]
    kept[...] = total[pl.ds(pl.multiple_of(mine * half, ROWS), half), :]
    sent[...] = total[pl.ds(pl.multiple_of((1 - mine) * half, ROWS), half), :].astype(BF16)


def feature_body(first, last, lead_in, weights, valid, grads, *refs):
    own, rest = refs[-2:]
    share = own.shape[0]

    def block(j, carry):
        here = pl.ds(pl.multiple_of((j - lead_in) * WIDTH, LANES), WIDTH)
        start = j * TILES + HALO // LANES
        total = product(
            weights, grads, valid, start + LEAD // LANES, start, lambda tap: TAPS - 1 - tap
        )
        own[:, here] = total[:share]
        rest[:, here] = total[share:].astype(BF16)
        return carry

    lax.fori_loop(first, last, block, 0)


def split_body(brick, chan, rep, kept, arrived, mine, sent):
    size = mine.shape[0]
    at = brick[0] % 2
    mine_rows = pl.ds(pl.multiple_of(at * size, ROWS), size)
    sent_rows = pl.ds(pl.multiple_of((1 - at) * size, ROWS), size)
    mine[...] = kept[mine_rows, :] + arrived[mine_rows, :].astype(F32)
    sent[...] = (kept[sent_rows, :] + arrived[sent_rows, :].astype(F32)).astype(BF16)


def merge_body(mine, other, out):
    out[...] = (mine[...].astype(F32) + other[...].astype(F32)).astype(BF16)


def gather_body(brick, chan, rep, mine, other, side):
    size = mine.shape[0]
    at = brick[0] % 2
    side[pl.ds(pl.multiple_of(at * size, ROWS), size), :] = mine[...]
    side[pl.ds(pl.multiple_of((1 - at) * size, ROWS), size), :] = other[...]


def join_body(half, share, brick, chan, rep, side, other, out, both):
    mine = rep[0]
    turn = chan[0] * share
    both[pl.ds(pl.multiple_of(mine * half, ROWS), half), :] = side[...]
    both[pl.ds(pl.multiple_of((1 - mine) * half, ROWS), half), :] = other[...]
    out[...] = pltpu.roll(both[: out.shape[0], :].astype(F32), turn, 1)


def emit_body(held, out, token):
    token[...] = jnp.zeros_like(token)
    out[...] = held[:, WIDTH + HALO : WIDTH + HALO + out.shape[1]]


def add_body(part, done, cotangent, own, *rest):
    *terms, out, token = rest
    token[...] = jnp.zeros_like(token)
    sites = own.shape[1]
    begin = part * (cotangent.shape[1] - sites)
    total = cotangent[:, begin : begin + sites].astype(F32) + own[...]
    for term in terms:
        total += term[...].astype(F32)
    if part == 0:
        out[...] = total.astype(BF16)
    else:
        out[:, :begin] = done[...]
        out[:, begin:] = total.astype(BF16)


def line_swap(x):
    count = lax.axis_size(("brick", "rep"))
    pairs = [p for i in range(1, count - 1, 2) for p in ((i, i + 1), (i + 1, i))]
    return lax.ppermute(x, ("brick", "rep"), pairs)


def local(features, conv_weight, neighbours, cotangent):
    share, sites = features.shape
    total = conv_weight.shape[1]
    left = total - share
    chans, bricks, reps = (lax.axis_size(axis) for axis in ("chan", "brick", "rep"))
    place = [lax.axis_index(axis)[None] for axis in LINE]
    margin = sites + 2 * HALO
    flops = 2 * TAPS * share * sites

    def around(x):
        return [
            lax.ppermute(x, "chan", [((i + over) % chans, i) for i in range(chans)])
            for over in range(1, chans)
        ]

    def stack(parts):
        return parts[0] if len(parts) == 1 else jnp.concatenate(parts, axis=0)

    assert reps == 2
    swap = [(0, 1), (1, 0)]
    rest = stack(around(features))
    to_core, to_line = kernel(
        pack_body,
        "pack",
        [shape((share + max(share, 32), FAR))] * 2,
        [features, cotangent, neighbours],
        scalars=place,
        scratch=[pltpu.VMEM((2, TAPS, HALO), jnp.int32), pltpu.SemaphoreType.DMA((6,))],
        held=True,
    )
    line = line_swap(to_line)
    core = lax.ppermute(to_core, "rep", swap)
    lanes = -(-TAPS * share // 128) * 128
    own_weights, rest_weights, by_in, shifts, valid = kernel(
        prepare_body,
        "prepare",
        [
            shape((share, TAPS * share)),
            shape((share, TAPS * left)),
            shape((total, lanes)),
            shape((9, (sites + 2 * FAR) // LANES, share, LANES)),
            shape((TAPS, margin // LANES, ROWS, LANES)),
        ],
        [jnp.transpose(conv_weight, (0, 2, 1)), features, neighbours],
        scalars=place,
        scratch=[
            pltpu.VMEM((lanes, total), BF16),
            pltpu.VMEM((TAPS, sites), F32),
            pltpu.VMEM((TAPS, share, total), BF16),
            pltpu.VMEM((share, sites), BF16),
            pltpu.VMEM((TAPS, sites), jnp.int32),
            pltpu.SemaphoreType.DMA((3,)),
        ],
        held=True,
    )
    before, behind, both = kernel(
        after(ends_body, 3),
        "ends",
        [shape(core.shape), shape(core.shape), shape((share, 2 * NEAR))],
        [own_weights, core, line],
        scalars=place,
    )
    ends = stack(around(both))
    begun, own_shifts, valid = kernel(
        own_body,
        "forward_own",
        [shape((share, margin), F32), shape(shifts.shape), shape(valid.shape)],
        [before, behind, own_weights, shifts, valid],
        scratch=[pltpu.VMEM((32, HALO), F32)],
        aliases={3: 1, 4: 2},
    )
    rest_shifts, across, own_shifts = kernel(
        arrive_body,
        "arrive",
        [shape((9, (sites + 2 * FAR) // LANES, left, LANES)), shape((sites, total)), shape(own_shifts.shape)],
        [rest, own_shifts],
        aliases={1: 2},
    )
    held, grads, valid, _ = kernel(
        rest_body,
        "forward_rest",
        [
            shape((share, WIDTH + margin)),
            shape((9, (margin + WIDTH) // LANES, share, LANES)),
            shape(valid.shape),
            shape(rest_shifts.shape),
        ],
        [ends, rest_shifts, rest_weights, valid, begun, before, behind, own_shifts, cotangent],
        scratch=[
            pltpu.VMEM(((LEAD + LANES + margin) // LANES, share, LANES), BF16),
            pltpu.VMEM((2, share, WIDTH), F32),
        ],
        aliases={1: 3, 3: 2},
        flops=flops * left,
    )

    size = -(-TAPS * share // (reps * 2 * ROWS)) * ROWS
    half = 2 * size
    kept, sent, valid, grads = kernel(
        functools.partial(weight_body, half),
        "grad_weight",
        [shape((half, total), F32), shape((half, total)), shape(valid.shape), shape(grads.shape)],
        [across, valid, grads],
        scalars=place,
        scratch=[pltpu.VMEM((reps * half, total), F32)],
        aliases={1: 2, 2: 3},
        flops=flops * total,
    )
    arrived = lax.ppermute(sent, "rep", swap)

    third = sites // WIDTH // 3

    def feature_part(part, ahead, so_far=()):
        lead_in = 2 * third if part == 2 else 0
        count = third if part == 2 else 2 * third
        return kernel(
            after(
                functools.partial(feature_body, part * third, (part + 1) * third, lead_in), 0
            ),
            "grad_features_%d" % part,
            [shape((share, count * WIDTH), F32), shape((left, count * WIDTH))],
            [ahead, by_in, valid, grads, *so_far],
            aliases={4 + i: i for i in range(len(so_far))},
            flops=flops * total // 3,
        )

    def terms_of(own, other):
        return [own] + [
            lax.ppermute(
                other if left == share else other[(over - 1) * share : over * share],
                "chan",
                [(i, (i + over) % chans) for i in range(chans)],
            )
            for over in range(1, chans)
        ]

    parts = feature_part(0, kept)
    mine, sent = kernel(
        after(split_body, 3),
        "split",
        [shape((size, total), F32), shape((size, total))],
        [parts[0], kept, arrived],
        scalars=place,
        flops=LATER,
    )
    pairs = [(i, i ^ 1) for i in range(bricks)]
    arrived = lax.ppermute(sent, "brick", pairs)
    first = terms_of(*feature_part(1, mine, parts))
    mine = kernel(
        after(merge_body, 0),
        "merge_1",
        shape((size, total)),
        [first[0], mine, arrived],
        flops=LATER,
    )
    second = terms_of(*feature_part(2, mine))
    output, token = kernel(
        after(emit_body, 0),
        "emit",
        [shape((share, sites)), shape((8, LANES), F32)],
        [second[0], held],
    )
    step = 2
    while step < bricks:
        other = lax.ppermute(mine, "brick", [(i, i ^ step) for i in range(bricks)])
        step *= 2
        mine = kernel(
            after(merge_body, 0),
            "merge_%d" % step,
            shape((size, total)),
            [token, mine, other],
            flops=LATER,
        )
    other = lax.ppermute(mine, "brick", pairs)
    begun, token = kernel(
        functools.partial(add_body, 0),
        "add_0",
        [shape((share, 2 * third * WIDTH)), shape((8, LANES), F32)],
        [mine, cotangent, *first],
    )
    side = kernel(
        after(after(gather_body, 3), 3),
        "gather",
        shape((half, total)),
        [token, second[1], mine, other],
        scalars=place,
        flops=LATER,
    )
    other = lax.ppermute(side, "rep", swap)
    grad_features, token = kernel(
        functools.partial(add_body, 1),
        "add_1",
        [shape((share, sites)), shape((8, LANES), F32)],
        [begun, cotangent, *second],
    )
    grad_weight = kernel(
        after(functools.partial(join_body, half, share), 3),
        "join",
        shape((TAPS * share, total), F32),
        [token, side, other],
        scalars=place,
        scratch=[pltpu.VMEM((reps * half, total), BF16)],
        flops=LATER,
    )
    grad_weight = jnp.transpose(grad_weight.reshape(TAPS, share, total), (0, 2, 1))
    return output, grad_features, grad_weight


def solution(mesh):
    return jax.shard_map(
        local,
        mesh=mesh,
        in_specs=(
            P("chan", ("scene", "brick", "rep")),
            P(None, None, "chan"),
            P(None, ("scene", "brick", "rep")),
            P("chan", ("scene", "brick", "rep")),
        ),
        out_specs=(
            P("chan", ("scene", "brick", "rep")),
            P("chan", ("scene", "brick", "rep")),
            P("scene", None, "chan"),
        ),
        check_vma=False,
    )
```
